512 devices in a mesh: grp: 256 (over z, y, x), mem: 2 (over core).
Axes of the slice: x: 4, y: 8, z: 8, core: 2. Of those that a mesh axis runs over, the one named last changes fastest.
Arguments:
- state: float32 [5, 125, 131072], P(None, None, ('grp', 'mem')), may hold values from -6 to 6
- rhs: float32 [5, 125, 131072], P(None, None, ('grp', 'mem')), may hold values from -6 to 6
- fine_diag: float32 [5, 125, 131072], P(None, None, ('grp', 'mem')), may hold values from 2 to 20
- q_fine: float32 [125, 125], replicated, may hold values from -0.5 to 0.5
- var_mix: float32 [5, 5], replicated, may hold values from -2.5 to 2.5
- mem_count: int32 [512, 2], P(('grp', 'mem')), may hold values from 42 to 128, as said below
- grp_count: int32 [512, 2], P(('grp', 'mem')), may hold values from 85 to 256, as said below
- send_mem_idx: int32 [512, 2, 128], P(('grp', 'mem')), may hold values from 0 to 1535
- send_grp_idx: int32 [512, 2, 256], P(('grp', 'mem')), may hold values from 0 to 1535
- face_src: int32 [6, 131072], P(None, ('grp', 'mem')), may hold values from 0 to 2304
- coarse_diag: float32 [5, 8, 131072], P(None, None, ('grp', 'mem')), may hold values from 3 to 12
- q_coarse: float32 [8, 8], replicated, may hold values from -2 to 2
- g_coarse: float32 [6, 8, 8], replicated, may hold values from -0.875 to 0.875
- owner: int32 [131072, 1], P(('grp', 'mem')), may hold values from 0 to 1; in each aligned block of 256 rows (0 to 255, 256 to 511, ...) at most 128 rows name the same one
- coarse_nbr: int32 [6, 131072], P(None, ('grp', 'mem')), may hold values from 0 to 768
Outputs:
- residual: float32 [5, 125, 131072], P(None, None, ('grp', 'mem'))
- correction: float32 [5, 125, 131072], P(None, None, ('grp', 'mem'))
The draws below stay inside these ranges and needn't reach their ends.
Inputs may be any that keep to these rules, and one draw needn't show every extreme that they name: `mem_count`: entries for a partition's own member are not used; some entry equals 128. `grp_count`: some entry equals 256. At most 128 elements of one partition have one owner, and exactly 128 in some partition.
All inputs are finite; a program needn't handle non-finite values.
Results may differ from the reference program's by a relative error of at most 0.0003.
Values sent between devices are 32-bit elements; how exact they have to be, the bound alone decides.
A program may use at most 64 MiB of HBM per device.

```python
import math
import jax
import jax.numpy as jnp
import numpy as np
from jax import lax

NV = 5
P5 = 125
P1 = 8
E = 256
FM = 128
FG = 256
ELEMS = 131072
SCAP = 128
CAPC = 256
N_GRP = 256
N_MEM = 2


def draw_mem_count(key, part):
    key = jax.random.fold_in(key, 7)
    counts = jax.random.randint(key, (ELEMS // E, N_MEM), FM // 3, FM + 1)
    return counts.at[0, 1].set(FM).astype(jnp.int32)


def draw_grp_count(key, part):
    key = jax.random.fold_in(key, 13)
    counts = jax.random.randint(key, (ELEMS // E, 2), FG // 3, FG + 1)
    return counts.at[0, 1].set(FG).astype(jnp.int32)


def with_ends(result, key, least, top_value):
    shape = result.shape
    spot = [jax.random.randint(jax.random.fold_in(key, axis), (), 0, shape[axis]) for axis in range(len(shape))]
    result = result.at[tuple(spot)].set(least)
    longest = shape.index(max(shape))
    spot[longest] = (spot[longest] + 1) % shape[longest]
    return result.at[tuple(spot)].set(top_value)


def levels(rng, extent, shards, smallest, top_value):
    factor_of, own = 1.0, jax.random.fold_in(rng, 6)
    for axis_at, shards_of in shards:
        heights = jnp.exp(jax.random.uniform(jax.random.fold_in(own, axis_at), (shards_of,), jnp.float32, smallest / len(shards), top_value / len(shards)))
        factor_of = factor_of * jnp.repeat(heights, extent[axis_at] // shards_of).reshape([-1 if axis == axis_at else 1 for axis in range(len(extent))])
    return factor_of


def deal_out(stream_key, own, number, rows, amount, top, reach, slope):
    sequence = jax.random.permutation(stream_key, amount)
    packed, usual = shares(amount, rows * top, reach, slope, True), shares(amount, rows * top, reach, slope, False)
    places = jnp.arange(amount)

    def named(tallies, offset_by):
        used = int((tallies > 0).sum())
        fixed = max(1, used // 4)
        shifted = fixed + (places - fixed + offset_by * (used - fixed)) % max(1, amount - fixed)
        return jnp.zeros((amount,), jnp.int32).at[sequence[jnp.where(places < fixed, places, shifted)]].set(jnp.asarray(tallies, jnp.int32))

    tallies = jnp.where(number % 4 == 0, named(packed, number // 4), named(usual, number - number // 4 - 1))
    mixed = jax.random.permutation(jax.random.fold_in(own, 3), amount)
    source_of, receiver = mixed[0:amount // 2 * 2:2], mixed[1:amount // 2 * 2:2]
    room = jnp.minimum(tallies[source_of] - 1, reach - tallies[receiver]) // 2
    room = jnp.where((source_of == sequence[0]) | (receiver == sequence[0]) | (tallies[receiver] == 0), 0, jnp.maximum(room, 0))
    shifted = jax.random.randint(jax.random.fold_in(own, 4), (amount // 2,), 0, 1 << 20) % (room + 1)
    tallies = tallies.at[source_of].add(-shifted).at[receiver].add(shifted)
    items = jnp.searchsorted(jnp.cumsum(tallies), jnp.arange(rows * top), side="right").astype(jnp.int32)
    listing = items.reshape(top, rows).T
    listing = listing[jax.random.permutation(jax.random.fold_in(own, 1), rows)]
    offset_by = jax.random.randint(jax.random.fold_in(own, 2), (rows, 1), 0, top)
    return jnp.take_along_axis(listing, (jnp.arange(top)[None, :] + offset_by) % top, axis=1)


def shares(count, total, most, slope, full):
    loads = [(1 << 20) // math.isqrt(standing ** slope) + 1 for standing in range(1, count + 1)]
    largest = most if full else min(most, max(-(-total // count), total * loads[0] // sum(loads)))
    least = 1 if total - largest >= count - 1 else 0
    holding, rest = [largest] + [least] * (count - 1), total - largest - least * (count - 1)
    while rest > 0:
        free = [i for i in range(1, count) if holding[i] < largest] or [i for i in range(1, count) if holding[i] < most]
        whole, budget = sum([loads[i] for i in free]), rest
        for i in free:
            extra = min(most - holding[i], max(1, budget * loads[i] // whole), rest)
            holding[i] = holding[i] + extra
            rest = rest - extra
    return np.array(holding)


def noise(own_key, extent, deviation, limit, pieces=(), kind=jnp.bfloat16):
    values = jax.random.normal(own_key, extent, jnp.float32) * deviation
    if len(pieces) > 0:
        values = levels(own_key, extent, pieces, -0.22, 0.18) * values
    return jnp.clip(values, min=-limit, max=limit).astype(kind)


def setup_inputs(seed: int = 0) -> dict:
    seeds = jax.random.split(jax.random.key(seed), 16)
    state = noise(seeds[0], (NV, P5, ELEMS), 1.0, 6.0, ((2, 512),), jnp.float32)
    rhs = noise(seeds[1], (NV, P5, ELEMS), 1.0, 6.0, ((2, 512),), jnp.float32)
    fine_diag = jnp.clip(jnp.exp(math.log(20.0) - 2.3025851 * jax.random.uniform(seeds[2], (NV, P5, ELEMS), jnp.float32) ** levels(seeds[2], (NV, P5, ELEMS), ((2, 512),), -0.2, 0.2)), 2.0, 20.0)
    q_fine = noise(seeds[3], (P5, P5), P5 ** -0.5, 0.5, (), jnp.float32)
    var_mix = noise(seeds[4], (NV, NV), NV ** -0.5, 2.5, (), jnp.float32)
    mem_count = draw_mem_count(jax.random.fold_in(seeds[15], 71), 0)
    grp_count = draw_grp_count(jax.random.fold_in(seeds[15], 71), 0)
    send_mem_idx = with_ends(jax.random.randint(seeds[7], (ELEMS // E, N_MEM, FM), 0, 6 * E), jax.random.fold_in(seeds[7], 1), 0, (6 * E) - 1).astype(jnp.int32)
    send_grp_idx = with_ends(jax.random.randint(seeds[8], (ELEMS // E, 2, FG), 0, 6 * E), jax.random.fold_in(seeds[8], 1), 0, (6 * E) - 1).astype(jnp.int32)
    face_src = with_ends(jax.random.randint(seeds[9], (6, ELEMS), 0, 6 * E + N_MEM * FM + 2 * FG + 1), jax.random.fold_in(seeds[9], 1), 0, 6 * E + N_MEM * FM + 2 * FG).astype(jnp.int32)
    coarse_diag = jnp.clip(jnp.exp(math.log(12.0) - 1.3862944 * jax.random.uniform(seeds[10], (NV, P1, ELEMS), jnp.float32) ** levels(seeds[10], (NV, P1, ELEMS), ((2, 512),), -0.2, 0.2)), 3.0, 12.0)
    q_coarse = noise(seeds[11], (P1, P1), P1 ** -0.5, 2.0, (), jnp.float32)
    g_coarse = noise(seeds[12], (6, P1, P1), (6 * P1) ** -0.5, 0.875, (), jnp.float32)
    owner_keys = jax.random.split(jax.random.fold_in(seeds[13], 1), ELEMS // E)
    owner_turns = jax.random.permutation(jax.random.fold_in(seeds[13], 3), ELEMS // E)
    owner = jax.vmap(lambda own, number: deal_out(jax.random.fold_in(seeds[13], 2), own, number, E, N_MEM, 1, SCAP, 2))(owner_keys, owner_turns).reshape((ELEMS, 1))
    coarse_nbr = with_ends(jax.random.randint(seeds[14], (6, CAPC * N_GRP * N_MEM), 0, 3 * CAPC + 1), jax.random.fold_in(seeds[14], 1), 0, 3 * CAPC).astype(jnp.int32)
    return dict(state=state, rhs=rhs, fine_diag=fine_diag, q_fine=q_fine, var_mix=var_mix, mem_count=mem_count, grp_count=grp_count, send_mem_idx=send_mem_idx, send_grp_idx=send_grp_idx, face_src=face_src, coarse_diag=coarse_diag, q_coarse=q_coarse, g_coarse=g_coarse, owner=owner, coarse_nbr=coarse_nbr)


OMEGA = 0.8
HIGH = lax.Precision.HIGHEST


def mult(form, left, right):
    return jnp.einsum(form, left, right, precision=HIGH)


def fine_tables():
    points = jnp.arange(125, dtype=jnp.int32)
    coords = [points // 25, (points // 5) % 5, points % 5]
    blocks = []
    for face in range(6):
        along = face // 2
        others = [c for b, c in enumerate(coords) if b != along]
        index = others[0] * 5 + others[1]
        on_face = coords[along] == 4 * (face % 2)
        blocks.append(((index[None, :] == jnp.arange(25, dtype=jnp.int32)[:, None]) & on_face[None, :]).astype(jnp.float32))
    extract = jnp.concatenate(blocks, axis=0)
    lift = extract.T
    nodes = -1.0 + 0.5 * jnp.arange(5, dtype=jnp.float32)
    basis = jnp.stack([(1.0 - nodes) / 2.0, (1.0 + nodes) / 2.0], axis=1)
    prolong = jnp.einsum("ia,jb,kc->ijkabc", basis, basis, basis).reshape(125, 8)
    restrict = prolong.T * 0.064
    return extract, lift, prolong, restrict


def trace_cols(field, extract):
    nvar, npts, elems = field.shape
    faces = mult("fp,vpe->vfe", extract, field)
    return faces.reshape(nvar, 6, 25, elems).transpose(0, 2, 1, 3).reshape(nvar * 25, 6 * elems)


def build_sends(faces, mcount, gcount, midx, gidx, member):
    members, mslots = midx.shape
    gslots = gidx.shape[1]
    rows = faces.shape[0]
    mkeep = ((jnp.arange(mslots, dtype=jnp.int32)[None, :] < mcount[:, None]) & (jnp.arange(members, dtype=jnp.int32)[:, None] != member)).astype(jnp.float32)
    gkeep = (jnp.arange(gslots, dtype=jnp.int32)[None, :] < gcount[:, None]).astype(jnp.float32)
    to_members = jnp.take(faces, midx.reshape(-1), axis=1).reshape(rows, members, mslots).transpose(1, 0, 2) * mkeep[:, None, :]
    to_groups = jnp.take(faces, gidx.reshape(-1), axis=1).reshape(rows, 2, gslots).transpose(1, 0, 2) * gkeep[:, None, :]
    return to_members, to_groups


def local_residual(field, rhs, diag, q_fine, var_mix, faces, from_members, from_prev, from_next, source, lift):
    nvar, npts, elems = field.shape
    rows = faces.shape[0]
    columns = jnp.concatenate([faces, from_members.transpose(1, 0, 2).reshape(rows, -1), from_prev, from_next, jnp.zeros((rows, 1), jnp.float32)], axis=1)
    near = jnp.take(columns, source.reshape(-1), axis=1).reshape(nvar, 25, 6, elems).transpose(0, 2, 1, 3).reshape(nvar, 150, elems)
    applied = diag * field + mult("pq,vqe->vpe", q_fine, field) + mult("vw,wpe->vpe", var_mix, field) - mult("pf,vfe->vpe", lift, near)
    return rhs - applied


def ranks(own, members):
    onehot = (own[None, :] == jnp.arange(members, dtype=jnp.int32)[:, None]).astype(jnp.int32)
    return jnp.sum((jnp.cumsum(onehot, axis=1) - 1) * onehot, axis=0).astype(jnp.int32)


def second_sweep(first, slot_rhs, slot_diag, rim, nbr_idx, q_coarse, g_coarse):
    width = first.shape[1]
    nvar = first.shape[0] // 8
    columns = jnp.concatenate([rim, jnp.zeros((rim.shape[0], 1), jnp.float32)], axis=1)
    near = jnp.take(columns, nbr_idx.reshape(-1), axis=1).reshape(nvar, 8, 6, width)
    inner = mult("ab,vbs->vas", q_coarse, first.reshape(nvar, 8, width))
    across = mult("fab,vbfs->vas", g_coarse, near)
    applied = slot_diag * first + (inner - across).reshape(nvar * 8, width)
    return first + OMEGA * (slot_rhs - applied) / slot_diag


def reference(state, rhs, fine_diag, q_fine, var_mix, mem_count, grp_count, send_mem_idx, send_grp_idx, face_src, coarse_diag, q_coarse, g_coarse, owner, coarse_nbr):
    extract, lift, prolong, restrict = fine_tables()
    parts = N_GRP * N_MEM
    rows = NV * 25

    def per_dev(a):
        return a.reshape(a.shape[0], a.shape[1], parts, E).transpose(2, 0, 1, 3)

    u_dev = per_dev(state)
    member_of = jnp.arange(parts, dtype=jnp.int32) % N_MEM

    def outgoing(args):
        field, mcount, gcount, midx, gidx, member = args
        return build_sends(trace_cols(field, extract), mcount, gcount, midx, gidx, member)

    to_members, to_groups = lax.map(outgoing, (u_dev, mem_count, grp_count, send_mem_idx, send_grp_idx, member_of))
    from_members = to_members.reshape(N_GRP, N_MEM, N_MEM, rows, FM).transpose(0, 2, 1, 3, 4).reshape(parts, N_MEM, rows, FM)
    grouped = to_groups.reshape(N_GRP, N_MEM, 2, rows, FG)
    blank = jnp.zeros((1, N_MEM, rows, FG), jnp.float32)
    from_prev = jnp.concatenate([blank, grouped[:-1, :, 1]], axis=0).reshape(parts, rows, FG)
    from_next = jnp.concatenate([grouped[1:, :, 0], blank], axis=0).reshape(parts, rows, FG)
    source = face_src.reshape(6, parts, E).transpose(1, 0, 2)

    def residual_one(args):
        field, right, diag, fmem, fprev, fnext, src = args
        return local_residual(field, right, diag, q_fine, var_mix, trace_cols(field, extract), fmem, fprev, fnext, src, lift)

    resid_dev = lax.map(residual_one, (u_dev, per_dev(rhs), per_dev(fine_diag), from_members, from_prev, from_next, source))
    restricted = mult("cp,dvpe->dvce", restrict, resid_dev).reshape(parts, NV * 8, E)
    cdiag = per_dev(coarse_diag).reshape(parts, NV * 8, E)
    own = owner.reshape(parts, E)
    rank = jax.vmap(lambda o: ranks(o, N_MEM))(own)
    group_of = (jnp.arange(parts, dtype=jnp.int32) // N_MEM)[:, None]
    target = (group_of * N_MEM + own).astype(jnp.int32)
    slot = (member_of[:, None] * SCAP + rank).astype(jnp.int32)
    slot_rhs = jnp.zeros((parts, NV * 8, CAPC), jnp.float32).at[target, :, slot].set(restricted.transpose(0, 2, 1))
    slot_diag = jnp.ones((parts, NV * 8, CAPC), jnp.float32).at[target, :, slot].set(cdiag.transpose(0, 2, 1))
    first = OMEGA * slot_rhs / slot_diag
    first_g = first.reshape(N_GRP, N_MEM, NV * 8, CAPC)
    zero_g = jnp.zeros((1, N_MEM, NV * 8, CAPC), jnp.float32)
    rim = jnp.concatenate([jnp.concatenate([zero_g, first_g[:-1]], axis=0), first_g, jnp.concatenate([first_g[1:], zero_g], axis=0)], axis=3).reshape(parts, NV * 8, 3 * CAPC)
    nbr = coarse_nbr.reshape(6, parts, CAPC).transpose(1, 0, 2)
    second = jax.vmap(lambda a, b, c, d, e: second_sweep(a, b, c, d, e, q_coarse, g_coarse))(first, slot_rhs, slot_diag, rim, nbr)
    picked = second[target, :, slot]
    corr_dev = mult("pc,dvce->dvpe", prolong, picked.transpose(0, 2, 1).reshape(parts, NV, 8, E))

    def back(a):
        return a.transpose(1, 2, 0, 3).reshape(NV, a.shape[2], parts * E)

    return back(resid_dev), back(corr_dev)
```

```python
import functools

import jax
import jax.numpy as jnp
import ml_dtypes
import numpy as np
from jax import lax
from jax.experimental import pallas as pl
from jax.experimental.pallas import tpu as pltpu
from jax.sharding import PartitionSpec as P

MESH = pl.DeviceIdType.MESH
HIGH = lax.Precision.HIGHEST
BF = jnp.bfloat16
F32 = jnp.float32
FAR = 1 << 20


def tables():
    points = np.arange(125)
    coords = [points // 25, points // 5 % 5, points % 5]
    extract = np.zeros((6, 25, 125), np.float32)
    for face in range(6):
        along = face // 2
        others = [c for b, c in enumerate(coords) if b != along]
        index = others[0] * 5 + others[1]
        on_face = coords[along] == 4 * (face % 2)
        extract[face] = (index[None, :] == np.arange(25)[:, None]) & on_face[None, :]
    nodes = -1.0 + 0.5 * np.arange(5)
    basis = np.stack([(1.0 - nodes) / 2.0, (1.0 + nodes) / 2.0], axis=1)
    prolong = np.einsum("ia,jb,kc->ijkabc", basis, basis, basis).reshape(125, 8)
    ext = np.zeros((6, 128, 5, 128), np.float32)
    for v in range(5):
        ext[:, v * 25 : v * 25 + 25, v, :125] = extract
    ext = ext.reshape(768, 640)
    lift = np.ascontiguousarray(ext.T)
    rest = np.zeros((48, 5, 128), np.float32)
    for v in range(5):
        rest[v * 8 : v * 8 + 8, v, :125] = prolong.T
    rest = rest.reshape(48, 640)
    rest_lift = rest @ lift
    pro = np.ascontiguousarray(rest[:40].T)
    pro2 = np.concatenate([pro, pro], axis=1)
    spread = np.zeros((8, 6, 5, 8), np.float32)
    for b in range(8):
        spread[b, :, :, b] = 1.0
    spread = spread.reshape(8, 240)
    gather_a = np.zeros((48, 48), np.float32)
    for v in range(5):
        for f in range(6):
            for a in range(8):
                gather_a[v * 8 + a, f * 8 + a] = 1.0
    same_f = np.zeros((6, 8, 6, 40), np.float32)
    for f in range(6):
        same_f[f, :, f, :] = 1.0
    same_f = same_f.reshape(48, 240)
    same_v = np.zeros((6, 8, 6, 5, 8), np.float32)
    for v in range(5):
        same_v[v, :, :, v, :] = 1.0
    same_v = same_v.reshape(48, 240)
    small = np.zeros((152, 240), np.float32)
    small[0:8] = spread
    small[8:56, :48] = gather_a
    small[56:104] = same_f
    small[104:152] = same_v
    cast = lambda a: np.asarray(a, ml_dtypes.bfloat16)
    return cast(ext), cast(lift), cast(rest), cast(rest_lift), cast(pro2), small


def halves(x):
    hi = x.astype(BF)
    return hi, (x - hi.astype(F32)).astype(BF)


def stacked(x):
    hi = x.astype(BF).astype(F32)
    return jnp.concatenate([hi, x - hi], axis=0).astype(BF)


def dot(a, b):
    return jnp.dot(a, b, preferred_element_type=F32)


def exact(a, b):
    return jnp.dot(a, b, precision=HIGH, preferred_element_type=F32)


def hot(row, base, size):
    places = lax.broadcasted_iota(jnp.int32, (size, row.shape[1]), 0)
    return jnp.where(places == row - base, 1.0, 0.0).astype(BF)


def padded(x):
    return jnp.concatenate([x, jnp.zeros((3, x.shape[1]), F32)], axis=0)


def main_kernel(
    n_grp,
    state, rhs, diag, ext_h, lift_h,
    q_fine, var_mix, mcount, gcount, midx, gidx, fsrc, cdiag, q_coarse, g_coarse, owner, cnbr,
    rest, rest_lift, small,
    resid_out, second_out,
    st, rh, dg, ext, lift, uh, ul, qs,
    ohs, tr, snd_g, snd_m, snd_n, rcv_g, rcv_m, rcv_n,
    ohr, nlh, nll, resl, ohc, st_hot, blks, mine, rim, resv,
    in_sem, snd_sem, rcv_sem, out_sem,
):
    g = lax.axis_index("grp")
    m = lax.axis_index("mem")
    other = 1 - m
    prev = lax.rem(g + n_grp - 1, n_grp)
    nxt = lax.rem(g + 1, n_grp)

    loads = [
        pltpu.make_async_copy(state, st, in_sem.at[0]),
        pltpu.make_async_copy(ext_h, ext, in_sem.at[1]),
        pltpu.make_async_copy(rhs, rh, in_sem.at[2]),
        pltpu.make_async_copy(diag, dg, in_sem.at[3]),
        pltpu.make_async_copy(lift_h, lift, in_sem.at[4]),
    ]
    for c in loads:
        c.start()

    barrier = pltpu.get_barrier_semaphore()
    near_devices = [(prev, 0), (prev, 1), (nxt, 0), (nxt, 1), (g, other)]
    for d in near_devices:
        pl.semaphore_signal(barrier, inc=1, device_id=d, device_id_type=MESH)

    lane_g = lax.broadcasted_iota(jnp.int32, (1, 256), 1)
    lane_m = lax.broadcasted_iota(jnp.int32, (1, 128), 1)
    for t in range(2):
        row = jnp.where(lane_g < gcount[0, t], gidx[0, t : t + 1, :], -1)
        ohs[:, t * 256 : t * 256 + 256] = hot(row, 0, 1536)
    mrow = jnp.where(m == 0, midx[0, 1:2, :], midx[0, 0:1, :])
    mlim = jnp.where(m == 0, mcount[0, 1], mcount[0, 0])
    ohs[:, 512:640] = hot(jnp.where(lane_m < mlim, mrow, -1), 0, 1536)
    nbr = cnbr[...]
    snd_n[0:6, :] = jnp.where(m == 0, nbr[:, 128:256], nbr[:, 0:128])
    snd_n[6:8, :] = jnp.zeros((2, 128), jnp.int32)

    loads[0].wait()
    for v in range(5):
        hi, lo = halves(padded(st[v]))
        uh[v * 128 : v * 128 + 128, :] = hi
        ul[v * 128 : v * 128 + 128, :] = lo
    loads[1].wait()
    for f in range(6):
        e = ext[f * 128 : f * 128 + 128, :]
        tr[0:128, f * 256 : f * 256 + 256] = dot(e, uh[...]).astype(BF)
        tr[128:256, f * 256 : f * 256 + 256] = dot(e, ul[...]).astype(BF)

    def remote(src, dst, i, j, device):
        return pltpu.make_async_remote_copy(
            src_ref=src, dst_ref=dst, send_sem=snd_sem.at[i], recv_sem=rcv_sem.at[j],
            device_id=device, device_id_type=MESH,
        )

    pl.semaphore_wait(barrier, 5)
    c_nbr = remote(snd_n, rcv_n, 0, 0, (g, other))
    c_nbr.start()
    picked = dot(tr[...], ohs[:, 0:256])
    snd_g[0] = picked[:128] + picked[128:]
    c_prev = remote(snd_g.at[0], rcv_g.at[1], 1, 1, (prev, m))
    c_prev.start()
    picked = dot(tr[...], ohs[:, 256:512])
    snd_g[1] = picked[:128] + picked[128:]
    c_next = remote(snd_g.at[1], rcv_g.at[0], 2, 2, (nxt, m))
    c_next.start()
    picked = dot(tr[...], ohs[:, 512:640])
    snd_m[...] = picked[:128] + picked[128:]
    c_mem = remote(snd_m, rcv_m, 3, 3, (g, other))
    c_mem.start()

    base_prev = jnp.where(g == 0, FAR, 1792)
    base_next = jnp.where(g == n_grp - 1, FAR, 2048)
    base_mem = 1536 + other * 128

    def local_faces(f, carry):
        row = fsrc[pl.ds(f, 1), :]
        acc = dot(tr[...], hot(row, 0, 1536))
        at = pl.multiple_of(f * 128, 128)
        nlh[pl.ds(at, 128), :] = acc[:128].astype(BF)
        nll[pl.ds(at, 128), :] = acc[128:].astype(BF)
        ohr[f, 0:256, :] = hot(row, base_prev, 256)
        ohr[f, 256:512, :] = hot(row, base_next, 256)
        ohr[f, 512:640, :] = hot(row, base_mem, 128)
        return carry

    lax.fori_loop(0, 6, local_faces, 0)

    qs[...] = jnp.zeros((128, 128), F32)
    qs[0:125, 0:125] = q_fine[...]
    qh, ql = halves(qs[...])
    loads[2].wait()
    loads[3].wait()
    for v in range(5):
        total = dot(qh, uh[v * 128 : v * 128 + 128, :]) + dot(qh, ul[v * 128 : v * 128 + 128, :])
        total = (total + dot(ql, uh[v * 128 : v * 128 + 128, :]))[:125]
        total = total + dg[v] * st[v]
        for w in range(5):
            total = total + var_mix[v, w] * st[w]
        resl[v * 128 : v * 128 + 128, :] = padded(rh[v] - total)
    rl_h, rl_l = halves(resl[...])
    rest0 = dot(rest[...], rl_h) + dot(rest[...], rl_l)
    rest0 = rest0 + dot(rest_lift[...], nlh[...]) + dot(rest_lift[...], nll[...])

    own = owner[...].astype(F32)
    before = lax.broadcasted_iota(jnp.int32, (256, 256), 0) < lax.broadcasted_iota(jnp.int32, (256, 256), 1)
    ones_before = dot(jnp.broadcast_to(own, (16, 256)).astype(BF), jnp.where(before, 1.0, 0.0).astype(BF))[0:1]
    ones_before = ones_before.astype(jnp.int32)
    target = jnp.where(owner[...] == 1, 128 + ones_before, lane_g - ones_before)
    st_hot[...] = hot(target, 0, 256)

    gfa = g_coarse[...]
    gg = exact(gfa, small[0:8, :]) * small[56:104, :]
    gg = exact(small[8:56, 0:48], gg) * small[104:152, :]
    ggh, ggl = halves(gg)
    qrep = jnp.concatenate([q_coarse[...]] * 5, axis=0)
    qq = exact(qrep, small[0:8, 0:40]) * small[104:144, 0:40]

    c_prev.wait_recv()
    c_next.wait_recv()
    c_mem.wait_recv()
    parts = []
    for ref in (rcv_g.at[0], rcv_g.at[1], rcv_m):
        hi, lo = halves(ref[...])
        parts.append(jnp.concatenate([hi, lo], axis=0))
    for f in range(6):
        acc = dot(parts[0], ohr[f, 0:256, :]) + dot(parts[1], ohr[f, 256:512, :]) + dot(parts[2], ohr[f, 512:640, :])
        nh, nl = acc[:128].astype(BF), acc[128:].astype(BF)
        rlf = rest_lift[:, f * 128 : f * 128 + 128]
        rest0 = rest0 + dot(rlf, nh) + dot(rlf, nl)
        nlh[f * 128 : f * 128 + 128, :] += nh
        nll[f * 128 : f * 128 + 128, :] += nl
    cd = cdiag[...]
    first = (0.8 * 0.064) * rest0[:40] / cd
    packed = lax.dot_general(stacked(first), st_hot[...], (((1,), (1,)), ((), ())), preferred_element_type=F32)
    mine[...] = packed[:40] + packed[40:]
    c_two = []
    for i, (d, place) in enumerate(
        [((prev, 0), 4 + m), ((prev, 1), 4 + m), ((nxt, 0), m), ((nxt, 1), m), ((g, other), 2 + m)]
    ):
        c = remote(mine, blks.at[place], 4 + i, 4 + place, d)
        c.start()
        c_two.append(c)

    for v in range(5):
        lf = lift[v * 128 : v * 128 + 128, :]
        if v == 0:
            loads[4].wait()
            lf = lift[0:128, :]
        full = resl[v * 128 : v * 128 + 128, :] + dot(lf, nlh[...]) + dot(lf, nll[...])
        resv[v] = full[:125]
    c_out = pltpu.make_async_copy(resv, resid_out, out_sem)
    c_out.start()
    inner = exact(qq, first)
    weight = 0.8 / cd
    base = 1.2 * first - weight * inner

    c_nbr.wait_recv()
    own_nbr = jnp.where(m == 0, nbr[:, 0:128], nbr[:, 128:256])
    got_nbr = rcv_n[0:6, :]
    for o in range(2):
        lists = jnp.where(m == o, own_nbr, got_nbr)
        lists = jnp.where((g == 0) & (lists < 256), FAR, lists)
        lists = jnp.where((g == n_grp - 1) & (lists >= 512), FAR, lists)
        for f in range(6):
            ohc[o, :, f * 128 : f * 128 + 128] = hot(lists[f : f + 1, :], 0, 768)

    def arrived(place):
        remote(mine, blks.at[place], 4, 4 + place, (g, other)).wait_recv()

    for place in (2 + other, 0, 1, 4, 5):
        arrived(place)
    blks[2 + m] = mine[...]
    for j in range(6):
        both = stacked(blks[j])
        rim[0, :, j * 128 : j * 128 + 128] = both[:, 0:128]
        rim[1, :, j * 128 : j * 128 + 128] = both[:, 128:256]
    nhs, nls = [], []
    for o in range(2):
        near = dot(rim[o], ohc[o])
        nhs.append(jnp.concatenate([near[:40, f * 128 : f * 128 + 128] for f in range(6)], axis=0))
        nls.append(jnp.concatenate([near[40:, f * 128 : f * 128 + 128] for f in range(6)], axis=0))
    nh = jnp.concatenate(nhs, axis=1).astype(BF)
    nl = jnp.concatenate(nls, axis=1).astype(BF)
    across = (dot(ggh, nh) + dot(ggh, nl) + dot(ggl, nh))[:40]
    back = dot(stacked(across), st_hot[...])
    second_out[...] = base + weight * (back[:40] + back[40:])

    for c in [c_nbr, c_prev, c_next, c_mem] + c_two:
        c.wait_send()
    c_out.wait()


def last_kernel(resid, second, pro2, resid_out, corr_out, corr, sem):
    c0 = pltpu.make_async_copy(resid, resid_out, sem.at[0])
    c0.start()
    both = stacked(second[...])
    copies = []
    for v in range(5):
        corr[v] = dot(pro2[v * 128 : v * 128 + 128, :], both)[:125]
        c = pltpu.make_async_copy(corr.at[v], corr_out.at[v], sem.at[1 + v])
        c.start()
        copies.append(c)
    c0.wait()
    for c in copies:
        c.wait()


def shards(
    state, rhs, fine_diag, q_fine, var_mix, mem_count, grp_count, send_mem_idx, send_grp_idx,
    face_src, coarse_diag, q_coarse, g_coarse, owner, coarse_nbr,
):
    ext, lift, rest, rest_lift, pro2, small = tables()
    n_grp = lax.axis_size("grp")
    hbm = pl.BlockSpec(memory_space=pl.ANY)
    vmem = pl.BlockSpec(memory_space=pltpu.VMEM)
    smem = pl.BlockSpec(memory_space=pltpu.SMEM)
    field = jax.ShapeDtypeStruct((5, 125, 256), F32)
    resid, second = pl.pallas_call(
        functools.partial(main_kernel, n_grp),
        out_shape=(field, jax.ShapeDtypeStruct((40, 256), F32)),
        in_specs=[hbm] * 5 + [vmem, smem, smem, smem] + [vmem] * 11,
        out_specs=(hbm, vmem),
        scratch_shapes=[
            pltpu.VMEM((5, 125, 256), F32),
            pltpu.VMEM((5, 125, 256), F32),
            pltpu.VMEM((5, 125, 256), F32),
            pltpu.VMEM((768, 640), BF),
            pltpu.VMEM((640, 768), BF),
            pltpu.VMEM((640, 256), BF),
            pltpu.VMEM((640, 256), BF),
            pltpu.VMEM((128, 128), F32),
            pltpu.VMEM((1536, 640), BF),
            pltpu.VMEM((256, 1536), BF),
            pltpu.VMEM((2, 128, 256), F32),
            pltpu.VMEM((128, 128), F32),
            pltpu.VMEM((8, 128), jnp.int32),
            pltpu.VMEM((2, 128, 256), F32),
            pltpu.VMEM((128, 128), F32),
            pltpu.VMEM((8, 128), jnp.int32),
            pltpu.VMEM((6, 640, 256), BF),
            pltpu.VMEM((768, 256), BF),
            pltpu.VMEM((768, 256), BF),
            pltpu.VMEM((640, 256), F32),
            pltpu.VMEM((2, 768, 768), BF),
            pltpu.VMEM((256, 256), BF),
            pltpu.VMEM((6, 40, 256), F32),
            pltpu.VMEM((40, 256), F32),
            pltpu.VMEM((2, 80, 768), BF),
            pltpu.VMEM((5, 125, 256), F32),
            pltpu.SemaphoreType.DMA((5,)),
            pltpu.SemaphoreType.DMA((9,)),
            pltpu.SemaphoreType.DMA((10,)),
            pltpu.SemaphoreType.DMA,
        ],
        compiler_params=pltpu.CompilerParams(
            collective_id=0, has_side_effects=True, vmem_limit_bytes=40 * 1024 * 1024
        ),
        name="residual_and_sweeps",
    )(
        state, rhs, fine_diag, jnp.asarray(ext), jnp.asarray(lift),
        q_fine, var_mix, mem_count, grp_count, send_mem_idx, send_grp_idx, face_src,
        coarse_diag.reshape(40, 256), q_coarse, g_coarse.reshape(48, 8), owner.reshape(1, 256), coarse_nbr,
        jnp.asarray(rest), jnp.asarray(rest_lift), jnp.asarray(small),
    )
    return pl.pallas_call(
        last_kernel,
        out_shape=(field, field),
        in_specs=[hbm, vmem, vmem],
        out_specs=(hbm, hbm),
        scratch_shapes=[pltpu.VMEM((5, 125, 256), F32), pltpu.SemaphoreType.DMA((6,))],
        compiler_params=pltpu.CompilerParams(vmem_limit_bytes=16 * 1024 * 1024),
        name="prolongation",
    )(resid, second, jnp.asarray(pro2))


def solution(mesh):
    whole = ("grp", "mem")
    return jax.shard_map(
        shards,
        mesh=mesh,
        in_specs=(
            P(None, None, whole), P(None, None, whole), P(None, None, whole), P(), P(),
            P(whole, None), P(whole, None), P(whole, None, None), P(whole, None, None), P(None, whole),
            P(None, None, whole), P(), P(), P(whole, None), P(None, whole),
        ),
        out_specs=(P(None, None, whole), P(None, None, whole)),
        check_vma=False,
    )
```

```python
import functools

import jax
import jax.numpy as jnp
import ml_dtypes
import numpy as np
from jax import lax
from jax.experimental import pallas as pl
from jax.experimental.pallas import tpu as pltpu
from jax.sharding import PartitionSpec as P

MESH = pl.DeviceIdType.MESH
HIGH = lax.Precision.HIGHEST
BF = jnp.bfloat16
F32 = jnp.float32
FAR = 1 << 20


def tables():
    points = np.arange(125)
    coords = [points // 25, points // 5 % 5, points % 5]
    extract = np.zeros((6, 25, 125), np.float32)
    for face in range(6):
        along = face // 2
        others = [c for b, c in enumerate(coords) if b != along]
        index = others[0] * 5 + others[1]
        on_face = coords[along] == 4 * (face % 2)
        extract[face] = (index[None, :] == np.arange(25)[:, None]) & on_face[None, :]
    nodes = -1.0 + 0.5 * np.arange(5)
    basis = np.stack([(1.0 - nodes) / 2.0, (1.0 + nodes) / 2.0], axis=1)
    prolong = np.einsum("ia,jb,kc->ijkabc", basis, basis, basis).reshape(125, 8)
    ext = np.zeros((6, 128, 5, 128), np.float32)
    for v in range(5):
        ext[:, v * 25 : v * 25 + 25, v, :125] = extract
    ext = ext.reshape(768, 640)
    lift = np.ascontiguousarray(ext.T)
    rest = np.zeros((48, 5, 128), np.float32)
    for v in range(5):
        rest[v * 8 : v * 8 + 8, v, :125] = prolong.T
    rest = rest.reshape(48, 640)
    rest_lift = rest @ lift
    pro = np.ascontiguousarray(rest[:40].T)
    pro2 = np.concatenate([pro, pro], axis=1)
    spread = np.zeros((8, 6, 5, 8), np.float32)
    for b in range(8):
        spread[b, :, :, b] = 1.0
    spread = spread.reshape(8, 240)
    gather_a = np.zeros((48, 48), np.float32)
    for v in range(5):
        for f in range(6):
            for a in range(8):
                gather_a[v * 8 + a, f * 8 + a] = 1.0
    same_f = np.zeros((6, 8, 6, 40), np.float32)
    for f in range(6):
        same_f[f, :, f, :] = 1.0
    same_f = same_f.reshape(48, 240)
    same_v = np.zeros((6, 8, 6, 5, 8), np.float32)
    for v in range(5):
        same_v[v, :, :, v, :] = 1.0
    same_v = same_v.reshape(48, 240)
    small = np.zeros((152, 240), np.float32)
    small[0:8] = spread
    small[8:56, :48] = gather_a
    small[56:104] = same_f
    small[104:152] = same_v
    cast = lambda a: np.asarray(a, ml_dtypes.bfloat16)
    return cast(ext), cast(lift), cast(rest), cast(rest_lift), cast(pro2), small


def halves(x):
    hi = x.astype(BF)
    return hi, (x - hi.astype(F32)).astype(BF)


def stacked(x):
    hi = x.astype(BF).astype(F32)
    return jnp.concatenate([hi, x - hi], axis=0).astype(BF)


def dot(a, b):
    return jnp.dot(a, b, preferred_element_type=F32)


def exact(a, b):
    return jnp.dot(a, b, precision=HIGH, preferred_element_type=F32)


def hot(row, base, size):
    places = lax.broadcasted_iota(jnp.int32, (size, row.shape[1]), 0)
    return jnp.where(places == row - base, 1.0, 0.0).astype(BF)


def padded(x):
    return jnp.concatenate([x, jnp.zeros((3, x.shape[1]), F32)], axis=0)


def main_kernel(n_grp, *refs):
    sources, (resid_out, second_out), scratch = refs[:20], refs[20:22], refs[22:]
    (
        st, midx, gidx, mcount, gcount, ext, cnbr, fsrc, rh, dg, q_fine, var_mix,
        rest, rest_lift, owner, cdiag, g_coarse, q_coarse, small, lift,
    ) = scratch[:20]
    (
        uh, ul, qs,
        ohs, tr, snd_g, snd_m, snd_n, rcv_g, rcv_m, rcv_n,
        ohr, nlh, nll, resl, ohc, st_hot, blks, mine, rim, resv, mine2,
        in_sem, snd_sem, rcv_sem, out_sem,
    ) = scratch[20:]
    g = lax.axis_index("grp")
    m = lax.axis_index("mem")
    other = 1 - m
    prev = lax.rem(g + n_grp - 1, n_grp)
    nxt = lax.rem(g + 1, n_grp)

    loads = [pltpu.make_async_copy(src, scratch[i], in_sem.at[i]) for i, src in enumerate(sources)]
    for c in loads:
        c.start()

    barrier = pltpu.get_barrier_semaphore()
    near_devices = [(prev, 0), (prev, 1), (nxt, 0), (nxt, 1), (g, other)]
    for d in near_devices:
        pl.semaphore_signal(barrier, inc=1, device_id=d, device_id_type=MESH)

    for i in (1, 2, 3, 4, 6):
        loads[i].wait()
    lane_g = lax.broadcasted_iota(jnp.int32, (1, 256), 1)
    lane_m = lax.broadcasted_iota(jnp.int32, (1, 128), 1)
    for t in range(2):
        row = jnp.where(lane_g < gcount[0:1, t : t + 1], gidx[0, t : t + 1, :], -1)
        ohs[:, t * 256 : t * 256 + 256] = hot(row, 0, 1536)
    mrow = jnp.where(m == 0, midx[0, 1:2, :], midx[0, 0:1, :])
    mlim = jnp.where(m == 0, mcount[0:1, 1:2], mcount[0:1, 0:1])
    ohs[:, 512:640] = hot(jnp.where(lane_m < mlim, mrow, -1), 0, 1536)
    nbr = cnbr[...]
    snd_n[0:6, :] = jnp.where(m == 0, nbr[:, 128:256], nbr[:, 0:128])
    snd_n[6:8, :] = jnp.zeros((2, 128), jnp.int32)

    loads[0].wait()
    for v in range(5):
        hi, lo = halves(padded(st[v]))
        uh[v * 128 : v * 128 + 128, :] = hi
        ul[v * 128 : v * 128 + 128, :] = lo
    loads[5].wait()
    for f in range(6):
        e = ext[f * 128 : f * 128 + 128, :]
        tr[0:128, f * 256 : f * 256 + 256] = dot(e, uh[...]).astype(BF)
        tr[128:256, f * 256 : f * 256 + 256] = dot(e, ul[...]).astype(BF)

    def remote(src, dst, i, j, device):
        return pltpu.make_async_remote_copy(
            src_ref=src, dst_ref=dst, send_sem=snd_sem.at[i], recv_sem=rcv_sem.at[j],
            device_id=device, device_id_type=MESH,
        )

    pl.semaphore_wait(barrier, 5)
    c_nbr = remote(snd_n, rcv_n, 0, 0, (g, other))
    c_nbr.start()
    picked = dot(tr[...], ohs[:, 0:256])
    snd_g[0] = picked[:128] + picked[128:]
    c_prev = remote(snd_g.at[0], rcv_g.at[1], 1, 1, (prev, m))
    c_prev.start()
    picked = dot(tr[...], ohs[:, 256:512])
    snd_g[1] = picked[:128] + picked[128:]
    c_next = remote(snd_g.at[1], rcv_g.at[0], 2, 2, (nxt, m))
    c_next.start()
    picked = dot(tr[...], ohs[:, 512:640])
    snd_m[...] = picked[:128] + picked[128:]
    c_mem = remote(snd_m, rcv_m, 3, 3, (g, other))
    c_mem.start()

    base_prev = jnp.where(g == 0, FAR, 1792)
    base_next = jnp.where(g == n_grp - 1, FAR, 2048)
    base_mem = 1536 + other * 128

    def local_faces(f, carry):
        row = fsrc[pl.ds(f, 1), :]
        acc = dot(tr[...], hot(row, 0, 1536))
        at = pl.multiple_of(f * 128, 128)
        nlh[pl.ds(at, 128), :] = acc[:128].astype(BF)
        nll[pl.ds(at, 128), :] = acc[128:].astype(BF)
        ohr[f, 0:256, :] = hot(row, base_prev, 256)
        ohr[f, 256:512, :] = hot(row, base_next, 256)
        ohr[f, 512:640, :] = hot(row, base_mem, 128)
        return carry

    loads[7].wait()
    lax.fori_loop(0, 6, local_faces, 0)

    for i in range(8, 19):
        loads[i].wait()
    qs[...] = jnp.zeros((128, 128), F32)
    qs[0:125, 0:125] = q_fine[...]
    qh, ql = halves(qs[...])
    for v in range(5):
        total = dot(qh, uh[v * 128 : v * 128 + 128, :]) + dot(qh, ul[v * 128 : v * 128 + 128, :])
        total = (total + dot(ql, uh[v * 128 : v * 128 + 128, :]))[:125]
        total = total + dg[v] * st[v]
        for w in range(5):
            total = total + var_mix[v : v + 1, w : w + 1] * st[w]
        resl[v * 128 : v * 128 + 128, :] = padded(rh[v] - total)
    rl_h, rl_l = halves(resl[...])
    rest0 = dot(rest[...], rl_h) + dot(rest[...], rl_l)
    rest0 = rest0 + dot(rest_lift[...], nlh[...]) + dot(rest_lift[...], nll[...])

    own = owner[...].astype(F32)
    before = lax.broadcasted_iota(jnp.int32, (256, 256), 0) < lax.broadcasted_iota(jnp.int32, (256, 256), 1)
    ones_before = dot(jnp.broadcast_to(own, (16, 256)).astype(BF), jnp.where(before, 1.0, 0.0).astype(BF))[0:1]
    ones_before = ones_before.astype(jnp.int32)
    target = jnp.where(owner[...] == 1, 128 + ones_before, lane_g - ones_before)
    st_hot[...] = hot(target, 0, 256)

    gfa = g_coarse[...]
    gg = exact(gfa, small[0:8, :]) * small[56:104, :]
    gg = exact(small[8:56, 0:48], gg) * small[104:152, :]
    ggh, ggl = halves(gg)
    qrep = jnp.concatenate([q_coarse[...]] * 5, axis=0)
    qq = exact(qrep, small[0:8, 0:40]) * small[104:144, 0:40]

    c_prev.wait_recv()
    c_next.wait_recv()
    c_mem.wait_recv()
    parts = []
    for ref in (rcv_g.at[0], rcv_g.at[1], rcv_m):
        hi, lo = halves(ref[...])
        parts.append(jnp.concatenate([hi, lo], axis=0))
    for f in range(6):
        acc = dot(parts[0], ohr[f, 0:256, :]) + dot(parts[1], ohr[f, 256:512, :]) + dot(parts[2], ohr[f, 512:640, :])
        nh, nl = acc[:128].astype(BF), acc[128:].astype(BF)
        rlf = rest_lift[:, f * 128 : f * 128 + 128]
        rest0 = rest0 + dot(rlf, nh) + dot(rlf, nl)
        nlh[f * 128 : f * 128 + 128, :] += nh
        nll[f * 128 : f * 128 + 128, :] += nl
    cd = cdiag[...]
    first = (0.8 * 0.064) * rest0[:40] / cd
    packed = lax.dot_general(stacked(first), st_hot[...], (((1,), (1,)), ((), ())), preferred_element_type=F32)
    mine[...] = packed[:40] + packed[40:]
    c_two = []
    for i, (d, place) in enumerate(
        [((prev, 0), 4 + m), ((prev, 1), 4 + m), ((nxt, 0), m), ((nxt, 1), m), ((g, other), 2 + m)]
    ):
        c = remote(mine, blks.at[place], 4 + i, 4 + place, d)
        c.start()
        c_two.append(c)

    for v in range(5):
        lf = lift[v * 128 : v * 128 + 128, :]
        if v == 0:
            loads[19].wait()
            lf = lift[0:128, :]
        full = resl[v * 128 : v * 128 + 128, :] + dot(lf, nlh[...]) + dot(lf, nll[...])
        resv[v] = full[:125]
    c_out = pltpu.make_async_copy(resv, resid_out, out_sem.at[0])
    c_out.start()
    inner = exact(qq, first)
    weight = 0.8 / cd
    base = 1.2 * first - weight * inner

    c_nbr.wait_recv()
    own_nbr = jnp.where(m == 0, nbr[:, 0:128], nbr[:, 128:256])
    got_nbr = rcv_n[0:6, :]
    for o in range(2):
        lists = jnp.where(m == o, own_nbr, got_nbr)
        lists = jnp.where((g == 0) & (lists < 256), FAR, lists)
        lists = jnp.where((g == n_grp - 1) & (lists >= 512), FAR, lists)
        for f in range(6):
            ohc[o, :, f * 128 : f * 128 + 128] = hot(lists[f : f + 1, :], 0, 768)

    def arrived(place):
        remote(mine, blks.at[place], 4, 4 + place, (g, other)).wait_recv()

    for place in (2 + other, 0, 1, 4, 5):
        arrived(place)
    blks[2 + m] = mine[...]
    for j in range(6):
        both = stacked(blks[j])
        rim[0, :, j * 128 : j * 128 + 128] = both[:, 0:128]
        rim[1, :, j * 128 : j * 128 + 128] = both[:, 128:256]
    nhs, nls = [], []
    for o in range(2):
        near = dot(rim[o], ohc[o])
        nhs.append(jnp.concatenate([near[:40, f * 128 : f * 128 + 128] for f in range(6)], axis=0))
        nls.append(jnp.concatenate([near[40:, f * 128 : f * 128 + 128] for f in range(6)], axis=0))
    nh = jnp.concatenate(nhs, axis=1).astype(BF)
    nl = jnp.concatenate(nls, axis=1).astype(BF)
    across = (dot(ggh, nh) + dot(ggh, nl) + dot(ggl, nh))[:40]
    back = dot(stacked(across), st_hot[...])
    mine2[...] = base + weight * (back[:40] + back[40:])
    c_second = pltpu.make_async_copy(mine2, second_out, out_sem.at[1])
    c_second.start()

    for c in [c_nbr, c_prev, c_next, c_mem] + c_two:
        c.wait_send()
    c_out.wait()
    c_second.wait()


def last_kernel(resid, second_h, pro2_h, resid_out, corr_out, second, pro2, corr, sem):
    loads = [pltpu.make_async_copy(second_h, second, sem.at[0]), pltpu.make_async_copy(pro2_h, pro2, sem.at[1])]
    whole = pltpu.make_async_copy(resid, resid_out, sem.at[2])
    for c in loads:
        c.start()
    whole.start()
    for c in loads:
        c.wait()
    both = stacked(second[...])
    copies = [whole]
    for v in range(5):
        corr[v] = dot(pro2[v * 128 : v * 128 + 128, :], both)[:125]
        c = pltpu.make_async_copy(corr.at[v], corr_out.at[v], sem.at[3 + v])
        c.start()
        copies.append(c)
    for c in copies:
        c.wait()


def shards(
    state, rhs, fine_diag, q_fine, var_mix, mem_count, grp_count, send_mem_idx, send_grp_idx,
    face_src, coarse_diag, q_coarse, g_coarse, owner, coarse_nbr,
):
    ext, lift, rest, rest_lift, pro2, small = tables()
    n_grp = lax.axis_size("grp")
    hbm = pl.BlockSpec(memory_space=pltpu.HBM)
    field = jax.ShapeDtypeStruct((5, 125, 256), F32)
    operands = (
        state, send_mem_idx, send_grp_idx, mem_count, grp_count, jnp.asarray(ext), coarse_nbr, face_src, rhs, fine_diag,
        q_fine, var_mix, jnp.asarray(rest), jnp.asarray(rest_lift), owner.reshape(1, 256), coarse_diag.reshape(40, 256),
        g_coarse.reshape(48, 8), q_coarse, jnp.asarray(small), jnp.asarray(lift),
    )
    resid, second = pl.pallas_call(
        functools.partial(main_kernel, n_grp),
        out_shape=(field, jax.ShapeDtypeStruct((40, 256), F32)),
        in_specs=[hbm] * 20,
        out_specs=(hbm, hbm),
        scratch_shapes=[pltpu.VMEM(a.shape, a.dtype) for a in operands]
        + [
            pltpu.VMEM((640, 256), BF),
            pltpu.VMEM((640, 256), BF),
            pltpu.VMEM((128, 128), F32),
            pltpu.VMEM((1536, 640), BF),
            pltpu.VMEM((256, 1536), BF),
            pltpu.VMEM((2, 128, 256), F32),
            pltpu.VMEM((128, 128), F32),
            pltpu.VMEM((8, 128), jnp.int32),
            pltpu.VMEM((2, 128, 256), F32),
            pltpu.VMEM((128, 128), F32),
            pltpu.VMEM((8, 128), jnp.int32),
            pltpu.VMEM((6, 640, 256), BF),
            pltpu.VMEM((768, 256), BF),
            pltpu.VMEM((768, 256), BF),
            pltpu.VMEM((640, 256), F32),
            pltpu.VMEM((2, 768, 768), BF),
            pltpu.VMEM((256, 256), BF),
            pltpu.VMEM((6, 40, 256), F32),
            pltpu.VMEM((40, 256), F32),
            pltpu.VMEM((2, 80, 768), BF),
            pltpu.VMEM((5, 125, 256), F32),
            pltpu.VMEM((40, 256), F32),
            pltpu.SemaphoreType.DMA((20,)),
            pltpu.SemaphoreType.DMA((9,)),
            pltpu.SemaphoreType.DMA((10,)),
            pltpu.SemaphoreType.DMA((2,)),
        ],
        compiler_params=pltpu.CompilerParams(
            collective_id=0, has_side_effects=True, vmem_limit_bytes=60 * 1024 * 1024
        ),
        name="residual_and_sweeps",
    )(*operands)
    return pl.pallas_call(
        last_kernel,
        out_shape=(field, field),
        in_specs=[hbm, hbm, hbm],
        out_specs=(hbm, hbm),
        scratch_shapes=[
            pltpu.VMEM((40, 256), F32),
            pltpu.VMEM((640, 80), BF),
            pltpu.VMEM((5, 125, 256), F32),
            pltpu.SemaphoreType.DMA((8,)),
        ],
        compiler_params=pltpu.CompilerParams(vmem_limit_bytes=60 * 1024 * 1024),
        name="prolongation",
    )(resid, second, jnp.asarray(pro2))


def solution(mesh):
    whole = ("grp", "mem")
    return jax.shard_map(
        shards,
        mesh=mesh,
        in_specs=(
            P(None, None, whole), P(None, None, whole), P(None, None, whole), P(), P(),
            P(whole, None), P(whole, None), P(whole, None, None), P(whole, None, None), P(None, whole),
            P(None, None, whole), P(), P(), P(whole, None), P(None, whole),
        ),
        out_specs=(P(None, None, whole), P(None, None, whole)),
        check_vma=False,
    )
```

```python
import functools

import jax
import jax.numpy as jnp
import ml_dtypes
import numpy as np
from jax import lax
from jax.experimental import pallas as pl
from jax.experimental.pallas import tpu as pltpu
from jax.sharding import PartitionSpec as P

MESH = pl.DeviceIdType.MESH
HIGH = lax.Precision.HIGHEST
BF = jnp.bfloat16
F32 = jnp.float32


def tables():
    points = np.arange(125)
    coords = [points // 25, points // 5 % 5, points % 5]
    extract = np.zeros((6, 25, 125), np.float32)
    for face in range(6):
        along = face // 2
        others = [c for b, c in enumerate(coords) if b != along]
        index = others[0] * 5 + others[1]
        on_face = coords[along] == 4 * (face % 2)
        extract[face] = (index[None, :] == np.arange(25)[:, None]) & on_face[None, :]
    nodes = -1.0 + 0.5 * np.arange(5)
    basis = np.stack([(1.0 - nodes) / 2.0, (1.0 + nodes) / 2.0], axis=1)
    prolong = np.einsum("ia,jb,kc->ijkabc", basis, basis, basis).reshape(125, 8)
    ext = np.zeros((6, 128, 5, 128), np.float32)
    for v in range(5):
        ext[:, v * 25 : v * 25 + 25, v, :125] = extract
    ext = ext.reshape(768, 640)
    lift = np.ascontiguousarray(ext.T)
    rest = np.zeros((48, 5, 128), np.float32)
    for v in range(5):
        rest[v * 8 : v * 8 + 8, v, :125] = prolong.T
    rest = rest.reshape(48, 640)
    rest_lift = rest @ lift
    pro = np.ascontiguousarray(rest[:40].T)
    pro2 = np.concatenate([pro, pro], axis=1)
    spread = np.zeros((8, 6, 5, 8), np.float32)
    for b in range(8):
        spread[b, :, :, b] = 1.0
    spread = spread.reshape(8, 240)
    gather_a = np.zeros((48, 48), np.float32)
    for v in range(5):
        for f in range(6):
            for a in range(8):
                gather_a[v * 8 + a, f * 8 + a] = 1.0
    same_f = np.zeros((6, 8, 6, 40), np.float32)
    for f in range(6):
        same_f[f, :, f, :] = 1.0
    same_f = same_f.reshape(48, 240)
    same_v = np.zeros((6, 8, 6, 5, 8), np.float32)
    for v in range(5):
        same_v[v, :, :, v, :] = 1.0
    same_v = same_v.reshape(48, 240)
    small = np.zeros((152, 240), np.float32)
    small[0:8] = spread
    small[8:56, :48] = gather_a
    small[56:104] = same_f
    small[104:152] = same_v
    cast = lambda a: np.asarray(a, ml_dtypes.bfloat16)
    return cast(ext), cast(lift), cast(rest), cast(rest_lift), cast(pro2), small


def halves(x):
    hi = x.astype(BF)
    return hi, (x - hi.astype(F32)).astype(BF)


def stacked(x):
    hi = x.astype(BF).astype(F32)
    return jnp.concatenate([hi, x - hi], axis=0).astype(BF)


def dot(a, b):
    return jnp.dot(a, b, preferred_element_type=F32)


def exact(a, b):
    return jnp.dot(a, b, precision=HIGH, preferred_element_type=F32)


def hot(row, base, size):
    places = lax.broadcasted_iota(jnp.int32, (size, row.shape[1]), 0)
    return jnp.where(places == row - base, 1.0, 0.0).astype(BF)


def padded(x):
    return jnp.concatenate([x, jnp.zeros((3, x.shape[1]), F32)], axis=0)


def main_kernel(n_grp, *refs):
    sources, (resid_out, second_out), scratch = refs[:20], refs[20:22], refs[22:]
    (
        st, midx, gidx, mcount, gcount, ext, cnbr, fsrc, rh, dg, q_fine, var_mix,
        rest, rest_lift, owner, cdiag, g_coarse, q_coarse, small, lift,
    ) = scratch[:20]
    (
        uh, ul, qs,
        ohs, tr, snd_g, snd_m, snd_n, rcv_g, rcv_m, rcv_n,
        ohr, nlh, nll, resl, ohc, st_hot, blks, mine, rim, resv, mine2, near_acc,
        in_sem, snd_sem, rcv_sem, out_sem,
    ) = scratch[20:]
    g = lax.axis_index("grp")
    m = lax.axis_index("mem")
    other = 1 - m
    has_prev, has_next = g > 0, g < n_grp - 1
    prev, nxt = jnp.maximum(g - 1, 0), jnp.minimum(g + 1, n_grp - 1)

    loads = [pltpu.make_async_copy(src, scratch[i], in_sem.at[i]) for i, src in enumerate(sources)]
    for c in loads[:8]:
        c.start()
    seen = set()

    def need(*which):
        for i in which:
            if i not in seen:
                seen.add(i)
                loads[i].wait()

    barrier = pltpu.get_barrier_semaphore()
    def greet(device):
        pl.semaphore_signal(barrier, inc=1, device_id=device, device_id_type=MESH)

    greet((g, other))

    @pl.when(has_prev)
    def _():
        greet((prev, 0))
        greet((prev, 1))

    @pl.when(has_next)
    def _():
        greet((nxt, 0))
        greet((nxt, 1))

    @pl.when(jnp.logical_not(has_prev))
    def _():
        rcv_g[0] = jnp.zeros((128, 256), F32)
        blks[0] = jnp.zeros((40, 256), F32)
        blks[1] = jnp.zeros((40, 256), F32)

    @pl.when(jnp.logical_not(has_next))
    def _():
        rcv_g[1] = jnp.zeros((128, 256), F32)
        blks[4] = jnp.zeros((40, 256), F32)
        blks[5] = jnp.zeros((40, 256), F32)

    need(1, 2, 3, 4, 6)
    lane_g = lax.broadcasted_iota(jnp.int32, (1, 256), 1)
    lane_m = lax.broadcasted_iota(jnp.int32, (1, 128), 1)
    for t in range(2):
        row = jnp.where(lane_g < gcount[0:1, t : t + 1], gidx[0, t : t + 1, :], -1)
        ohs[:, t * 256 : t * 256 + 256] = hot(row, 0, 1536)
    mrow = jnp.where(m == 0, midx[0, 1:2, :], midx[0, 0:1, :])
    mlim = jnp.where(m == 0, mcount[0:1, 1:2], mcount[0:1, 0:1])
    ohs[:, 512:640] = hot(jnp.where(lane_m < mlim, mrow, -1), 0, 1536)
    nbr = cnbr[...]
    snd_n[0:6, :] = jnp.where(m == 0, nbr[:, 128:256], nbr[:, 0:128])
    snd_n[6:8, :] = jnp.zeros((2, 128), jnp.int32)

    need(0)
    for c in loads[8:]:
        c.start()
    for v in range(5):
        hi, lo = halves(padded(st[v]))
        uh[v * 128 : v * 128 + 128, :] = hi
        ul[v * 128 : v * 128 + 128, :] = lo
    need(5)
    for f in range(6):
        e = ext[f * 128 : f * 128 + 128, :]
        tr[0:128, f * 256 : f * 256 + 256] = dot(e, uh[...]).astype(BF)
        tr[128:256, f * 256 : f * 256 + 256] = dot(e, ul[...]).astype(BF)

    def remote(src, dst, i, j, device):
        return pltpu.make_async_remote_copy(
            src_ref=src, dst_ref=dst, send_sem=snd_sem.at[i], recv_sem=rcv_sem.at[j],
            device_id=device, device_id_type=MESH,
        )

    pl.semaphore_wait(barrier, 1 + 2 * has_prev.astype(jnp.int32) + 2 * has_next.astype(jnp.int32))
    c_nbr = remote(snd_n, rcv_n, 0, 0, (g, other))
    c_nbr.start()
    picked = dot(tr[...], ohs[:, 0:256])
    snd_g[0] = picked[:128] + picked[128:]
    c_prev = remote(snd_g.at[0], rcv_g.at[1], 1, 1, (prev, m))
    pl.when(has_prev)(c_prev.start)
    picked = dot(tr[...], ohs[:, 256:512])
    snd_g[1] = picked[:128] + picked[128:]
    c_next = remote(snd_g.at[1], rcv_g.at[0], 2, 2, (nxt, m))
    pl.when(has_next)(c_next.start)
    picked = dot(tr[...], ohs[:, 512:640])
    snd_m[...] = picked[:128] + picked[128:]
    c_mem = remote(snd_m, rcv_m, 3, 3, (g, other))
    c_mem.start()

    base_mem = 1536 + other * 128

    def local_faces(f, carry):
        row = fsrc[pl.ds(f, 1), :]
        acc = dot(tr[...], hot(row, 0, 1536))
        at = pl.multiple_of(f * 128, 128)
        nlh[pl.ds(at, 128), :] = acc[:128].astype(BF)
        nll[pl.ds(at, 128), :] = acc[128:].astype(BF)
        ohr[f, 0:256, :] = hot(row, 1792, 256)
        ohr[f, 256:512, :] = hot(row, 2048, 256)
        ohr[f, 512:640, :] = hot(row, base_mem, 128)
        return carry

    need(7)
    lax.fori_loop(0, 6, local_faces, 0)

    need(*range(8, 19))
    qs[...] = jnp.zeros((128, 128), F32)
    qs[0:125, 0:125] = q_fine[...]
    qh, ql = halves(qs[...])
    for v in range(5):
        total = dot(qh, uh[v * 128 : v * 128 + 128, :]) + dot(qh, ul[v * 128 : v * 128 + 128, :])
        total = (total + dot(ql, uh[v * 128 : v * 128 + 128, :]))[:125]
        total = total + dg[v] * st[v]
        for w in range(5):
            total = total + var_mix[v : v + 1, w : w + 1] * st[w]
        resl[v * 128 : v * 128 + 128, :] = padded(rh[v] - total)
    rl_h, rl_l = halves(resl[...])
    rest0 = dot(rest[...], rl_h) + dot(rest[...], rl_l)
    rest0 = rest0 + dot(rest_lift[...], nlh[...]) + dot(rest_lift[...], nll[...])

    own = owner[...].astype(F32)
    before = lax.broadcasted_iota(jnp.int32, (256, 256), 0) < lax.broadcasted_iota(jnp.int32, (256, 256), 1)
    ones_before = dot(jnp.broadcast_to(own, (16, 256)).astype(BF), jnp.where(before, 1.0, 0.0).astype(BF))[0:1]
    ones_before = ones_before.astype(jnp.int32)
    target = jnp.where(owner[...] == 1, 128 + ones_before, lane_g - ones_before)
    st_hot[...] = hot(target, 0, 256)

    gfa = g_coarse[...]
    gg = exact(gfa, small[0:8, :]) * small[56:104, :]
    gg = exact(small[8:56, 0:48], gg) * small[104:152, :]
    ggh, ggl = halves(gg)
    qrep = jnp.concatenate([q_coarse[...]] * 5, axis=0)
    qq = exact(qrep, small[0:8, 0:40]) * small[104:144, 0:40]

    def both_halves(ref):
        hi, lo = halves(ref[...])
        return jnp.concatenate([hi, lo], axis=0)

    c_mem.wait_recv()
    part = both_halves(rcv_m)
    for f in range(6):
        near_acc[f] = dot(part, ohr[f, 512:640, :])
    pl.when(has_next)(c_prev.wait_recv)
    pl.when(has_prev)(c_next.wait_recv)
    parts = [both_halves(rcv_g.at[0]), both_halves(rcv_g.at[1])]
    for f in range(6):
        acc = near_acc[f] + dot(parts[0], ohr[f, 0:256, :]) + dot(parts[1], ohr[f, 256:512, :])
        nh, nl = acc[:128].astype(BF), acc[128:].astype(BF)
        rlf = rest_lift[:, f * 128 : f * 128 + 128]
        rest0 = rest0 + dot(rlf, nh) + dot(rlf, nl)
        nlh[f * 128 : f * 128 + 128, :] += nh
        nll[f * 128 : f * 128 + 128, :] += nl
    cd = cdiag[...]
    first = (0.8 * 0.064) * rest0[:40] / cd
    packed = lax.dot_general(stacked(first), st_hot[...], (((1,), (1,)), ((), ())), preferred_element_type=F32)
    mine[...] = packed[:40] + packed[40:]
    c_two = []
    for i, (ok, d, place) in enumerate(
        [
            (has_prev, (prev, 0), 4 + m),
            (has_prev, (prev, 1), 4 + m),
            (has_next, (nxt, 0), m),
            (has_next, (nxt, 1), m),
            (None, (g, other), 2 + m),
        ]
    ):
        c = remote(mine, blks.at[place], 4 + i, 4 + place, d)
        c_two.append((ok, c))
        if ok is None:
            c.start()
        else:
            pl.when(ok)(c.start)

    need(19)
    for v in range(5):
        lf = lift[v * 128 : v * 128 + 128, :]
        full = resl[v * 128 : v * 128 + 128, :] + dot(lf, nlh[...]) + dot(lf, nll[...])
        resv[v] = full[:125]
    c_out = pltpu.make_async_copy(resv, resid_out, out_sem.at[0])
    c_out.start()
    inner = exact(qq, first)
    weight = 0.8 / cd
    base = 1.2 * first - weight * inner

    c_nbr.wait_recv()
    own_nbr = jnp.where(m == 0, nbr[:, 0:128], nbr[:, 128:256])
    got_nbr = rcv_n[0:6, :]
    for o in range(2):
        lists = jnp.where(m == o, own_nbr, got_nbr)
        for f in range(6):
            ohc[o, :, f * 128 : f * 128 + 128] = hot(lists[f : f + 1, :], 0, 768)

    def arrived(place):
        remote(mine, blks.at[place], 4, 4 + place, (g, other)).wait_recv()

    arrived(2 + other)

    @pl.when(has_prev)
    def _():
        arrived(0)
        arrived(1)

    @pl.when(has_next)
    def _():
        arrived(4)
        arrived(5)

    blks[2 + m] = mine[...]
    for j in range(6):
        both = stacked(blks[j])
        rim[0, :, j * 128 : j * 128 + 128] = both[:, 0:128]
        rim[1, :, j * 128 : j * 128 + 128] = both[:, 128:256]
    nhs, nls = [], []
    for o in range(2):
        near = dot(rim[o], ohc[o])
        nhs.append(jnp.concatenate([near[:40, f * 128 : f * 128 + 128] for f in range(6)], axis=0))
        nls.append(jnp.concatenate([near[40:, f * 128 : f * 128 + 128] for f in range(6)], axis=0))
    nh = jnp.concatenate(nhs, axis=1).astype(BF)
    nl = jnp.concatenate(nls, axis=1).astype(BF)
    across = (dot(ggh, nh) + dot(ggh, nl) + dot(ggl, nh))[:40]
    back = dot(stacked(across), st_hot[...])
    mine2[...] = base + weight * (back[:40] + back[40:])
    c_second = pltpu.make_async_copy(mine2, second_out, out_sem.at[1])
    c_second.start()

    for ok, c in [(None, c_nbr), (has_prev, c_prev), (has_next, c_next), (None, c_mem)] + c_two:
        if ok is None:
            c.wait_send()
        else:
            pl.when(ok)(c.wait_send)
    c_out.wait()
    c_second.wait()


def last_kernel(resid, second_h, pro2_h, resid_out, corr_out, second, pro2, corr, held, sem):
    loads = [pltpu.make_async_copy(second_h, second, sem.at[0]), pltpu.make_async_copy(pro2_h, pro2, sem.at[1])]
    loads += [pltpu.make_async_copy(resid.at[v], held.at[v], sem.at[2 + v]) for v in range(5)]
    for c in loads:
        c.start()
    copies = []
    for v in range(5):
        loads[2 + v].wait()
        c = pltpu.make_async_copy(held.at[v], resid_out.at[v], sem.at[7 + v])
        c.start()
        copies.append(c)
    loads[0].wait()
    loads[1].wait()
    both = stacked(second[...])
    for v in range(5):
        corr[v] = dot(pro2[v * 128 : v * 128 + 128, :], both)[:125]
        c = pltpu.make_async_copy(corr.at[v], corr_out.at[v], sem.at[12 + v])
        c.start()
        copies.append(c)
    for c in copies:
        c.wait()


def shards(
    state, rhs, fine_diag, q_fine, var_mix, mem_count, grp_count, send_mem_idx, send_grp_idx,
    face_src, coarse_diag, q_coarse, g_coarse, owner, coarse_nbr,
):
    ext, lift, rest, rest_lift, pro2, small = tables()
    n_grp = lax.axis_size("grp")
    hbm = pl.BlockSpec(memory_space=pltpu.HBM)
    field = jax.ShapeDtypeStruct((5, 125, 256), F32)
    operands = (
        state, send_mem_idx, send_grp_idx, mem_count, grp_count, jnp.asarray(ext), coarse_nbr, face_src, rhs, fine_diag,
        q_fine, var_mix, jnp.asarray(rest), jnp.asarray(rest_lift), owner.reshape(1, 256), coarse_diag.reshape(40, 256),
        g_coarse.reshape(48, 8), q_coarse, jnp.asarray(small), jnp.asarray(lift),
    )
    resid, second = pl.pallas_call(
        functools.partial(main_kernel, n_grp),
        out_shape=(field, jax.ShapeDtypeStruct((40, 256), F32)),
        in_specs=[hbm] * 20,
        out_specs=(hbm, hbm),
        scratch_shapes=[pltpu.VMEM(a.shape, a.dtype) for a in operands]
        + [
            pltpu.VMEM((640, 256), BF),
            pltpu.VMEM((640, 256), BF),
            pltpu.VMEM((128, 128), F32),
            pltpu.VMEM((1536, 640), BF),
            pltpu.VMEM((256, 1536), BF),
            pltpu.VMEM((2, 128, 256), F32),
            pltpu.VMEM((128, 128), F32),
            pltpu.VMEM((8, 128), jnp.int32),
            pltpu.VMEM((2, 128, 256), F32),
            pltpu.VMEM((128, 128), F32),
            pltpu.VMEM((8, 128), jnp.int32),
            pltpu.VMEM((6, 640, 256), BF),
            pltpu.VMEM((768, 256), BF),
            pltpu.VMEM((768, 256), BF),
            pltpu.VMEM((640, 256), F32),
            pltpu.VMEM((2, 768, 768), BF),
            pltpu.VMEM((256, 256), BF),
            pltpu.VMEM((6, 40, 256), F32),
            pltpu.VMEM((40, 256), F32),
            pltpu.VMEM((2, 80, 768), BF),
            pltpu.VMEM((5, 125, 256), F32),
            pltpu.VMEM((40, 256), F32),
            pltpu.VMEM((6, 256, 256), F32),
            pltpu.SemaphoreType.DMA((20,)),
            pltpu.SemaphoreType.DMA((9,)),
            pltpu.SemaphoreType.DMA((10,)),
            pltpu.SemaphoreType.DMA((2,)),
        ],
        compiler_params=pltpu.CompilerParams(
            collective_id=0, has_side_effects=True, vmem_limit_bytes=60 * 1024 * 1024
        ),
        name="residual_and_sweeps",
    )(*operands)
    return pl.pallas_call(
        last_kernel,
        out_shape=(field, field),
        in_specs=[hbm, hbm, hbm],
        out_specs=(hbm, hbm),
        scratch_shapes=[
            pltpu.VMEM((40, 256), F32),
            pltpu.VMEM((640, 80), BF),
            pltpu.VMEM((5, 125, 256), F32),
            pltpu.VMEM((5, 125, 256), F32),
            pltpu.SemaphoreType.DMA((17,)),
        ],
        compiler_params=pltpu.CompilerParams(vmem_limit_bytes=60 * 1024 * 1024),
        name="prolongation",
    )(resid, second, jnp.asarray(pro2))


def solution(mesh):
    whole = ("grp", "mem")
    return jax.shard_map(
        shards,
        mesh=mesh,
        in_specs=(
            P(None, None, whole), P(None, None, whole), P(None, None, whole), P(), P(),
            P(whole, None), P(whole, None), P(whole, None, None), P(whole, None, None), P(None, whole),
            P(None, None, whole), P(), P(), P(whole, None), P(None, whole),
        ),
        out_specs=(P(None, None, whole), P(None, None, whole)),
        check_vma=False,
    )
```

```python
import functools

import jax
import jax.numpy as jnp
import ml_dtypes
import numpy as np
from jax import lax
from jax.experimental import pallas as pl
from jax.experimental.pallas import tpu as pltpu
from jax.sharding import PartitionSpec as P

MESH = pl.DeviceIdType.MESH
HIGH = lax.Precision.HIGHEST
BF = jnp.bfloat16
F32 = jnp.float32


def tables():
    points = np.arange(125)
    coords = [points // 25, points // 5 % 5, points % 5]
    extract = np.zeros((6, 25, 125), np.float32)
    for face in range(6):
        along = face // 2
        others = [c for b, c in enumerate(coords) if b != along]
        index = others[0] * 5 + others[1]
        on_face = coords[along] == 4 * (face % 2)
        extract[face] = (index[None, :] == np.arange(25)[:, None]) & on_face[None, :]
    nodes = -1.0 + 0.5 * np.arange(5)
    basis = np.stack([(1.0 - nodes) / 2.0, (1.0 + nodes) / 2.0], axis=1)
    prolong = np.einsum("ia,jb,kc->ijkabc", basis, basis, basis).reshape(125, 8)
    ext = np.zeros((6, 128, 5, 128), np.float32)
    for v in range(5):
        ext[:, v * 25 : v * 25 + 25, v, :125] = extract
    ext = ext.reshape(768, 640)
    places = np.full((8, 640), -1, np.int32)
    for face in range(6):
        block = ext[face * 128 : face * 128 + 128]
        places[face] = np.where(block.any(axis=0), block.argmax(axis=0), -1)
    lift = np.ascontiguousarray(ext.T)
    rest = np.zeros((48, 5, 128), np.float32)
    for v in range(5):
        rest[v * 8 : v * 8 + 8, v, :125] = prolong.T
    rest = rest.reshape(48, 640)
    rest_lift = rest @ lift
    by_face = rest_lift.reshape(48, 6, 128).transpose(1, 0, 2).reshape(288, 128)
    by_face = np.concatenate([by_face, by_face], axis=1)
    pro = np.ascontiguousarray(rest[:40].T)
    pro2 = np.concatenate([pro, pro], axis=1)
    spread = np.zeros((8, 6, 5, 8), np.float32)
    for b in range(8):
        spread[b, :, :, b] = 1.0
    spread = spread.reshape(8, 240)
    gather_a = np.zeros((48, 48), np.float32)
    for v in range(5):
        for f in range(6):
            for a in range(8):
                gather_a[v * 8 + a, f * 8 + a] = 1.0
    same_f = np.zeros((6, 8, 6, 40), np.float32)
    for f in range(6):
        same_f[f, :, f, :] = 1.0
    same_f = same_f.reshape(48, 240)
    same_v = np.zeros((6, 8, 6, 5, 8), np.float32)
    for v in range(5):
        same_v[v, :, :, v, :] = 1.0
    same_v = same_v.reshape(48, 240)
    small = np.zeros((152, 240), np.float32)
    small[0:8] = spread
    small[8:56, :48] = gather_a
    small[56:104] = same_f
    small[104:152] = same_v
    cast = lambda a: np.asarray(a, ml_dtypes.bfloat16)
    return places, cast(lift), cast(rest), cast(rest_lift), cast(by_face), cast(pro2), small


def halves(x):
    hi = x.astype(BF)
    return hi, (x - hi.astype(F32)).astype(BF)


def stacked(x):
    hi = x.astype(BF).astype(F32)
    return jnp.concatenate([hi, x - hi], axis=0).astype(BF)


def dot(a, b):
    return jnp.dot(a, b, preferred_element_type=F32)


def exact(a, b):
    return jnp.dot(a, b, precision=HIGH, preferred_element_type=F32)


def hot(row, base, size):
    row = (row - base).astype(jnp.int16)
    places = lax.broadcasted_iota(jnp.int16, (size, row.shape[1]), 0)
    return jnp.where(places == row, jnp.ones((), BF), jnp.zeros((), BF))


def padded(x):
    return jnp.concatenate([x, jnp.zeros((3, x.shape[1]), F32)], axis=0)


def main_kernel(n_grp, *refs):
    sources, (resid_out, second_out), scratch = refs[:21], refs[21:23], refs[23:]
    (
        st, midx, gidx, mcount, gcount, places, cnbr, fsrc, rh, dg, q_fine, var_mix,
        rest, rest_lift, owner, cdiag, g_coarse, q_coarse, small, by_face, lift,
    ) = scratch[:21]
    (
        uh, ul, qs,
        ohs, tr, snd_g, snd_m, snd_n, rcv_g, rcv_m, rcv_n,
        ohr, nlh, nll, resl, ohc, st_hot, blks, mine, rim, resv, mine2, ext, arrived_hl, zs,
        in_sem, snd_sem, rcv_sem, out_sem,
    ) = scratch[21:]
    g = lax.axis_index("grp")
    m = lax.axis_index("mem")
    other = 1 - m
    has_prev, has_next = g > 0, g < n_grp - 1
    prev, nxt = jnp.maximum(g - 1, 0), jnp.minimum(g + 1, n_grp - 1)

    loads = [pltpu.make_async_copy(src, scratch[i], in_sem.at[i]) for i, src in enumerate(sources)]
    for c in loads[:8]:
        c.start()
    seen = set()

    def need(*which):
        for i in which:
            if i not in seen:
                seen.add(i)
                loads[i].wait()

    barrier = pltpu.get_barrier_semaphore()
    def greet(device):
        pl.semaphore_signal(barrier, inc=1, device_id=device, device_id_type=MESH)

    greet((g, other))

    @pl.when(has_prev)
    def _():
        greet((prev, 0))
        greet((prev, 1))

    @pl.when(has_next)
    def _():
        greet((nxt, 0))
        greet((nxt, 1))

    @pl.when(jnp.logical_not(has_prev))
    def _():
        rcv_g[0] = jnp.zeros((128, 256), F32)
        blks[0] = jnp.zeros((40, 256), F32)
        blks[1] = jnp.zeros((40, 256), F32)

    @pl.when(jnp.logical_not(has_next))
    def _():
        rcv_g[1] = jnp.zeros((128, 256), F32)
        blks[4] = jnp.zeros((40, 256), F32)
        blks[5] = jnp.zeros((40, 256), F32)

    need(1, 2, 3, 4, 5, 6)
    lane_g = lax.broadcasted_iota(jnp.int32, (1, 256), 1)
    lane_m = lax.broadcasted_iota(jnp.int32, (1, 128), 1)
    for t in range(2):
        row = jnp.where(lane_g < gcount[0:1, t : t + 1], gidx[0, t : t + 1, :], -1)
        ohs[:, t * 256 : t * 256 + 256] = hot(row, 0, 1536)
    mrow = jnp.where(m == 0, midx[0, 1:2, :], midx[0, 0:1, :])
    mlim = jnp.where(m == 0, mcount[0:1, 1:2], mcount[0:1, 0:1])
    ohs[:, 512:640] = hot(jnp.where(lane_m < mlim, mrow, -1), 0, 1536)
    nbr = cnbr[...]
    snd_n[0:6, :] = jnp.where(m == 0, nbr[:, 128:256], nbr[:, 0:128])
    snd_n[6:8, :] = jnp.zeros((2, 128), jnp.int32)

    for f in range(6):
        ext[f * 128 : f * 128 + 128, :] = hot(places[f : f + 1, :], 0, 128)

    need(0)
    for c in loads[8:]:
        c.start()
    for v in range(5):
        hi, lo = halves(padded(st[v]))
        uh[v * 128 : v * 128 + 128, :] = hi
        ul[v * 128 : v * 128 + 128, :] = lo
    for f in range(6):
        e = ext[f * 128 : f * 128 + 128, :]
        tr[0:128, f * 256 : f * 256 + 256] = dot(e, uh[...]).astype(BF)
        tr[128:256, f * 256 : f * 256 + 256] = dot(e, ul[...]).astype(BF)

    def remote(src, dst, i, j, device):
        return pltpu.make_async_remote_copy(
            src_ref=src, dst_ref=dst, send_sem=snd_sem.at[i], recv_sem=rcv_sem.at[j],
            device_id=device, device_id_type=MESH,
        )

    pl.semaphore_wait(barrier, 1 + 2 * has_prev.astype(jnp.int32) + 2 * has_next.astype(jnp.int32))
    c_nbr = remote(snd_n, rcv_n, 0, 0, (g, other))
    c_nbr.start()
    picked = dot(tr[...], ohs[:, 0:256])
    snd_g[0] = picked[:128] + picked[128:]
    c_prev = remote(snd_g.at[0], rcv_g.at[1], 1, 1, (prev, m))
    pl.when(has_prev)(c_prev.start)
    picked = dot(tr[...], ohs[:, 256:512])
    snd_g[1] = picked[:128] + picked[128:]
    c_next = remote(snd_g.at[1], rcv_g.at[0], 2, 2, (nxt, m))
    pl.when(has_next)(c_next.start)
    picked = dot(tr[...], ohs[:, 512:640])
    snd_m[...] = picked[:128] + picked[128:]
    c_mem = remote(snd_m, rcv_m, 3, 3, (g, other))
    c_mem.start()

    base_mem = 1536 + other * 128

    def local_faces(f, carry):
        row = fsrc[pl.ds(f, 1), :]
        acc = dot(tr[...], hot(row, 0, 1536))
        at = pl.multiple_of(f * 128, 128)
        nlh[pl.ds(at, 128), :] = acc[:128].astype(BF)
        nll[pl.ds(at, 128), :] = acc[128:].astype(BF)
        ohr[f, 0:256, :] = hot(row, 1792, 256)
        ohr[f, 256:512, :] = hot(row, 2048, 256)
        ohr[f, 512:640, :] = hot(row, base_mem, 128)
        return carry

    need(7)
    lax.fori_loop(0, 6, local_faces, 0)

    need(*range(8, 20))
    qs[...] = jnp.zeros((128, 128), F32)
    qs[0:125, 0:125] = q_fine[...]
    qh, ql = halves(qs[...])
    for v in range(5):
        total = dot(qh, uh[v * 128 : v * 128 + 128, :]) + dot(qh, ul[v * 128 : v * 128 + 128, :])
        total = (total + dot(ql, uh[v * 128 : v * 128 + 128, :]))[:125]
        total = total + dg[v] * st[v]
        for w in range(5):
            total = total + var_mix[v : v + 1, w : w + 1] * st[w]
        resl[v * 128 : v * 128 + 128, :] = padded(rh[v] - total)
    rl_h, rl_l = halves(resl[...])
    rest0 = dot(rest[...], rl_h) + dot(rest[...], rl_l)
    rest0 = rest0 + dot(rest_lift[...], nlh[...]) + dot(rest_lift[...], nll[...])
    rest0 = rest0[:40]

    own = owner[...].astype(F32)
    before = lax.broadcasted_iota(jnp.int32, (256, 256), 0) < lax.broadcasted_iota(jnp.int32, (256, 256), 1)
    ones_before = dot(jnp.broadcast_to(own, (16, 256)).astype(BF), jnp.where(before, 1.0, 0.0).astype(BF))[0:1]
    ones_before = ones_before.astype(jnp.int32)
    target = jnp.where(owner[...] == 1, 128 + ones_before, lane_g - ones_before)
    st_hot[...] = hot(target, 0, 256)

    gfa = g_coarse[...]
    gg = exact(gfa, small[0:8, :]) * small[56:104, :]
    gg = exact(small[8:56, 0:48], gg) * small[104:152, :]
    ggh, ggl = halves(gg)
    qrep = jnp.concatenate([q_coarse[...]] * 5, axis=0)
    qq = exact(qrep, small[0:8, 0:40]) * small[104:144, 0:40]

    c_nbr.wait_recv()
    own_nbr = jnp.where(m == 0, nbr[:, 0:128], nbr[:, 128:256])
    got_nbr = rcv_n[0:6, :]
    for o in range(2):
        lists = jnp.where(m == o, own_nbr, got_nbr)
        for f in range(6):
            ohc[o, :, f * 128 : f * 128 + 128] = hot(lists[f : f + 1, :], 0, 768)

    def take(ref, at, width):
        hi, lo = halves(ref[...])
        arrived_hl[0:128, at : at + width] = hi
        arrived_hl[128:256, at : at + width] = lo

    c_mem.wait_recv()
    take(rcv_m, 512, 128)
    pl.when(has_next)(c_prev.wait_recv)
    pl.when(has_prev)(c_next.wait_recv)
    take(rcv_g.at[0], 0, 256)
    take(rcv_g.at[1], 256, 256)
    zs[...] = dot(by_face[...], arrived_hl[...])
    for f in range(6):
        part = dot(stacked(zs[f * 48 : f * 48 + 40, :]), ohr[f])
        rest0 = rest0 + (part[:40] + part[40:])
    cd = cdiag[...]
    first = (0.8 * 0.064) * rest0 / cd
    packed = lax.dot_general(stacked(first), st_hot[...], (((1,), (1,)), ((), ())), preferred_element_type=F32)
    mine[...] = packed[:40] + packed[40:]
    c_two = []
    for i, (ok, d, place) in enumerate(
        [
            (has_prev, (prev, 0), 4 + m),
            (has_prev, (prev, 1), 4 + m),
            (has_next, (nxt, 0), m),
            (has_next, (nxt, 1), m),
            (None, (g, other), 2 + m),
        ]
    ):
        c = remote(mine, blks.at[place], 4 + i, 4 + place, d)
        c_two.append((ok, c))
        if ok is None:
            c.start()
        else:
            pl.when(ok)(c.start)

    for f in range(6):
        acc = dot(arrived_hl[...], ohr[f])
        nlh[f * 128 : f * 128 + 128, :] += acc[:128].astype(BF)
        nll[f * 128 : f * 128 + 128, :] += acc[128:].astype(BF)
    need(20)
    for v in range(5):
        lf = lift[v * 128 : v * 128 + 128, :]
        full = resl[v * 128 : v * 128 + 128, :] + dot(lf, nlh[...]) + dot(lf, nll[...])
        resv[v] = full[:125]
    c_out = pltpu.make_async_copy(resv, resid_out, out_sem.at[0])
    c_out.start()
    inner = exact(qq, first)
    weight = 0.8 / cd
    base = 1.2 * first - weight * inner

    def arrived(place):
        remote(mine, blks.at[place], 4, 4 + place, (g, other)).wait_recv()

    arrived(2 + other)

    @pl.when(has_prev)
    def _():
        arrived(0)
        arrived(1)

    @pl.when(has_next)
    def _():
        arrived(4)
        arrived(5)

    blks[2 + m] = mine[...]
    for j in range(6):
        both = stacked(blks[j])
        rim[0, :, j * 128 : j * 128 + 128] = both[:, 0:128]
        rim[1, :, j * 128 : j * 128 + 128] = both[:, 128:256]
    nhs, nls = [], []
    for o in range(2):
        near = dot(rim[o], ohc[o])
        nhs.append(jnp.concatenate([near[:40, f * 128 : f * 128 + 128] for f in range(6)], axis=0))
        nls.append(jnp.concatenate([near[40:, f * 128 : f * 128 + 128] for f in range(6)], axis=0))
    nh = jnp.concatenate(nhs, axis=1).astype(BF)
    nl = jnp.concatenate(nls, axis=1).astype(BF)
    across = (dot(ggh, nh) + dot(ggh, nl) + dot(ggl, nh))[:40]
    back = dot(stacked(across), st_hot[...])
    mine2[...] = base + weight * (back[:40] + back[40:])
    c_second = pltpu.make_async_copy(mine2, second_out, out_sem.at[1])
    c_second.start()

    for ok, c in [(None, c_nbr), (has_prev, c_prev), (has_next, c_next), (None, c_mem)] + c_two:
        if ok is None:
            c.wait_send()
        else:
            pl.when(ok)(c.wait_send)
    c_out.wait()
    c_second.wait()


def last_kernel(resid, second_h, pro2_h, resid_out, corr_out, second, pro2, corr, held, sem):
    loads = [pltpu.make_async_copy(second_h, second, sem.at[0]), pltpu.make_async_copy(pro2_h, pro2, sem.at[1])]
    loads += [pltpu.make_async_copy(resid.at[v], held.at[v], sem.at[2 + v]) for v in range(5)]
    for c in loads:
        c.start()
    copies = []
    for v in range(5):
        loads[2 + v].wait()
        c = pltpu.make_async_copy(held.at[v], resid_out.at[v], sem.at[7 + v])
        c.start()
        copies.append(c)
    loads[0].wait()
    loads[1].wait()
    both = stacked(second[...])
    for v in range(5):
        corr[v] = dot(pro2[v * 128 : v * 128 + 128, :], both)[:125]
        c = pltpu.make_async_copy(corr.at[v], corr_out.at[v], sem.at[12 + v])
        c.start()
        copies.append(c)
    for c in copies:
        c.wait()


def shards(
    state, rhs, fine_diag, q_fine, var_mix, mem_count, grp_count, send_mem_idx, send_grp_idx,
    face_src, coarse_diag, q_coarse, g_coarse, owner, coarse_nbr,
):
    places, lift, rest, rest_lift, by_face, pro2, small = tables()
    n_grp = lax.axis_size("grp")
    hbm = pl.BlockSpec(memory_space=pltpu.HBM)
    field = jax.ShapeDtypeStruct((5, 125, 256), F32)
    operands = (
        state, send_mem_idx, send_grp_idx, mem_count, grp_count, jnp.asarray(places), coarse_nbr, face_src, rhs, fine_diag,
        q_fine, var_mix, jnp.asarray(rest), jnp.asarray(rest_lift), owner.reshape(1, 256), coarse_diag.reshape(40, 256),
        g_coarse.reshape(48, 8), q_coarse, jnp.asarray(small), jnp.asarray(by_face), jnp.asarray(lift),
    )
    resid, second = pl.pallas_call(
        functools.partial(main_kernel, n_grp),
        out_shape=(field, jax.ShapeDtypeStruct((40, 256), F32)),
        in_specs=[hbm] * 21,
        out_specs=(hbm, hbm),
        scratch_shapes=[pltpu.VMEM(a.shape, a.dtype) for a in operands]
        + [
            pltpu.VMEM((640, 256), BF),
            pltpu.VMEM((640, 256), BF),
            pltpu.VMEM((128, 128), F32),
            pltpu.VMEM((1536, 640), BF),
            pltpu.VMEM((256, 1536), BF),
            pltpu.VMEM((2, 128, 256), F32),
            pltpu.VMEM((128, 128), F32),
            pltpu.VMEM((8, 128), jnp.int32),
            pltpu.VMEM((2, 128, 256), F32),
            pltpu.VMEM((128, 128), F32),
            pltpu.VMEM((8, 128), jnp.int32),
            pltpu.VMEM((6, 640, 256), BF),
            pltpu.VMEM((768, 256), BF),
            pltpu.VMEM((768, 256), BF),
            pltpu.VMEM((640, 256), F32),
            pltpu.VMEM((2, 768, 768), BF),
            pltpu.VMEM((256, 256), BF),
            pltpu.VMEM((6, 40, 256), F32),
            pltpu.VMEM((40, 256), F32),
            pltpu.VMEM((2, 80, 768), BF),
            pltpu.VMEM((5, 125, 256), F32),
            pltpu.VMEM((40, 256), F32),
            pltpu.VMEM((768, 640), BF),
            pltpu.VMEM((256, 640), BF),
            pltpu.VMEM((288, 640), F32),
            pltpu.SemaphoreType.DMA((21,)),
            pltpu.SemaphoreType.DMA((9,)),
            pltpu.SemaphoreType.DMA((10,)),
            pltpu.SemaphoreType.DMA((2,)),
        ],
        compiler_params=pltpu.CompilerParams(
            collective_id=0, has_side_effects=True, vmem_limit_bytes=60 * 1024 * 1024
        ),
        name="residual_and_sweeps",
    )(*operands)
    return pl.pallas_call(
        last_kernel,
        out_shape=(field, field),
        in_specs=[hbm, hbm, hbm],
        out_specs=(hbm, hbm),
        scratch_shapes=[
            pltpu.VMEM((40, 256), F32),
            pltpu.VMEM((640, 80), BF),
            pltpu.VMEM((5, 125, 256), F32),
            pltpu.VMEM((5, 125, 256), F32),
            pltpu.SemaphoreType.DMA((17,)),
        ],
        compiler_params=pltpu.CompilerParams(vmem_limit_bytes=60 * 1024 * 1024),
        name="prolongation",
    )(resid, second, jnp.asarray(pro2))


def solution(mesh):
    whole = ("grp", "mem")
    return jax.shard_map(
        shards,
        mesh=mesh,
        in_specs=(
            P(None, None, whole), P(None, None, whole), P(None, None, whole), P(), P(),
            P(whole, None), P(whole, None), P(whole, None, None), P(whole, None, None), P(None, whole),
            P(None, None, whole), P(), P(), P(whole, None), P(None, whole),
        ),
        out_specs=(P(None, None, whole), P(None, None, whole)),
        check_vma=False,
    )
```

```python
import functools

import jax
import jax.numpy as jnp
import ml_dtypes
import numpy as np
from jax import lax
from jax.experimental import pallas as pl
from jax.experimental.pallas import tpu as pltpu
from jax.sharding import PartitionSpec as P

MESH = pl.DeviceIdType.MESH
HIGH = lax.Precision.HIGHEST
BF = jnp.bfloat16
F32 = jnp.float32


def tables():
    points = np.arange(125)
    coords = [points // 25, points // 5 % 5, points % 5]
    extract = np.zeros((6, 25, 125), np.float32)
    for face in range(6):
        along = face // 2
        others = [c for b, c in enumerate(coords) if b != along]
        index = others[0] * 5 + others[1]
        on_face = coords[along] == 4 * (face % 2)
        extract[face] = (index[None, :] == np.arange(25)[:, None]) & on_face[None, :]
    nodes = -1.0 + 0.5 * np.arange(5)
    basis = np.stack([(1.0 - nodes) / 2.0, (1.0 + nodes) / 2.0], axis=1)
    prolong = np.einsum("ia,jb,kc->ijkabc", basis, basis, basis).reshape(125, 8)
    ext = np.zeros((6, 128, 5, 128), np.float32)
    for v in range(5):
        ext[:, v * 25 : v * 25 + 25, v, :125] = extract
    ext = ext.reshape(768, 640)
    places = np.full((8, 640), -1, np.int32)
    for face in range(6):
        block = ext[face * 128 : face * 128 + 128]
        places[face] = np.where(block.any(axis=0), block.argmax(axis=0), -1)
    lift = np.ascontiguousarray(ext.T)
    rest = np.zeros((48, 5, 128), np.float32)
    for v in range(5):
        rest[v * 8 : v * 8 + 8, v, :125] = prolong.T
    rest = rest.reshape(48, 640)
    rest_lift = rest @ lift
    by_face = rest_lift.reshape(48, 6, 128).transpose(1, 0, 2).reshape(288, 128)
    by_face = np.concatenate([by_face, by_face], axis=1)
    pro2 = np.concatenate([rest[:8, :128].T, rest[:8, :128].T], axis=1)
    spread = np.zeros((8, 6, 5, 8), np.float32)
    for b in range(8):
        spread[b, :, :, b] = 1.0
    spread = spread.reshape(8, 240)
    gather_a = np.zeros((48, 48), np.float32)
    for v in range(5):
        for f in range(6):
            for a in range(8):
                gather_a[v * 8 + a, f * 8 + a] = 1.0
    same_f = np.zeros((6, 8, 6, 40), np.float32)
    for f in range(6):
        same_f[f, :, f, :] = 1.0
    same_f = same_f.reshape(48, 240)
    same_v = np.zeros((6, 8, 6, 5, 8), np.float32)
    for v in range(5):
        same_v[v, :, :, v, :] = 1.0
    same_v = same_v.reshape(48, 240)
    small = np.zeros((152, 240), np.float32)
    small[0:8] = spread
    small[8:56, :48] = gather_a
    small[56:104] = same_f
    small[104:152] = same_v
    cast = lambda a: np.asarray(a, ml_dtypes.bfloat16)
    return places, cast(lift), cast(rest), cast(rest_lift), cast(by_face), cast(pro2), small


def halves(x):
    hi = x.astype(BF)
    return hi, (x - hi.astype(F32)).astype(BF)


def stacked(x):
    hi = x.astype(BF).astype(F32)
    return jnp.concatenate([hi, x - hi], axis=0).astype(BF)


def dot(a, b):
    return jnp.dot(a, b, preferred_element_type=F32)


def exact(a, b):
    return jnp.dot(a, b, precision=HIGH, preferred_element_type=F32)


def hot(row, base, size):
    row = (row - base).astype(jnp.int16)
    places = lax.broadcasted_iota(jnp.int16, (size, row.shape[1]), 0)
    return jnp.where(places == row, jnp.ones((), BF), jnp.zeros((), BF))


def padded(x):
    return jnp.concatenate([x, jnp.zeros((3, x.shape[1]), F32)], axis=0)


def main_kernel(n_grp, *refs):
    sources, (resid_out, second_out), scratch = refs[:21], refs[21:23], refs[23:]
    (
        st, midx, gidx, mcount, gcount, places, cnbr, fsrc, rh, dg, q_fine, var_mix,
        rest, rest_lift, owner, cdiag, g_coarse, q_coarse, small, by_face, lift,
    ) = scratch[:21]
    (
        uh, ul, qs,
        ohs, ohm, tr, snd_g, snd_m, snd_n, rcv_g, rcv_m, rcv_n,
        ohr, ohrm, nlh, nll, resl, ohc, st_hot, blks, mine, resv, mine2, ext, arr_g, arr_m,
        in_sem, st_sem, snd_sem, rcv_sem, out_sem,
    ) = scratch[21:]
    g = lax.axis_index("grp")
    m = lax.axis_index("mem")
    other = 1 - m
    has_prev, has_next = g > 0, g < n_grp - 1
    far = jnp.where(lax.rem(g, 4) == 3, 1, 0)
    prev, nxt = jnp.maximum(g - 1, 0), jnp.minimum(g + 1, n_grp - 1)

    loads = [None] + [pltpu.make_async_copy(sources[i], scratch[i], in_sem.at[i]) for i in range(1, 21)]
    fields = [pltpu.make_async_copy(sources[0].at[v], st.at[v], st_sem.at[v]) for v in range(5)]
    for c in loads[1:7] + fields + loads[7:8]:
        c.start()
    seen = set()

    def need(*which):
        for i in which:
            if i not in seen:
                seen.add(i)
                loads[i].wait()

    barrier = pltpu.get_barrier_semaphore()
    def greet(device):
        pl.semaphore_signal(barrier, inc=1, device_id=device, device_id_type=MESH)

    greet((g, other))

    @pl.when(has_prev)
    def _():
        greet((prev, 0))
        greet((prev, 1))

    @pl.when(has_next)
    def _():
        greet((nxt, 0))
        greet((nxt, 1))

    @pl.when(jnp.logical_not(has_prev))
    def _():
        rcv_g[0] = jnp.zeros((128, 256), F32)
        blks[0] = jnp.zeros((40, 256), F32)
        blks[1] = jnp.zeros((40, 256), F32)

    @pl.when(jnp.logical_not(has_next))
    def _():
        rcv_g[1] = jnp.zeros((128, 256), F32)
        blks[4] = jnp.zeros((40, 256), F32)
        blks[5] = jnp.zeros((40, 256), F32)

    need(1, 2, 3, 4, 5, 6)
    lane_g = lax.broadcasted_iota(jnp.int32, (1, 256), 1)
    lane_m = lax.broadcasted_iota(jnp.int32, (1, 128), 1)
    for t in range(2):
        row = jnp.where(lane_g < gcount[0:1, t : t + 1], gidx[0, t : t + 1, :], -1)
        ohs[t] = hot(row, 0, 1536)
    mrow = jnp.where(m == 0, midx[0, 1:2, :], midx[0, 0:1, :])
    mlim = jnp.where(m == 0, mcount[0:1, 1:2], mcount[0:1, 0:1])
    ohm[...] = hot(jnp.where(lane_m < mlim, mrow, -1), 0, 1536)
    nbr = cnbr[...]
    snd_n[0:6, :] = jnp.where(m == 0, nbr[:, 128:256], nbr[:, 0:128])
    snd_n[6:8, :] = jnp.zeros((2, 128), jnp.int32)

    for f in range(6):
        ext[f * 128 : f * 128 + 128, :] = hot(places[f : f + 1, :], 0, 128)

    for c in loads[8:]:
        c.start()
    for v in range(5):
        fields[v].wait()
        hi, lo = halves(padded(st[v]))
        uh[v * 128 : v * 128 + 128, :] = hi
        ul[v * 128 : v * 128 + 128, :] = lo
    for f in range(6):
        e = ext[f * 128 : f * 128 + 128, :]
        tr[0:128, f * 256 : f * 256 + 256] = dot(e, uh[...]).astype(BF)
        tr[128:256, f * 256 : f * 256 + 256] = dot(e, ul[...]).astype(BF)

    def remote(src, dst, i, j, device):
        return pltpu.make_async_remote_copy(
            src_ref=src, dst_ref=dst, send_sem=snd_sem.at[i], recv_sem=rcv_sem.at[j],
            device_id=device, device_id_type=MESH,
        )

    pl.semaphore_wait(barrier, 1 + 2 * has_prev.astype(jnp.int32) + 2 * has_next.astype(jnp.int32))
    c_nbr = remote(snd_n, rcv_n, 0, 0, (g, other))
    c_nbr.start()
    def side(t):
        return jnp.where(t == 0, prev, nxt), jnp.where(t == 0, has_prev, has_next)

    c_grp = []
    for t in (far, 1 - far):
        group, there = side(t)
        picked = dot(tr[...], ohs[t])
        snd_g[t] = picked[:128] + picked[128:]
        c = remote(snd_g.at[t], rcv_g.at[1 - t], 1 + t, 2 - t, (group, m))
        pl.when(there)(c.start)
        c_grp.append((there, c))
    picked = dot(tr[...], ohm[...])
    snd_m[...] = picked[:128] + picked[128:]
    c_mem = remote(snd_m, rcv_m, 3, 3, (g, other))
    c_mem.start()

    base_mem = 1536 + other * 128

    def local_faces(f, carry):
        row = fsrc[pl.ds(f, 1), :]
        acc = dot(tr[...], hot(row, 0, 1536))
        at = pl.multiple_of(f * 128, 128)
        nlh[pl.ds(at, 128), :] = acc[:128].astype(BF)
        nll[pl.ds(at, 128), :] = acc[128:].astype(BF)
        ohr[0, f] = hot(row, 1792, 256)
        ohr[1, f] = hot(row, 2048, 256)
        ohrm[f] = hot(row, base_mem, 128)
        return carry

    need(7)
    lax.fori_loop(0, 6, local_faces, 0)

    need(*range(8, 20))
    qs[...] = jnp.zeros((128, 128), F32)
    qs[0:125, 0:125] = q_fine[...]
    qh, ql = halves(qs[...])
    for v in range(5):
        total = dot(qh, uh[v * 128 : v * 128 + 128, :]) + dot(qh, ul[v * 128 : v * 128 + 128, :])
        total = (total + dot(ql, uh[v * 128 : v * 128 + 128, :]))[:125]
        total = total + dg[v] * st[v]
        for w in range(5):
            total = total + var_mix[v : v + 1, w : w + 1] * st[w]
        resl[v * 128 : v * 128 + 128, :] = padded(rh[v] - total)
    rl_h, rl_l = halves(resl[...])
    rest0 = dot(rest[...], rl_h) + dot(rest[...], rl_l)
    rest0 = rest0 + dot(rest_lift[...], nlh[...]) + dot(rest_lift[...], nll[...])
    rest0 = rest0[:40]

    own = owner[...].astype(F32)
    before = lax.broadcasted_iota(jnp.int32, (256, 256), 0) < lax.broadcasted_iota(jnp.int32, (256, 256), 1)
    ones_before = dot(jnp.broadcast_to(own, (16, 256)).astype(BF), jnp.where(before, 1.0, 0.0).astype(BF))[0:1]
    ones_before = ones_before.astype(jnp.int32)
    target = jnp.where(owner[...] == 1, 128 + ones_before, lane_g - ones_before)
    st_hot[...] = hot(target, 0, 256)

    gfa = g_coarse[...]
    gg = exact(gfa, small[0:8, :]) * small[56:104, :]
    gg = exact(small[8:56, 0:48], gg) * small[104:152, :]
    ggh, ggl = halves(gg)
    qrep = jnp.concatenate([q_coarse[...]] * 5, axis=0)
    qq = exact(qrep, small[0:8, 0:40]) * small[104:144, 0:40]

    c_nbr.wait_recv()
    own_nbr = jnp.where(m == 0, nbr[:, 0:128], nbr[:, 128:256])
    got_nbr = rcv_n[0:6, :]
    for o in range(2):
        lists = jnp.where(m == o, own_nbr, got_nbr)
        for f in range(6):
            for d in range(3):
                ohc[o, d, :, f * 128 : f * 128 + 128] = hot(lists[f : f + 1, :], d * 256, 256)

    def take(ref):
        hi, lo = halves(ref[...])
        return jnp.concatenate([hi, lo], axis=0)

    c_mem.wait_recv()
    arr_m[...] = take(rcv_m)
    z = dot(by_face[...], arr_m[...])
    for f in range(6):
        part = dot(stacked(z[f * 48 : f * 48 + 40]), ohrm[f])
        rest0 = rest0 + (part[:40] + part[40:])
    for t in (1 - far, far):
        group, there = side(t)
        pl.when(there)(remote(snd_g.at[t], rcv_g.at[t], 1 + t, 1 + t, (group, m)).wait_recv)
        arr_g[t] = take(rcv_g.at[t])
        z = dot(by_face[...], arr_g[t])
        for f in range(6):
            part = dot(stacked(z[f * 48 : f * 48 + 40]), ohr[t, f])
            rest0 = rest0 + (part[:40] + part[40:])
    cd = cdiag[...]
    first = (0.8 * 0.064) * rest0 / cd
    packed = lax.dot_general(stacked(first), st_hot[...], (((1,), (1,)), ((), ())), preferred_element_type=F32)
    mine[...] = packed[:40] + packed[40:]
    c_two = []
    for t in (far, 1 - far):
        group, there = side(t)
        place = jnp.where(t == 0, 4 + m, m)
        for k in range(2):
            c = remote(mine, blks.at[place], 4 + 2 * t + k, 4 + place, (group, k))
            pl.when(there)(c.start)
            c_two.append((there, c))
    c_own = remote(mine, blks.at[2 + m], 8, 6 + m, (g, other))
    c_own.start()

    for f in range(6):
        acc = dot(arr_g[0], ohr[0, f]) + dot(arr_g[1], ohr[1, f]) + dot(arr_m[...], ohrm[f])
        nlh[f * 128 : f * 128 + 128, :] += acc[:128].astype(BF)
        nll[f * 128 : f * 128 + 128, :] += acc[128:].astype(BF)
    need(20)
    for v in range(5):
        lf = lift[v * 128 : v * 128 + 128, :]
        full = resl[v * 128 : v * 128 + 128, :] + dot(lf, nlh[...]) + dot(lf, nll[...])
        resv[v] = full[:125]
    c_out = pltpu.make_async_copy(resv, resid_out, out_sem.at[0])
    c_out.start()
    inner = exact(qq, first)
    weight = 0.8 / cd
    base = 1.2 * first - weight * inner

    def arrived(place):
        remote(mine, blks.at[place], 8, 4 + place, (g, other)).wait_recv()

    def neighbours(d):
        a, b = stacked(blks[2 * d]), stacked(blks[2 * d + 1])
        return [
            dot(jnp.concatenate([a[:, o * 128 : o * 128 + 128], b[:, o * 128 : o * 128 + 128]], axis=1), ohc[o, d])
            for o in range(2)
        ]

    arrived(2 + other)
    blks[2 + m] = mine[...]
    nears = neighbours(1)
    for t in (1 - far, far):

        @pl.when(side(t)[1])
        def _(t=t):
            arrived(4 * t)
            arrived(4 * t + 1)

        nears = [x + y for x, y in zip(nears, neighbours(2 * t))]
    nhs, nls = [], []
    for o in range(2):
        near = nears[o]
        nhs.append(jnp.concatenate([near[:40, f * 128 : f * 128 + 128] for f in range(6)], axis=0))
        nls.append(jnp.concatenate([near[40:, f * 128 : f * 128 + 128] for f in range(6)], axis=0))
    nh = jnp.concatenate(nhs, axis=1).astype(BF)
    nl = jnp.concatenate(nls, axis=1).astype(BF)
    across = (dot(ggh, nh) + dot(ggh, nl) + dot(ggl, nh))[:40]
    back = dot(stacked(across), st_hot[...])
    mine2[...] = base + weight * (back[:40] + back[40:])
    c_second = pltpu.make_async_copy(mine2, second_out, out_sem.at[1])
    c_second.start()

    for c in (c_nbr, c_mem, c_own):
        c.wait_send()
    for there, c in c_grp + c_two:
        pl.when(there)(c.wait_send)
    c_out.wait()
    c_second.wait()


def last_kernel(resid, second_h, pro2_h, resid_out, corr_out, second, pro2, corr, held, sem):
    loads = [pltpu.make_async_copy(second_h, second, sem.at[0]), pltpu.make_async_copy(pro2_h, pro2, sem.at[1])]
    loads += [pltpu.make_async_copy(resid.at[v], held.at[v], sem.at[2 + v]) for v in range(5)]
    for c in loads:
        c.start()
    copies = []
    loads[0].wait()
    loads[1].wait()
    for v in range(5):
        corr[v] = dot(pro2[...], stacked(second[v * 8 : v * 8 + 8, :]))[:125]
        loads[2 + v].wait()
        c = pltpu.make_async_copy(held.at[v], resid_out.at[v], sem.at[7 + v])
        c.start()
        copies.append(c)
        c = pltpu.make_async_copy(corr.at[v], corr_out.at[v], sem.at[12 + v])
        c.start()
        copies.append(c)
    for c in copies:
        c.wait()


def shards(
    state, rhs, fine_diag, q_fine, var_mix, mem_count, grp_count, send_mem_idx, send_grp_idx,
    face_src, coarse_diag, q_coarse, g_coarse, owner, coarse_nbr,
):
    places, lift, rest, rest_lift, by_face, pro2, small = tables()
    n_grp = lax.axis_size("grp")
    hbm = pl.BlockSpec(memory_space=pltpu.HBM)
    field = jax.ShapeDtypeStruct((5, 125, 256), F32)
    operands = (
        state, send_mem_idx, send_grp_idx, mem_count, grp_count, jnp.asarray(places), coarse_nbr, face_src, rhs, fine_diag,
        q_fine, var_mix, jnp.asarray(rest), jnp.asarray(rest_lift), owner.reshape(1, 256), coarse_diag.reshape(40, 256),
        g_coarse.reshape(48, 8), q_coarse, jnp.asarray(small), jnp.asarray(by_face), jnp.asarray(lift),
    )
    resid, second = pl.pallas_call(
        functools.partial(main_kernel, n_grp),
        out_shape=(field, jax.ShapeDtypeStruct((40, 256), F32)),
        in_specs=[hbm] * 21,
        out_specs=(hbm, hbm),
        scratch_shapes=[pltpu.VMEM(a.shape, a.dtype) for a in operands]
        + [
            pltpu.VMEM((640, 256), BF),
            pltpu.VMEM((640, 256), BF),
            pltpu.VMEM((128, 128), F32),
            pltpu.VMEM((2, 1536, 256), BF),
            pltpu.VMEM((1536, 128), BF),
            pltpu.VMEM((256, 1536), BF),
            pltpu.VMEM((2, 128, 256), F32),
            pltpu.VMEM((128, 128), F32),
            pltpu.VMEM((8, 128), jnp.int32),
            pltpu.VMEM((2, 128, 256), F32),
            pltpu.VMEM((128, 128), F32),
            pltpu.VMEM((8, 128), jnp.int32),
            pltpu.VMEM((2, 6, 256, 256), BF),
            pltpu.VMEM((6, 128, 256), BF),
            pltpu.VMEM((768, 256), BF),
            pltpu.VMEM((768, 256), BF),
            pltpu.VMEM((640, 256), F32),
            pltpu.VMEM((2, 3, 256, 768), BF),
            pltpu.VMEM((256, 256), BF),
            pltpu.VMEM((6, 40, 256), F32),
            pltpu.VMEM((40, 256), F32),
            pltpu.VMEM((5, 125, 256), F32),
            pltpu.VMEM((40, 256), F32),
            pltpu.VMEM((768, 640), BF),
            pltpu.VMEM((2, 256, 256), BF),
            pltpu.VMEM((256, 128), BF),
            pltpu.SemaphoreType.DMA((21,)),
            pltpu.SemaphoreType.DMA((5,)),
            pltpu.SemaphoreType.DMA((9,)),
            pltpu.SemaphoreType.DMA((10,)),
            pltpu.SemaphoreType.DMA((2,)),
        ],
        compiler_params=pltpu.CompilerParams(
            collective_id=0, has_side_effects=True, vmem_limit_bytes=60 * 1024 * 1024
        ),
        name="residual_and_sweeps",
    )(*operands)
    return pl.pallas_call(
        last_kernel,
        out_shape=(field, field),
        in_specs=[hbm, hbm, hbm],
        out_specs=(hbm, hbm),
        scratch_shapes=[
            pltpu.VMEM((40, 256), F32),
            pltpu.VMEM((128, 16), BF),
            pltpu.VMEM((5, 125, 256), F32),
            pltpu.VMEM((5, 125, 256), F32),
            pltpu.SemaphoreType.DMA((17,)),
        ],
        compiler_params=pltpu.CompilerParams(vmem_limit_bytes=60 * 1024 * 1024),
        name="prolongation",
    )(resid, second, jnp.asarray(pro2))


def solution(mesh):
    whole = ("grp", "mem")
    return jax.shard_map(
        shards,
        mesh=mesh,
        in_specs=(
            P(None, None, whole), P(None, None, whole), P(None, None, whole), P(), P(),
            P(whole, None), P(whole, None), P(whole, None, None), P(whole, None, None), P(None, whole),
            P(None, None, whole), P(), P(), P(whole, None), P(None, whole),
        ),
        out_specs=(P(None, None, whole), P(None, None, whole)),
        check_vma=False,
    )
```

```python
import functools

import jax
import jax.numpy as jnp
import ml_dtypes
import numpy as np
from jax import lax
from jax.experimental import pallas as pl
from jax.experimental.pallas import tpu as pltpu
from jax.sharding import PartitionSpec as P

MESH = pl.DeviceIdType.MESH
HIGH = lax.Precision.HIGHEST
BF = jnp.bfloat16
F32 = jnp.float32


def tables():
    points = np.arange(125)
    coords = [points // 25, points // 5 % 5, points % 5]
    extract = np.zeros((6, 25, 125), np.float32)
    for face in range(6):
        along = face // 2
        others = [c for b, c in enumerate(coords) if b != along]
        index = others[0] * 5 + others[1]
        on_face = coords[along] == 4 * (face % 2)
        extract[face] = (index[None, :] == np.arange(25)[:, None]) & on_face[None, :]
    nodes = -1.0 + 0.5 * np.arange(5)
    basis = np.stack([(1.0 - nodes) / 2.0, (1.0 + nodes) / 2.0], axis=1)
    prolong = np.einsum("ia,jb,kc->ijkabc", basis, basis, basis).reshape(125, 8)
    ext = np.zeros((6, 128, 5, 128), np.float32)
    for v in range(5):
        ext[:, v * 25 : v * 25 + 25, v, :125] = extract
    ext = ext.reshape(768, 640)
    places = np.full((8, 640), -1, np.int32)
    for face in range(6):
        block = ext[face * 128 : face * 128 + 128]
        places[face] = np.where(block.any(axis=0), block.argmax(axis=0), -1)
    lift = np.ascontiguousarray(ext.T)
    rest = np.zeros((48, 5, 128), np.float32)
    for v in range(5):
        rest[v * 8 : v * 8 + 8, v, :125] = prolong.T
    rest = rest.reshape(48, 640)
    rest_lift = rest @ lift
    by_face = rest_lift.reshape(48, 6, 128).transpose(1, 0, 2).reshape(288, 128)
    by_face = np.concatenate([by_face, by_face], axis=1)
    pro2 = np.concatenate([rest[:8, :128].T, rest[:8, :128].T], axis=1)
    spread = np.zeros((8, 6, 5, 8), np.float32)
    for b in range(8):
        spread[b, :, :, b] = 1.0
    spread = spread.reshape(8, 240)
    gather_a = np.zeros((48, 48), np.float32)
    for v in range(5):
        for f in range(6):
            for a in range(8):
                gather_a[v * 8 + a, f * 8 + a] = 1.0
    same_f = np.zeros((6, 8, 6, 40), np.float32)
    for f in range(6):
        same_f[f, :, f, :] = 1.0
    same_f = same_f.reshape(48, 240)
    same_v = np.zeros((6, 8, 6, 5, 8), np.float32)
    for v in range(5):
        same_v[v, :, :, v, :] = 1.0
    same_v = same_v.reshape(48, 240)
    small = np.zeros((152, 240), np.float32)
    small[0:8] = spread
    small[8:56, :48] = gather_a
    small[56:104] = same_f
    small[104:152] = same_v
    cast = lambda a: np.asarray(a, ml_dtypes.bfloat16)
    return places, cast(lift), cast(rest), cast(rest_lift), cast(by_face), cast(pro2), small


def halves(x):
    hi = x.astype(BF)
    return hi, (x - hi.astype(F32)).astype(BF)


def stacked(x):
    hi = x.astype(BF).astype(F32)
    return jnp.concatenate([hi, x - hi], axis=0).astype(BF)


def dot(a, b):
    return jnp.dot(a, b, preferred_element_type=F32)


def exact(a, b):
    return jnp.dot(a, b, precision=HIGH, preferred_element_type=F32)


def hot(row, base, size):
    row = (row - base).astype(jnp.int16)
    places = lax.broadcasted_iota(jnp.int16, (size, row.shape[1]), 0)
    return jnp.where(places == row, jnp.ones((), BF), jnp.zeros((), BF))


def padded(x):
    return jnp.concatenate([x, jnp.zeros((3, x.shape[1]), F32)], axis=0)


def main_kernel(n_grp, *refs):
    sources, (resid_out, second_out), scratch = refs[:21], refs[21:23], refs[23:]
    (
        st, midx, gidx, mcount, gcount, places, cnbr, fsrc, rh, dg, q_fine, var_mix,
        rest, rest_lift, owner, cdiag, g_coarse, q_coarse, small, by_face, lift,
    ) = scratch[:21]
    (
        uh, ul, qs,
        ohs, ohm, tr, snd_g, snd_m, snd_n, rcv_g, rcv_m, rcv_n,
        ohr, ohrm, nlh, nll, resl, ohc, st_hot, blks, mine, resv, mine2, ext01, ext23, ext4, arr_g, arr_m,
        in_sem, st_sem, snd_sem, rcv_sem, out_sem,
    ) = scratch[21:]
    g = lax.axis_index("grp")
    m = lax.axis_index("mem")
    other = 1 - m
    has_prev, has_next = g > 0, g < n_grp - 1
    far = jnp.where(lax.rem(g, 4) == 3, 1, 0)
    prev, nxt = jnp.maximum(g - 1, 0), jnp.minimum(g + 1, n_grp - 1)

    def side(t):
        return jnp.where(t == 0, prev, nxt), jnp.where(t == 0, has_prev, has_next)

    barrier = pltpu.get_barrier_semaphore()
    def greet(device):
        pl.semaphore_signal(barrier, inc=1, device_id=device, device_id_type=MESH)

    for t in (far, 1 - far):

        @pl.when(side(t)[1])
        def _(t=t):
            greet((side(t)[0], 0))
            greet((side(t)[0], 1))

    greet((g, other))

    loads = [None] + [pltpu.make_async_copy(sources[i], scratch[i], in_sem.at[i]) for i in range(1, 21)]
    fields = [pltpu.make_async_copy(sources[0].at[v], st.at[v], st_sem.at[v]) for v in range(5)]
    for c in loads[1:7] + fields + loads[7:8]:
        c.start()
    seen = set()

    def need(*which):
        for i in which:
            if i not in seen:
                seen.add(i)
                loads[i].wait()

    @pl.when(jnp.logical_not(has_prev))
    def _():
        rcv_g[0] = jnp.zeros((128, 256), F32)
        blks[0] = jnp.zeros((40, 256), F32)
        blks[1] = jnp.zeros((40, 256), F32)

    @pl.when(jnp.logical_not(has_next))
    def _():
        rcv_g[1] = jnp.zeros((128, 256), F32)
        blks[4] = jnp.zeros((40, 256), F32)
        blks[5] = jnp.zeros((40, 256), F32)

    need(1, 2, 3, 4, 5, 6)
    lane_g = lax.broadcasted_iota(jnp.int32, (1, 256), 1)
    lane_m = lax.broadcasted_iota(jnp.int32, (1, 128), 1)
    for t in range(2):
        row = jnp.where(lane_g < gcount[0:1, t : t + 1], gidx[0, t : t + 1, :], -1)
        ohs[t] = hot(row, 0, 1536)
    mrow = jnp.where(m == 0, midx[0, 1:2, :], midx[0, 0:1, :])
    mlim = jnp.where(m == 0, mcount[0:1, 1:2], mcount[0:1, 0:1])
    ohm[...] = hot(jnp.where(lane_m < mlim, mrow, -1), 0, 1536)
    nbr = cnbr[...]
    snd_n[0:6, :] = jnp.where(m == 0, nbr[:, 128:256], nbr[:, 0:128])
    snd_n[6:8, :] = jnp.zeros((2, 128), jnp.int32)

    for f in range(6):
        ext01[f * 64 : f * 64 + 64, :] = hot(places[f : f + 1, 0:256], 0, 64)
        ext23[f * 64 : f * 64 + 64, :] = hot(places[f : f + 1, 256:512], 48, 64)
        ext4[f * 32 : f * 32 + 32, :] = hot(places[f : f + 1, 512:640], 96, 32)

    for c in loads[8:]:
        c.start()
    for v in range(5):
        fields[v].wait()
        hi, lo = halves(padded(st[v]))
        uh[v * 128 : v * 128 + 128, :] = hi
        ul[v * 128 : v * 128 + 128, :] = lo
    for u, top in ((uh, 0), (ul, 128)):
        x, y, z = dot(ext01[...], u[0:256, :]), dot(ext23[...], u[256:512, :]), dot(ext4[...], u[512:640, :])
        for f in range(6):
            xf, yf, zf = x[f * 64 : f * 64 + 64], y[f * 64 : f * 64 + 64], z[f * 32 : f * 32 + 32]
            rows = [xf[:48], xf[48:] + yf[:16], yf[16:48], yf[48:] + zf[:16], zf[16:]]
            tr[top : top + 128, f * 256 : f * 256 + 256] = jnp.concatenate(rows, axis=0).astype(BF)

    def remote(src, dst, i, j, device):
        return pltpu.make_async_remote_copy(
            src_ref=src, dst_ref=dst, send_sem=snd_sem.at[i], recv_sem=rcv_sem.at[j],
            device_id=device, device_id_type=MESH,
        )

    pl.semaphore_wait(barrier, 1 + 2 * has_prev.astype(jnp.int32) + 2 * has_next.astype(jnp.int32))
    c_nbr = remote(snd_n, rcv_n, 0, 0, (g, other))
    c_nbr.start()
    c_grp = []
    for t in (far, 1 - far):
        group, there = side(t)
        picked = dot(tr[...], ohs[t])
        snd_g[t] = picked[:128] + picked[128:]
        c = remote(snd_g.at[t], rcv_g.at[1 - t], 1 + t, 2 - t, (group, m))
        pl.when(there)(c.start)
        c_grp.append((there, c))
    picked = dot(tr[...], ohm[...])
    snd_m[...] = picked[:128] + picked[128:]
    c_mem = remote(snd_m, rcv_m, 3, 3, (g, other))
    c_mem.start()

    base_mem = 1536 + other * 128

    def local_faces(f, carry):
        row = fsrc[pl.ds(f, 1), :]
        acc = dot(tr[...], hot(row, 0, 1536))
        at = pl.multiple_of(f * 128, 128)
        nlh[pl.ds(at, 128), :] = acc[:128].astype(BF)
        nll[pl.ds(at, 128), :] = acc[128:].astype(BF)
        ohr[0, f] = hot(row, 1792, 256)
        ohr[1, f] = hot(row, 2048, 256)
        ohrm[f] = hot(row, base_mem, 128)
        return carry

    need(7)
    lax.fori_loop(0, 6, local_faces, 0)

    need(*range(8, 20))
    qs[...] = jnp.zeros((128, 128), F32)
    qs[0:125, 0:125] = q_fine[...]
    qh, ql = halves(qs[...])
    for v in range(5):
        total = dot(qh, uh[v * 128 : v * 128 + 128, :]) + dot(qh, ul[v * 128 : v * 128 + 128, :])
        total = (total + dot(ql, uh[v * 128 : v * 128 + 128, :]))[:125]
        total = total + dg[v] * st[v]
        for w in range(5):
            total = total + var_mix[v : v + 1, w : w + 1] * st[w]
        resl[v * 128 : v * 128 + 128, :] = padded(rh[v] - total)
    rl_h, rl_l = halves(resl[...])
    rest0 = dot(rest[...], rl_h) + dot(rest[...], rl_l)
    rest0 = rest0 + dot(rest_lift[...], nlh[...]) + dot(rest_lift[...], nll[...])
    rest0 = rest0[:40]

    own = owner[...].astype(F32)
    before = lax.broadcasted_iota(jnp.int32, (256, 256), 0) < lax.broadcasted_iota(jnp.int32, (256, 256), 1)
    ones_before = dot(jnp.broadcast_to(own, (16, 256)).astype(BF), jnp.where(before, 1.0, 0.0).astype(BF))[0:1]
    ones_before = ones_before.astype(jnp.int32)
    target = jnp.where(owner[...] == 1, 128 + ones_before, lane_g - ones_before)
    st_hot[...] = hot(target, 0, 256)

    gfa = g_coarse[...]
    gg = exact(gfa, small[0:8, :]) * small[56:104, :]
    gg = exact(small[8:56, 0:48], gg) * small[104:152, :]
    ggh, ggl = halves(gg)
    qrep = jnp.concatenate([q_coarse[...]] * 5, axis=0)
    qq = exact(qrep, small[0:8, 0:40]) * small[104:144, 0:40]

    c_nbr.wait_recv()
    own_nbr = jnp.where(m == 0, nbr[:, 0:128], nbr[:, 128:256])
    got_nbr = rcv_n[0:6, :]
    for o in range(2):
        lists = jnp.where(m == o, own_nbr, got_nbr)
        for f in range(6):
            for d in range(3):
                ohc[o, d, :, f * 128 : f * 128 + 128] = hot(lists[f : f + 1, :], d * 256, 256)

    def take(ref):
        hi, lo = halves(ref[...])
        return jnp.concatenate([hi, lo], axis=0)

    c_mem.wait_recv()
    arr_m[...] = take(rcv_m)
    z = dot(by_face[...], arr_m[...])
    for f in range(6):
        part = dot(stacked(z[f * 48 : f * 48 + 40]), ohrm[f])
        rest0 = rest0 + (part[:40] + part[40:])
    for t in (1 - far, far):
        group, there = side(t)
        pl.when(there)(remote(snd_g.at[t], rcv_g.at[t], 1 + t, 1 + t, (group, m)).wait_recv)
        arr_g[t] = take(rcv_g.at[t])
        z = dot(by_face[...], arr_g[t])
        for f in range(6):
            part = dot(stacked(z[f * 48 : f * 48 + 40]), ohr[t, f])
            rest0 = rest0 + (part[:40] + part[40:])
    cd = cdiag[...]
    first = (0.8 * 0.064) * rest0 / cd
    packed = lax.dot_general(stacked(first), st_hot[...], (((1,), (1,)), ((), ())), preferred_element_type=F32)
    mine[...] = packed[:40] + packed[40:]
    c_two = []
    for t in (far, 1 - far):
        group, there = side(t)
        place = jnp.where(t == 0, 4 + m, m)
        for k in range(2):
            c = remote(mine, blks.at[place], 4 + 2 * t + k, 4 + place, (group, k))
            pl.when(there)(c.start)
            c_two.append((there, c))
    c_own = remote(mine, blks.at[2 + m], 8, 6 + m, (g, other))
    c_own.start()

    for f in range(6):
        acc = dot(arr_g[0], ohr[0, f]) + dot(arr_g[1], ohr[1, f]) + dot(arr_m[...], ohrm[f])
        nlh[f * 128 : f * 128 + 128, :] += acc[:128].astype(BF)
        nll[f * 128 : f * 128 + 128, :] += acc[128:].astype(BF)
    need(20)
    for v in range(5):
        lf = lift[v * 128 : v * 128 + 128, :]
        full = resl[v * 128 : v * 128 + 128, :] + dot(lf, nlh[...]) + dot(lf, nll[...])
        resv[v] = full[:125]
    c_out = pltpu.make_async_copy(resv, resid_out, out_sem.at[0])
    c_out.start()
    inner = exact(qq, first)
    weight = 0.8 / cd
    base = 1.2 * first - weight * inner

    def arrived(place):
        remote(mine, blks.at[place], 8, 4 + place, (g, other)).wait_recv()

    def neighbours(d):
        a, b = stacked(blks[2 * d]), stacked(blks[2 * d + 1])
        return [
            dot(jnp.concatenate([a[:, o * 128 : o * 128 + 128], b[:, o * 128 : o * 128 + 128]], axis=1), ohc[o, d])
            for o in range(2)
        ]

    arrived(2 + other)
    blks[2 + m] = mine[...]
    nears = neighbours(1)
    for t in (1 - far, far):

        @pl.when(side(t)[1])
        def _(t=t):
            arrived(4 * t)
            arrived(4 * t + 1)

        nears = [x + y for x, y in zip(nears, neighbours(2 * t))]
    nhs, nls = [], []
    for o in range(2):
        near = nears[o]
        nhs.append(jnp.concatenate([near[:40, f * 128 : f * 128 + 128] for f in range(6)], axis=0))
        nls.append(jnp.concatenate([near[40:, f * 128 : f * 128 + 128] for f in range(6)], axis=0))
    nh = jnp.concatenate(nhs, axis=1).astype(BF)
    nl = jnp.concatenate(nls, axis=1).astype(BF)
    across = (dot(ggh, nh) + dot(ggh, nl) + dot(ggl, nh))[:40]
    back = dot(stacked(across), st_hot[...])
    mine2[...] = base + weight * (back[:40] + back[40:])
    c_second = pltpu.make_async_copy(mine2, second_out, out_sem.at[1])
    c_second.start()

    for c in (c_nbr, c_mem, c_own):
        c.wait_send()
    for there, c in c_grp + c_two:
        pl.when(there)(c.wait_send)
    c_out.wait()
    c_second.wait()


def last_kernel(resid, second_h, pro2_h, resid_out, corr_out, second, pro2, corr, held, sem):
    loads = [pltpu.make_async_copy(second_h, second, sem.at[0]), pltpu.make_async_copy(pro2_h, pro2, sem.at[1])]
    whole = pltpu.make_async_copy(resid, held, sem.at[2])
    for c in loads:
        c.start()
    whole.start()
    for c in loads:
        c.wait()
    copies = []
    for v in range(5):
        corr[v] = dot(pro2[...], stacked(second[v * 8 : v * 8 + 8, :]))[:125]
        c = pltpu.make_async_copy(corr.at[v], corr_out.at[v], sem.at[4 + v])
        c.start()
        copies.append(c)
    whole.wait()
    c = pltpu.make_async_copy(held, resid_out, sem.at[3])
    c.start()
    copies.append(c)
    for c in copies:
        c.wait()


def shards(
    state, rhs, fine_diag, q_fine, var_mix, mem_count, grp_count, send_mem_idx, send_grp_idx,
    face_src, coarse_diag, q_coarse, g_coarse, owner, coarse_nbr,
):
    places, lift, rest, rest_lift, by_face, pro2, small = tables()
    n_grp = lax.axis_size("grp")
    hbm = pl.BlockSpec(memory_space=pltpu.HBM)
    field = jax.ShapeDtypeStruct((5, 125, 256), F32)
    operands = (
        state, send_mem_idx, send_grp_idx, mem_count, grp_count, jnp.asarray(places), coarse_nbr, face_src, rhs, fine_diag,
        q_fine, var_mix, jnp.asarray(rest), jnp.asarray(rest_lift), owner.reshape(1, 256), coarse_diag.reshape(40, 256),
        g_coarse.reshape(48, 8), q_coarse, jnp.asarray(small), jnp.asarray(by_face), jnp.asarray(lift),
    )
    resid, second = pl.pallas_call(
        functools.partial(main_kernel, n_grp),
        out_shape=(field, jax.ShapeDtypeStruct((40, 256), F32)),
        in_specs=[hbm] * 21,
        out_specs=(hbm, hbm),
        scratch_shapes=[pltpu.VMEM(a.shape, a.dtype) for a in operands]
        + [
            pltpu.VMEM((640, 256), BF),
            pltpu.VMEM((640, 256), BF),
            pltpu.VMEM((128, 128), F32),
            pltpu.VMEM((2, 1536, 256), BF),
            pltpu.VMEM((1536, 128), BF),
            pltpu.VMEM((256, 1536), BF),
            pltpu.VMEM((2, 128, 256), F32),
            pltpu.VMEM((128, 128), F32),
            pltpu.VMEM((8, 128), jnp.int32),
            pltpu.VMEM((2, 128, 256), F32),
            pltpu.VMEM((128, 128), F32),
            pltpu.VMEM((8, 128), jnp.int32),
            pltpu.VMEM((2, 6, 256, 256), BF),
            pltpu.VMEM((6, 128, 256), BF),
            pltpu.VMEM((768, 256), BF),
            pltpu.VMEM((768, 256), BF),
            pltpu.VMEM((640, 256), F32),
            pltpu.VMEM((2, 3, 256, 768), BF),
            pltpu.VMEM((256, 256), BF),
            pltpu.VMEM((6, 40, 256), F32),
            pltpu.VMEM((40, 256), F32),
            pltpu.VMEM((5, 125, 256), F32),
            pltpu.VMEM((40, 256), F32),
            pltpu.VMEM((384, 256), BF),
            pltpu.VMEM((384, 256), BF),
            pltpu.VMEM((192, 128), BF),
            pltpu.VMEM((2, 256, 256), BF),
            pltpu.VMEM((256, 128), BF),
            pltpu.SemaphoreType.DMA((21,)),
            pltpu.SemaphoreType.DMA((5,)),
            pltpu.SemaphoreType.DMA((9,)),
            pltpu.SemaphoreType.DMA((10,)),
            pltpu.SemaphoreType.DMA((2,)),
        ],
        compiler_params=pltpu.CompilerParams(
            collective_id=0, has_side_effects=True, vmem_limit_bytes=60 * 1024 * 1024
        ),
        name="residual_and_sweeps",
    )(*operands)
    return pl.pallas_call(
        last_kernel,
        out_shape=(field, field),
        in_specs=[hbm, hbm, hbm],
        out_specs=(hbm, hbm),
        scratch_shapes=[
            pltpu.VMEM((40, 256), F32),
            pltpu.VMEM((128, 16), BF),
            pltpu.VMEM((5, 125, 256), F32),
            pltpu.VMEM((5, 125, 256), F32),
            pltpu.SemaphoreType.DMA((9,)),
        ],
        compiler_params=pltpu.CompilerParams(vmem_limit_bytes=60 * 1024 * 1024),
        name="prolongation",
    )(resid, second, jnp.asarray(pro2))


def solution(mesh):
    whole = ("grp", "mem")
    return jax.shard_map(
        shards,
        mesh=mesh,
        in_specs=(
            P(None, None, whole), P(None, None, whole), P(None, None, whole), P(), P(),
            P(whole, None), P(whole, None), P(whole, None, None), P(whole, None, None), P(None, whole),
            P(None, None, whole), P(), P(), P(whole, None), P(None, whole),
        ),
        out_specs=(P(None, None, whole), P(None, None, whole)),
        check_vma=False,
    )
```

```python
import functools

import jax
import jax.numpy as jnp
import ml_dtypes
import numpy as np
from jax import lax
from jax.experimental import pallas as pl
from jax.experimental.pallas import tpu as pltpu
from jax.sharding import PartitionSpec as P

MESH = pl.DeviceIdType.MESH
HIGH = lax.Precision.HIGHEST
BF = jnp.bfloat16
F32 = jnp.float32


def tables():
    points = np.arange(125)
    coords = [points // 25, points // 5 % 5, points % 5]
    extract = np.zeros((6, 25, 125), np.float32)
    for face in range(6):
        along = face // 2
        others = [c for b, c in enumerate(coords) if b != along]
        index = others[0] * 5 + others[1]
        on_face = coords[along] == 4 * (face % 2)
        extract[face] = (index[None, :] == np.arange(25)[:, None]) & on_face[None, :]
    nodes = -1.0 + 0.5 * np.arange(5)
    basis = np.stack([(1.0 - nodes) / 2.0, (1.0 + nodes) / 2.0], axis=1)
    prolong = np.einsum("ia,jb,kc->ijkabc", basis, basis, basis).reshape(125, 8)
    ext = np.zeros((6, 128, 5, 128), np.float32)
    for v in range(5):
        ext[:, v * 25 : v * 25 + 25, v, :125] = extract
    ext = ext.reshape(768, 640)
    places = np.full((8, 640), -1, np.int32)
    for face in range(6):
        block = ext[face * 128 : face * 128 + 128]
        places[face] = np.where(block.any(axis=0), block.argmax(axis=0), -1)
    lift = np.ascontiguousarray(ext.T)
    rest = np.zeros((48, 5, 128), np.float32)
    for v in range(5):
        rest[v * 8 : v * 8 + 8, v, :125] = prolong.T
    rest = rest.reshape(48, 640)
    rest_lift = rest @ lift
    by_face = rest_lift.reshape(48, 6, 128).transpose(1, 0, 2).reshape(288, 128)
    by_face = np.concatenate([by_face, by_face], axis=1)
    pro2 = np.concatenate([rest[:8, :128].T, rest[:8, :128].T], axis=1)
    spread = np.zeros((8, 6, 5, 8), np.float32)
    for b in range(8):
        spread[b, :, :, b] = 1.0
    spread = spread.reshape(8, 240)
    gather_a = np.zeros((48, 48), np.float32)
    for v in range(5):
        for f in range(6):
            for a in range(8):
                gather_a[v * 8 + a, f * 8 + a] = 1.0
    same_f = np.zeros((6, 8, 6, 40), np.float32)
    for f in range(6):
        same_f[f, :, f, :] = 1.0
    same_f = same_f.reshape(48, 240)
    same_v = np.zeros((6, 8, 6, 5, 8), np.float32)
    for v in range(5):
        same_v[v, :, :, v, :] = 1.0
    same_v = same_v.reshape(48, 240)
    small = np.zeros((152, 240), np.float32)
    small[0:8] = spread
    small[8:56, :48] = gather_a
    small[56:104] = same_f
    small[104:152] = same_v
    cast = lambda a: np.asarray(a, ml_dtypes.bfloat16)
    return places, cast(lift), cast(rest), cast(rest_lift), cast(by_face), cast(pro2), small


def halves(x):
    hi = x.astype(BF)
    return hi, (x - hi.astype(F32)).astype(BF)


def stacked(x):
    hi = x.astype(BF).astype(F32)
    return jnp.concatenate([hi, x - hi], axis=0).astype(BF)


def dot(a, b):
    return jnp.dot(a, b, preferred_element_type=F32)


def exact(a, b):
    return jnp.dot(a, b, precision=HIGH, preferred_element_type=F32)


def hot(row, base, size):
    row = (row - base).astype(jnp.int16)
    places = lax.broadcasted_iota(jnp.int16, (size, row.shape[1]), 0)
    return jnp.where(places == row, jnp.ones((), BF), jnp.zeros((), BF))


def padded(x):
    return jnp.concatenate([x, jnp.zeros((3, x.shape[1]), F32)], axis=0)


def main_kernel(n_grp, *refs):
    sources, (resid_out, second_out), scratch = refs[:21], refs[21:23], refs[23:]
    (
        st, midx, gidx, mcount, gcount, places, cnbr, fsrc, rh, dg, q_fine, var_mix,
        rest, rest_lift, owner, cdiag, g_coarse, q_coarse, small, by_face, lift,
    ) = scratch[:21]
    (
        uh, ul, qs,
        ohs, ohm, tr, snd_g, snd_m, snd_n, rcv_g, rcv_m, rcv_n,
        ohr, ohrm, nlh, nll, resl, ohc, st_hot, s_hot, first_weight, blks, mine, resv, mine2, ext01, ext23, ext4, arr_g, arr_m,
        in_sem, st_sem, snd_sem, rcv_sem, out_sem,
    ) = scratch[21:]
    g = lax.axis_index("grp")
    m = lax.axis_index("mem")
    other = 1 - m
    has_prev, has_next = g > 0, g < n_grp - 1
    far = jnp.where(lax.rem(g, 4) == 3, 1, 0)
    prev, nxt = jnp.maximum(g - 1, 0), jnp.minimum(g + 1, n_grp - 1)

    def side(t):
        return jnp.where(t == 0, prev, nxt), jnp.where(t == 0, has_prev, has_next)

    barrier = pltpu.get_barrier_semaphore()
    def greet(device):
        pl.semaphore_signal(barrier, inc=1, device_id=device, device_id_type=MESH)

    for t in (far, 1 - far):

        @pl.when(side(t)[1])
        def _(t=t):
            greet((side(t)[0], 0))
            greet((side(t)[0], 1))

    greet((g, other))

    loads = [None] + [pltpu.make_async_copy(sources[i], scratch[i], in_sem.at[i]) for i in range(1, 21)]
    fields = [pltpu.make_async_copy(sources[0].at[v], st.at[v], st_sem.at[v]) for v in range(5)]
    for c in loads[1:7] + fields + loads[7:8]:
        c.start()
    seen = set()

    def need(*which):
        for i in which:
            if i not in seen:
                seen.add(i)
                loads[i].wait()

    @pl.when(jnp.logical_not(has_prev))
    def _():
        rcv_g[0] = jnp.zeros((2, 128, 128), F32)
        blks[0] = jnp.zeros((40, 256), F32)
        blks[1] = jnp.zeros((40, 256), F32)

    @pl.when(jnp.logical_not(has_next))
    def _():
        rcv_g[1] = jnp.zeros((2, 128, 128), F32)
        blks[4] = jnp.zeros((40, 256), F32)
        blks[5] = jnp.zeros((40, 256), F32)

    need(1, 2, 3, 4, 5, 6)
    lane_g = lax.broadcasted_iota(jnp.int32, (1, 256), 1)
    lane_m = lax.broadcasted_iota(jnp.int32, (1, 128), 1)
    for t in range(2):
        row = jnp.where(lane_g < gcount[0:1, t : t + 1], gidx[0, t : t + 1, :], -1)
        ohs[t] = hot(row, 0, 1536)
    mrow = jnp.where(m == 0, midx[0, 1:2, :], midx[0, 0:1, :])
    mlim = jnp.where(m == 0, mcount[0:1, 1:2], mcount[0:1, 0:1])
    ohm[...] = hot(jnp.where(lane_m < mlim, mrow, -1), 0, 1536)
    nbr = cnbr[...]
    snd_n[0:6, :] = jnp.where(m == 0, nbr[:, 128:256], nbr[:, 0:128])
    snd_n[6:8, :] = jnp.zeros((2, 128), jnp.int32)

    for f in range(6):
        ext01[f * 64 : f * 64 + 64, :] = hot(places[f : f + 1, 0:256], 0, 64)
        ext23[f * 64 : f * 64 + 64, :] = hot(places[f : f + 1, 256:512], 48, 64)
        ext4[f * 32 : f * 32 + 32, :] = hot(places[f : f + 1, 512:640], 96, 32)

    for c in loads[8:]:
        c.start()
    for v in range(5):
        fields[v].wait()
        hi, lo = halves(padded(st[v]))
        uh[v * 128 : v * 128 + 128, :] = hi
        ul[v * 128 : v * 128 + 128, :] = lo
    for u, top in ((uh, 0), (ul, 128)):
        x, y, z = dot(ext01[...], u[0:256, :]), dot(ext23[...], u[256:512, :]), dot(ext4[...], u[512:640, :])
        for f in range(6):
            xf, yf, zf = x[f * 64 : f * 64 + 64], y[f * 64 : f * 64 + 64], z[f * 32 : f * 32 + 32]
            rows = [xf[:48], xf[48:] + yf[:16], yf[16:48], yf[48:] + zf[:16], zf[16:]]
            tr[top : top + 128, f * 256 : f * 256 + 256] = jnp.concatenate(rows, axis=0).astype(BF)

    def remote(src, dst, i, j, device):
        return pltpu.make_async_remote_copy(
            src_ref=src, dst_ref=dst, send_sem=snd_sem.at[i], recv_sem=rcv_sem.at[j],
            device_id=device, device_id_type=MESH,
        )

    pl.semaphore_wait(barrier, 1 + 2 * has_prev.astype(jnp.int32) + 2 * has_next.astype(jnp.int32))
    c_nbr = remote(snd_n, rcv_n, 0, 0, (g, other))
    c_nbr.start()
    c_grp = []
    for t in (far, 1 - far):
        group, there = side(t)
        picked = dot(tr[...], ohs[t])
        whole = picked[:128] + picked[128:]
        for h in range(2):
            snd_g[t, h] = whole[:, h * 128 : h * 128 + 128]
            c = remote(snd_g.at[t, h], rcv_g.at[1 - t, h], (1, 9)[h] + t, (2, 11)[h] - t, (group, m))
            pl.when(there)(c.start)
            c_grp.append((there, c))
    picked = dot(tr[...], ohm[...])
    snd_m[...] = picked[:128] + picked[128:]
    c_mem = remote(snd_m, rcv_m, 3, 3, (g, other))
    c_mem.start()

    base_mem = 1536 + other * 128

    def local_faces(f, carry):
        row = fsrc[pl.ds(f, 1), :]
        acc = dot(tr[...], hot(row, 0, 1536))
        at = pl.multiple_of(f * 128, 128)
        nlh[pl.ds(at, 128), :] = acc[:128].astype(BF)
        nll[pl.ds(at, 128), :] = acc[128:].astype(BF)
        ohr[0, f] = hot(row, 1792, 256)
        ohr[1, f] = hot(row, 2048, 256)
        ohrm[f] = hot(row, base_mem, 128)
        return carry

    need(7)
    lax.fori_loop(0, 6, local_faces, 0)

    need(*range(8, 20))
    qs[...] = jnp.zeros((128, 128), F32)
    qs[0:125, 0:125] = q_fine[...]
    qh, ql = halves(qs[...])
    for v in range(5):
        total = dot(qh, uh[v * 128 : v * 128 + 128, :]) + dot(qh, ul[v * 128 : v * 128 + 128, :])
        total = (total + dot(ql, uh[v * 128 : v * 128 + 128, :]))[:125]
        total = total + dg[v] * st[v]
        for w in range(5):
            total = total + var_mix[v : v + 1, w : w + 1] * st[w]
        resl[v * 128 : v * 128 + 128, :] = padded(rh[v] - total)
    rl_h, rl_l = halves(resl[...])
    rest0 = dot(rest[...], rl_h) + dot(rest[...], rl_l)
    rest0 = rest0 + dot(rest_lift[...], nlh[...]) + dot(rest_lift[...], nll[...])
    rest0 = rest0[:40]

    own = owner[...].astype(F32)
    before = lax.broadcasted_iota(jnp.int32, (256, 256), 0) < lax.broadcasted_iota(jnp.int32, (256, 256), 1)
    ones_before = dot(jnp.broadcast_to(own, (16, 256)).astype(BF), jnp.where(before, 1.0, 0.0).astype(BF))[0:1]
    ones_before = ones_before.astype(jnp.int32)
    target = jnp.where(owner[...] == 1, 128 + ones_before, lane_g - ones_before)
    st_hot[...] = hot(target, 0, 256)
    s_hot[...] = st_hot[...].astype(F32).T.astype(BF)
    cd = cdiag[...]
    first_weight[...] = (0.8 * 0.064) / cd
    weight = 0.8 / cd

    gfa = g_coarse[...]
    gg = exact(gfa, small[0:8, :]) * small[56:104, :]
    gg = exact(small[8:56, 0:48], gg) * small[104:152, :]
    ggh, ggl = halves(gg)
    qrep = jnp.concatenate([q_coarse[...]] * 5, axis=0)
    qq = exact(qrep, small[0:8, 0:40]) * small[104:144, 0:40]

    c_nbr.wait_recv()
    own_nbr = jnp.where(m == 0, nbr[:, 0:128], nbr[:, 128:256])
    got_nbr = rcv_n[0:6, :]
    for o in range(2):
        lists = jnp.where(m == o, own_nbr, got_nbr)
        for f in range(6):
            for d in range(3):
                ohc[o, d, :, f * 128 : f * 128 + 128] = hot(lists[f : f + 1, :], d * 256, 256)

    def take(ref):
        hi, lo = halves(ref[...])
        return jnp.concatenate([hi, lo], axis=0)

    c_mem.wait_recv()
    arr_m[...] = take(rcv_m)
    z = dot(by_face[...], arr_m[...])
    for f in range(6):
        part = dot(stacked(z[f * 48 : f * 48 + 40]), ohrm[f])
        rest0 = rest0 + (part[:40] + part[40:])
    for t in (1 - far, far):
        group, there = side(t)
        halves_of = [remote(snd_g.at[t, h], rcv_g.at[t, h], 1 + t, (1, 10)[h] + t, (group, m)) for h in range(2)]
        for h in range(2):
            pl.when(there)(halves_of[h].wait_recv)
            arr_g[t, :, h * 128 : h * 128 + 128] = take(rcv_g.at[t, h])
            if t is far:
                z = dot(by_face[...], arr_g[t, :, h * 128 : h * 128 + 128])
                for f in range(6):
                    part = dot(stacked(z[f * 48 : f * 48 + 40]), ohr[t, f, h * 128 : h * 128 + 128, :])
                    rest0 = rest0 + (part[:40] + part[40:])
        if t is not far:
            z = dot(by_face[...], arr_g[t])
            for f in range(6):
                part = dot(stacked(z[f * 48 : f * 48 + 40]), ohr[t, f])
                rest0 = rest0 + (part[:40] + part[40:])
    first = rest0 * first_weight[...]
    packed = dot(stacked(first), s_hot[...])
    mine[...] = packed[:40] + packed[40:]
    c_two = []
    for t in (far, 1 - far):
        group, there = side(t)
        place = jnp.where(t == 0, 4 + m, m)
        for k in range(2):
            c = remote(mine, blks.at[place], 4 + 2 * t + k, 4 + place, (group, k))
            pl.when(there)(c.start)
            c_two.append((there, c))
    c_own = remote(mine, blks.at[2 + m], 8, 6 + m, (g, other))
    c_own.start()

    for f in range(6):
        acc = dot(arr_g[0], ohr[0, f]) + dot(arr_g[1], ohr[1, f]) + dot(arr_m[...], ohrm[f])
        nlh[f * 128 : f * 128 + 128, :] += acc[:128].astype(BF)
        nll[f * 128 : f * 128 + 128, :] += acc[128:].astype(BF)
    need(20)
    for v in range(5):
        lf = lift[v * 128 : v * 128 + 128, :]
        full = resl[v * 128 : v * 128 + 128, :] + dot(lf, nlh[...]) + dot(lf, nll[...])
        resv[v] = full[:125]
    c_out = pltpu.make_async_copy(resv, resid_out, out_sem.at[0])
    c_out.start()
    inner = exact(qq, first)
    base = 1.2 * first - weight * inner

    def arrived(place):
        remote(mine, blks.at[place], 8, 4 + place, (g, other)).wait_recv()

    def neighbours(d):
        a, b = stacked(blks[2 * d]), stacked(blks[2 * d + 1])
        return [
            dot(jnp.concatenate([a[:, o * 128 : o * 128 + 128], b[:, o * 128 : o * 128 + 128]], axis=1), ohc[o, d])
            for o in range(2)
        ]

    arrived(2 + other)
    blks[2 + m] = mine[...]
    nears = neighbours(1)
    for t in (1 - far, far):

        @pl.when(side(t)[1])
        def _(t=t):
            arrived(4 * t)
            arrived(4 * t + 1)

        nears = [x + y for x, y in zip(nears, neighbours(2 * t))]
    nhs, nls = [], []
    for o in range(2):
        near = nears[o]
        nhs.append(jnp.concatenate([near[:40, f * 128 : f * 128 + 128] for f in range(6)], axis=0))
        nls.append(jnp.concatenate([near[40:, f * 128 : f * 128 + 128] for f in range(6)], axis=0))
    nh = jnp.concatenate(nhs, axis=1).astype(BF)
    nl = jnp.concatenate(nls, axis=1).astype(BF)
    across = (dot(ggh, nh) + dot(ggh, nl) + dot(ggl, nh))[:40]
    back = dot(stacked(across), st_hot[...])
    mine2[...] = base + weight * (back[:40] + back[40:])
    c_second = pltpu.make_async_copy(mine2, second_out, out_sem.at[1])
    c_second.start()

    for c in (c_nbr, c_mem, c_own):
        c.wait_send()
    for there, c in c_grp + c_two:
        pl.when(there)(c.wait_send)
    c_out.wait()
    c_second.wait()


def last_kernel(resid, second_h, pro2_h, resid_out, corr_out, second, pro2, corr, held, sem):
    loads = [pltpu.make_async_copy(second_h, second, sem.at[0]), pltpu.make_async_copy(pro2_h, pro2, sem.at[1])]
    whole = pltpu.make_async_copy(resid, held, sem.at[2])
    for c in loads:
        c.start()
    whole.start()
    for c in loads:
        c.wait()
    copies = []
    for v in range(5):
        corr[v] = dot(pro2[...], stacked(second[v * 8 : v * 8 + 8, :]))[:125]
        c = pltpu.make_async_copy(corr.at[v], corr_out.at[v], sem.at[4 + v])
        c.start()
        copies.append(c)
    whole.wait()
    c = pltpu.make_async_copy(held, resid_out, sem.at[3])
    c.start()
    copies.append(c)
    for c in copies:
        c.wait()


def shards(
    state, rhs, fine_diag, q_fine, var_mix, mem_count, grp_count, send_mem_idx, send_grp_idx,
    face_src, coarse_diag, q_coarse, g_coarse, owner, coarse_nbr,
):
    places, lift, rest, rest_lift, by_face, pro2, small = tables()
    n_grp = lax.axis_size("grp")
    hbm = pl.BlockSpec(memory_space=pltpu.HBM)
    field = jax.ShapeDtypeStruct((5, 125, 256), F32)
    operands = (
        state, send_mem_idx, send_grp_idx, mem_count, grp_count, jnp.asarray(places), coarse_nbr, face_src, rhs, fine_diag,
        q_fine, var_mix, jnp.asarray(rest), jnp.asarray(rest_lift), owner.reshape(1, 256), coarse_diag.reshape(40, 256),
        g_coarse.reshape(48, 8), q_coarse, jnp.asarray(small), jnp.asarray(by_face), jnp.asarray(lift),
    )
    resid, second = pl.pallas_call(
        functools.partial(main_kernel, n_grp),
        out_shape=(field, jax.ShapeDtypeStruct((40, 256), F32)),
        in_specs=[hbm] * 21,
        out_specs=(hbm, hbm),
        scratch_shapes=[pltpu.VMEM(a.shape, a.dtype) for a in operands]
        + [
            pltpu.VMEM((640, 256), BF),
            pltpu.VMEM((640, 256), BF),
            pltpu.VMEM((128, 128), F32),
            pltpu.VMEM((2, 1536, 256), BF),
            pltpu.VMEM((1536, 128), BF),
            pltpu.VMEM((256, 1536), BF),
            pltpu.VMEM((2, 2, 128, 128), F32),
            pltpu.VMEM((128, 128), F32),
            pltpu.VMEM((8, 128), jnp.int32),
            pltpu.VMEM((2, 2, 128, 128), F32),
            pltpu.VMEM((128, 128), F32),
            pltpu.VMEM((8, 128), jnp.int32),
            pltpu.VMEM((2, 6, 256, 256), BF),
            pltpu.VMEM((6, 128, 256), BF),
            pltpu.VMEM((768, 256), BF),
            pltpu.VMEM((768, 256), BF),
            pltpu.VMEM((640, 256), F32),
            pltpu.VMEM((2, 3, 256, 768), BF),
            pltpu.VMEM((256, 256), BF),
            pltpu.VMEM((256, 256), BF),
            pltpu.VMEM((40, 256), F32),
            pltpu.VMEM((6, 40, 256), F32),
            pltpu.VMEM((40, 256), F32),
            pltpu.VMEM((5, 125, 256), F32),
            pltpu.VMEM((40, 256), F32),
            pltpu.VMEM((384, 256), BF),
            pltpu.VMEM((384, 256), BF),
            pltpu.VMEM((192, 128), BF),
            pltpu.VMEM((2, 256, 256), BF),
            pltpu.VMEM((256, 128), BF),
            pltpu.SemaphoreType.DMA((21,)),
            pltpu.SemaphoreType.DMA((5,)),
            pltpu.SemaphoreType.DMA((11,)),
            pltpu.SemaphoreType.DMA((12,)),
            pltpu.SemaphoreType.DMA((2,)),
        ],
        compiler_params=pltpu.CompilerParams(
            collective_id=0, has_side_effects=True, vmem_limit_bytes=60 * 1024 * 1024
        ),
        name="residual_and_sweeps",
    )(*operands)
    return pl.pallas_call(
        last_kernel,
        out_shape=(field, field),
        in_specs=[hbm, hbm, hbm],
        out_specs=(hbm, hbm),
        scratch_shapes=[
            pltpu.VMEM((40, 256), F32),
            pltpu.VMEM((128, 16), BF),
            pltpu.VMEM((5, 125, 256), F32),
            pltpu.VMEM((5, 125, 256), F32),
            pltpu.SemaphoreType.DMA((9,)),
        ],
        compiler_params=pltpu.CompilerParams(vmem_limit_bytes=60 * 1024 * 1024),
        name="prolongation",
    )(resid, second, jnp.asarray(pro2))


def solution(mesh):
    whole = ("grp", "mem")
    return jax.shard_map(
        shards,
        mesh=mesh,
        in_specs=(
            P(None, None, whole), P(None, None, whole), P(None, None, whole), P(), P(),
            P(whole, None), P(whole, None), P(whole, None, None), P(whole, None, None), P(None, whole),
            P(None, None, whole), P(), P(), P(whole, None), P(None, whole),
        ),
        out_specs=(P(None, None, whole), P(None, None, whole)),
        check_vma=False,
    )
```

```python
import functools

import jax
import jax.numpy as jnp
import ml_dtypes
import numpy as np
from jax import lax
from jax.experimental import pallas as pl
from jax.experimental.pallas import tpu as pltpu
from jax.sharding import PartitionSpec as P

MESH = pl.DeviceIdType.MESH
HIGH = lax.Precision.HIGHEST
BF = jnp.bfloat16
F32 = jnp.float32


def tables():
    points = np.arange(125)
    coords = [points // 25, points // 5 % 5, points % 5]
    extract = np.zeros((6, 25, 125), np.float32)
    for face in range(6):
        along = face // 2
        others = [c for b, c in enumerate(coords) if b != along]
        index = others[0] * 5 + others[1]
        on_face = coords[along] == 4 * (face % 2)
        extract[face] = (index[None, :] == np.arange(25)[:, None]) & on_face[None, :]
    nodes = -1.0 + 0.5 * np.arange(5)
    basis = np.stack([(1.0 - nodes) / 2.0, (1.0 + nodes) / 2.0], axis=1)
    prolong = np.einsum("ia,jb,kc->ijkabc", basis, basis, basis).reshape(125, 8)
    ext = np.zeros((6, 128, 5, 128), np.float32)
    for v in range(5):
        ext[:, v * 25 : v * 25 + 25, v, :125] = extract
    ext = ext.reshape(768, 640)
    places = np.full((8, 640), -1, np.int32)
    for face in range(6):
        block = ext[face * 128 : face * 128 + 128]
        places[face] = np.where(block.any(axis=0), block.argmax(axis=0), -1)
    lift = np.ascontiguousarray(ext.T)
    rest = np.zeros((48, 5, 128), np.float32)
    for v in range(5):
        rest[v * 8 : v * 8 + 8, v, :125] = prolong.T
    rest = rest.reshape(48, 640)
    rest_lift = rest @ lift
    by_face = rest_lift.reshape(48, 6, 128).transpose(1, 0, 2).reshape(288, 128)
    by_face = np.concatenate([by_face, by_face], axis=1)
    pro2 = np.concatenate([rest[:8, :128].T, rest[:8, :128].T], axis=1)
    spread = np.zeros((8, 6, 5, 8), np.float32)
    for b in range(8):
        spread[b, :, :, b] = 1.0
    spread = spread.reshape(8, 240)
    gather_a = np.zeros((48, 48), np.float32)
    for v in range(5):
        for f in range(6):
            for a in range(8):
                gather_a[v * 8 + a, f * 8 + a] = 1.0
    same_f = np.zeros((6, 8, 6, 40), np.float32)
    for f in range(6):
        same_f[f, :, f, :] = 1.0
    same_f = same_f.reshape(48, 240)
    same_v = np.zeros((6, 8, 6, 5, 8), np.float32)
    for v in range(5):
        same_v[v, :, :, v, :] = 1.0
    same_v = same_v.reshape(48, 240)
    small = np.zeros((152, 240), np.float32)
    small[0:8] = spread
    small[8:56, :48] = gather_a
    small[56:104] = same_f
    small[104:152] = same_v
    cast = lambda a: np.asarray(a, ml_dtypes.bfloat16)
    return places, cast(lift), cast(rest), cast(rest_lift), cast(by_face), cast(pro2), small


def halves(x):
    hi = x.astype(BF)
    return hi, (x - hi.astype(F32)).astype(BF)


def stacked(x):
    hi = x.astype(BF).astype(F32)
    return jnp.concatenate([hi, x - hi], axis=0).astype(BF)


def dot(a, b):
    return jnp.dot(a, b, preferred_element_type=F32)


def exact(a, b):
    return jnp.dot(a, b, precision=HIGH, preferred_element_type=F32)


def hot(row, base, size):
    row = (row - base).astype(jnp.int16)
    places = lax.broadcasted_iota(jnp.int16, (size, row.shape[1]), 0)
    return jnp.where(places == row, jnp.ones((), BF), jnp.zeros((), BF))


def padded(x):
    return jnp.concatenate([x, jnp.zeros((3, x.shape[1]), F32)], axis=0)


def main_kernel(n_grp, *refs):
    sources, (resid_out, second_out), scratch = refs[:21], refs[21:23], refs[23:]
    (
        st, midx, gidx, mcount, gcount, places, cnbr, fsrc, rh, dg, q_fine, var_mix,
        rest, rest_lift, owner, cdiag, g_coarse, q_coarse, small, by_face, lift,
    ) = scratch[:21]
    (
        uh, ul, qs,
        ohs, ohm, tr, snd_g, snd_m, snd_n, rcv_g, rcv_m, rcv_n,
        ohr, ohrm, nlh, nll, resl, ohc, st_hot, blks, mine, resv, mine2, ext01, ext23, ext4, arr_g, arr_m,
        in_sem, st_sem, snd_sem, rcv_sem, out_sem,
    ) = scratch[21:]
    g = lax.axis_index("grp")
    m = lax.axis_index("mem")
    other = 1 - m
    has_prev, has_next = g > 0, g < n_grp - 1
    far = jnp.where(g == 0, 1, jnp.where((lax.rem(g, 4) == 3) & has_next, 1, 0))
    prev, nxt = jnp.maximum(g - 1, 0), jnp.minimum(g + 1, n_grp - 1)

    def side(t):
        return jnp.where(t == 0, prev, nxt), jnp.where(t == 0, has_prev, has_next)

    barrier = pltpu.get_barrier_semaphore()
    def greet(device):
        pl.semaphore_signal(barrier, inc=1, device_id=device, device_id_type=MESH)

    for t in (far, 1 - far):

        @pl.when(side(t)[1])
        def _(t=t):
            greet((side(t)[0], 0))
            greet((side(t)[0], 1))

    greet((g, other))

    loads = [None] + [pltpu.make_async_copy(sources[i], scratch[i], in_sem.at[i]) for i in range(1, 21)]
    fields = [pltpu.make_async_copy(sources[0].at[v], st.at[v], st_sem.at[v]) for v in range(5)]
    for c in loads[1:7] + fields + loads[7:8]:
        c.start()
    seen = set()

    def need(*which):
        for i in which:
            if i not in seen:
                seen.add(i)
                loads[i].wait()

    @pl.when(jnp.logical_not(has_prev))
    def _():
        rcv_g[0] = jnp.zeros((128, 256), F32)
        blks[0] = jnp.zeros((40, 256), F32)
        blks[1] = jnp.zeros((40, 256), F32)

    @pl.when(jnp.logical_not(has_next))
    def _():
        rcv_g[1] = jnp.zeros((128, 256), F32)
        blks[4] = jnp.zeros((40, 256), F32)
        blks[5] = jnp.zeros((40, 256), F32)

    need(1, 2, 3, 4, 5, 6)
    lane_g = lax.broadcasted_iota(jnp.int32, (1, 256), 1)
    lane_m = lax.broadcasted_iota(jnp.int32, (1, 128), 1)
    for t in range(2):
        row = jnp.where(lane_g < gcount[0:1, t : t + 1], gidx[0, t : t + 1, :], -1)
        ohs[t] = hot(row, 0, 1536)
    mrow = jnp.where(m == 0, midx[0, 1:2, :], midx[0, 0:1, :])
    mlim = jnp.where(m == 0, mcount[0:1, 1:2], mcount[0:1, 0:1])
    ohm[...] = hot(jnp.where(lane_m < mlim, mrow, -1), 0, 1536)
    nbr = cnbr[...]
    snd_n[0:6, :] = jnp.where(m == 0, nbr[:, 128:256], nbr[:, 0:128])
    snd_n[6:8, :] = jnp.zeros((2, 128), jnp.int32)

    for f in range(6):
        ext01[f * 64 : f * 64 + 64, :] = hot(places[f : f + 1, 0:256], 0, 64)
        ext23[f * 64 : f * 64 + 64, :] = hot(places[f : f + 1, 256:512], 48, 64)
        ext4[f * 32 : f * 32 + 32, :] = hot(places[f : f + 1, 512:640], 96, 32)

    for c in loads[8:]:
        c.start()
    for v in range(5):
        fields[v].wait()
        hi, lo = halves(padded(st[v]))
        uh[v * 128 : v * 128 + 128, :] = hi
        ul[v * 128 : v * 128 + 128, :] = lo
    for u, top in ((uh, 0), (ul, 128)):
        x, y, z = dot(ext01[...], u[0:256, :]), dot(ext23[...], u[256:512, :]), dot(ext4[...], u[512:640, :])
        for f in range(6):
            xf, yf, zf = x[f * 64 : f * 64 + 64], y[f * 64 : f * 64 + 64], z[f * 32 : f * 32 + 32]
            rows = [xf[:48], xf[48:] + yf[:16], yf[16:48], yf[48:] + zf[:16], zf[16:]]
            tr[top : top + 128, f * 256 : f * 256 + 256] = jnp.concatenate(rows, axis=0).astype(BF)

    def remote(src, dst, i, j, device):
        return pltpu.make_async_remote_copy(
            src_ref=src, dst_ref=dst, send_sem=snd_sem.at[i], recv_sem=rcv_sem.at[j],
            device_id=device, device_id_type=MESH,
        )

    c_nbr = remote(snd_n, rcv_n, 0, 0, (g, other))
    c_grp = []
    for t in (far, 1 - far):
        group, there = side(t)
        picked = dot(tr[...], ohs[t])
        snd_g[t] = picked[:128] + picked[128:]
        c = remote(snd_g.at[t], rcv_g.at[1 - t], 1 + t, 2 - t, (group, m))
        if t is far:
            pl.semaphore_wait(barrier, 1 + 2 * has_prev.astype(jnp.int32) + 2 * has_next.astype(jnp.int32))
        pl.when(there)(c.start)
        c_grp.append((there, c))
    picked = dot(tr[...], ohm[...])
    snd_m[...] = picked[:128] + picked[128:]
    c_mem = remote(snd_m, rcv_m, 3, 3, (g, other))
    c_mem.start()
    c_nbr.start()

    base_mem = 1536 + other * 128

    def local_faces(f, carry):
        row = fsrc[pl.ds(f, 1), :]
        acc = dot(tr[...], hot(row, 0, 1536))
        at = pl.multiple_of(f * 128, 128)
        nlh[pl.ds(at, 128), :] = acc[:128].astype(BF)
        nll[pl.ds(at, 128), :] = acc[128:].astype(BF)
        ohr[0, f] = hot(row, 1792, 256)
        ohr[1, f] = hot(row, 2048, 256)
        ohrm[f] = hot(row, base_mem, 128)
        return carry

    need(7)
    lax.fori_loop(0, 6, local_faces, 0)

    need(*range(8, 20))
    qs[...] = jnp.zeros((128, 128), F32)
    qs[0:125, 0:125] = q_fine[...]
    qh, ql = halves(qs[...])
    for v in range(5):
        total = dot(qh, uh[v * 128 : v * 128 + 128, :]) + dot(qh, ul[v * 128 : v * 128 + 128, :])
        total = (total + dot(ql, uh[v * 128 : v * 128 + 128, :]))[:125]
        total = total + dg[v] * st[v]
        for w in range(5):
            total = total + var_mix[v : v + 1, w : w + 1] * st[w]
        resl[v * 128 : v * 128 + 128, :] = padded(rh[v] - total)
    rl_h, rl_l = halves(resl[...])
    rest0 = dot(rest[...], rl_h) + dot(rest[...], rl_l)
    rest0 = rest0 + dot(rest_lift[...], nlh[...]) + dot(rest_lift[...], nll[...])
    rest0 = rest0[:40]

    own = owner[...].astype(F32)
    before = lax.broadcasted_iota(jnp.int32, (256, 256), 0) < lax.broadcasted_iota(jnp.int32, (256, 256), 1)
    ones_before = dot(jnp.broadcast_to(own, (16, 256)).astype(BF), jnp.where(before, 1.0, 0.0).astype(BF))[0:1]
    ones_before = ones_before.astype(jnp.int32)
    target = jnp.where(owner[...] == 1, 128 + ones_before, lane_g - ones_before)
    st_hot[...] = hot(target, 0, 256)

    gfa = g_coarse[...]
    gg = exact(gfa, small[0:8, :]) * small[56:104, :]
    gg = exact(small[8:56, 0:48], gg) * small[104:152, :]
    ggh, ggl = halves(gg)
    qrep = jnp.concatenate([q_coarse[...]] * 5, axis=0)
    qq = exact(qrep, small[0:8, 0:40]) * small[104:144, 0:40]

    c_nbr.wait_recv()
    own_nbr = jnp.where(m == 0, nbr[:, 0:128], nbr[:, 128:256])
    got_nbr = rcv_n[0:6, :]
    for o in range(2):
        lists = jnp.where(m == o, own_nbr, got_nbr)
        for f in range(6):
            for d in range(3):
                ohc[o, d, :, f * 128 : f * 128 + 128] = hot(lists[f : f + 1, :], d * 256, 256)

    def take(ref):
        hi, lo = halves(ref[...])
        return jnp.concatenate([hi, lo], axis=0)

    c_mem.wait_recv()
    arr_m[...] = take(rcv_m)
    z = dot(by_face[...], arr_m[...])
    for f in range(6):
        part = dot(stacked(z[f * 48 : f * 48 + 40]), ohrm[f])
        rest0 = rest0 + (part[:40] + part[40:])
    for t in (1 - far, far):
        group, there = side(t)
        pl.when(there)(remote(snd_g.at[t], rcv_g.at[t], 1 + t, 1 + t, (group, m)).wait_recv)
        arr_g[t] = take(rcv_g.at[t])
        z = dot(by_face[...], arr_g[t])
        for f in range(6):
            part = dot(stacked(z[f * 48 : f * 48 + 40]), ohr[t, f])
            rest0 = rest0 + (part[:40] + part[40:])
    cd = cdiag[...]
    first = (0.8 * 0.064) * rest0 / cd
    packed = lax.dot_general(stacked(first), st_hot[...], (((1,), (1,)), ((), ())), preferred_element_type=F32)
    mine[...] = packed[:40] + packed[40:]
    c_two = []
    for t in (far, 1 - far):
        group, there = side(t)
        place = jnp.where(t == 0, 4 + m, m)
        for k in range(2):
            c = remote(mine, blks.at[place], 4 + 2 * t + k, 4 + place, (group, k))
            pl.when(there)(c.start)
            c_two.append((there, c))
    c_own = remote(mine, blks.at[2 + m], 8, 6 + m, (g, other))
    c_own.start()

    for f in range(6):
        acc = dot(arr_g[0], ohr[0, f]) + dot(arr_g[1], ohr[1, f]) + dot(arr_m[...], ohrm[f])
        nlh[f * 128 : f * 128 + 128, :] += acc[:128].astype(BF)
        nll[f * 128 : f * 128 + 128, :] += acc[128:].astype(BF)
    need(20)
    for v in range(5):
        lf = lift[v * 128 : v * 128 + 128, :]
        full = resl[v * 128 : v * 128 + 128, :] + dot(lf, nlh[...]) + dot(lf, nll[...])
        resv[v] = full[:125]
    c_out = pltpu.make_async_copy(resv, resid_out, out_sem.at[0])
    c_out.start()
    inner = exact(qq, first)
    weight = 0.8 / cd
    base = 1.2 * first - weight * inner

    def arrived(place):
        remote(mine, blks.at[place], 8, 4 + place, (g, other)).wait_recv()

    def neighbours(d):
        a, b = stacked(blks[2 * d]), stacked(blks[2 * d + 1])
        return [
            dot(jnp.concatenate([a[:, o * 128 : o * 128 + 128], b[:, o * 128 : o * 128 + 128]], axis=1), ohc[o, d])
            for o in range(2)
        ]

    arrived(2 + other)
    blks[2 + m] = mine[...]
    nears = neighbours(1)
    for t in (1 - far, far):

        @pl.when(side(t)[1])
        def _(t=t):
            arrived(4 * t)
            arrived(4 * t + 1)

        nears = [x + y for x, y in zip(nears, neighbours(2 * t))]
    nhs, nls = [], []
    for o in range(2):
        near = nears[o]
        nhs.append(jnp.concatenate([near[:40, f * 128 : f * 128 + 128] for f in range(6)], axis=0))
        nls.append(jnp.concatenate([near[40:, f * 128 : f * 128 + 128] for f in range(6)], axis=0))
    nh = jnp.concatenate(nhs, axis=1).astype(BF)
    nl = jnp.concatenate(nls, axis=1).astype(BF)
    across = (dot(ggh, nh) + dot(ggh, nl) + dot(ggl, nh))[:40]
    back = dot(stacked(across), st_hot[...])
    mine2[...] = base + weight * (back[:40] + back[40:])
    c_second = pltpu.make_async_copy(mine2, second_out, out_sem.at[1])
    c_second.start()

    for c in (c_nbr, c_mem, c_own):
        c.wait_send()
    for there, c in c_grp + c_two:
        pl.when(there)(c.wait_send)
    c_out.wait()
    c_second.wait()


def last_kernel(resid, second_h, pro2_h, resid_out, corr_out, second, pro2, corr, held, sem):
    loads = [pltpu.make_async_copy(second_h, second, sem.at[0]), pltpu.make_async_copy(pro2_h, pro2, sem.at[1])]
    whole = pltpu.make_async_copy(resid, held, sem.at[2])
    for c in loads:
        c.start()
    whole.start()
    for c in loads:
        c.wait()
    copies = []
    for v in range(5):
        corr[v] = dot(pro2[...], stacked(second[v * 8 : v * 8 + 8, :]))[:125]
        c = pltpu.make_async_copy(corr.at[v], corr_out.at[v], sem.at[4 + v])
        c.start()
        copies.append(c)
    whole.wait()
    c = pltpu.make_async_copy(held, resid_out, sem.at[3])
    c.start()
    copies.append(c)
    for c in copies:
        c.wait()


def shards(
    state, rhs, fine_diag, q_fine, var_mix, mem_count, grp_count, send_mem_idx, send_grp_idx,
    face_src, coarse_diag, q_coarse, g_coarse, owner, coarse_nbr,
):
    places, lift, rest, rest_lift, by_face, pro2, small = tables()
    n_grp = lax.axis_size("grp")
    hbm = pl.BlockSpec(memory_space=pltpu.HBM)
    field = jax.ShapeDtypeStruct((5, 125, 256), F32)
    operands = (
        state, send_mem_idx, send_grp_idx, mem_count, grp_count, jnp.asarray(places), coarse_nbr, face_src, rhs, fine_diag,
        q_fine, var_mix, jnp.asarray(rest), jnp.asarray(rest_lift), owner.reshape(1, 256), coarse_diag.reshape(40, 256),
        g_coarse.reshape(48, 8), q_coarse, jnp.asarray(small), jnp.asarray(by_face), jnp.asarray(lift),
    )
    resid, second = pl.pallas_call(
        functools.partial(main_kernel, n_grp),
        out_shape=(field, jax.ShapeDtypeStruct((40, 256), F32)),
        in_specs=[hbm] * 21,
        out_specs=(hbm, hbm),
        scratch_shapes=[pltpu.VMEM(a.shape, a.dtype) for a in operands]
        + [
            pltpu.VMEM((640, 256), BF),
            pltpu.VMEM((640, 256), BF),
            pltpu.VMEM((128, 128), F32),
            pltpu.VMEM((2, 1536, 256), BF),
            pltpu.VMEM((1536, 128), BF),
            pltpu.VMEM((256, 1536), BF),
            pltpu.VMEM((2, 128, 256), F32),
            pltpu.VMEM((128, 128), F32),
            pltpu.VMEM((8, 128), jnp.int32),
            pltpu.VMEM((2, 128, 256), F32),
            pltpu.VMEM((128, 128), F32),
            pltpu.VMEM((8, 128), jnp.int32),
            pltpu.VMEM((2, 6, 256, 256), BF),
            pltpu.VMEM((6, 128, 256), BF),
            pltpu.VMEM((768, 256), BF),
            pltpu.VMEM((768, 256), BF),
            pltpu.VMEM((640, 256), F32),
            pltpu.VMEM((2, 3, 256, 768), BF),
            pltpu.VMEM((256, 256), BF),
            pltpu.VMEM((6, 40, 256), F32),
            pltpu.VMEM((40, 256), F32),
            pltpu.VMEM((5, 125, 256), F32),
            pltpu.VMEM((40, 256), F32),
            pltpu.VMEM((384, 256), BF),
            pltpu.VMEM((384, 256), BF),
            pltpu.VMEM((192, 128), BF),
            pltpu.VMEM((2, 256, 256), BF),
            pltpu.VMEM((256, 128), BF),
            pltpu.SemaphoreType.DMA((21,)),
            pltpu.SemaphoreType.DMA((5,)),
            pltpu.SemaphoreType.DMA((9,)),
            pltpu.SemaphoreType.DMA((10,)),
            pltpu.SemaphoreType.DMA((2,)),
        ],
        compiler_params=pltpu.CompilerParams(
            collective_id=0, has_side_effects=True, vmem_limit_bytes=60 * 1024 * 1024
        ),
        name="residual_and_sweeps",
    )(*operands)
    return pl.pallas_call(
        last_kernel,
        out_shape=(field, field),
        in_specs=[hbm, hbm, hbm],
        out_specs=(hbm, hbm),
        scratch_shapes=[
            pltpu.VMEM((40, 256), F32),
            pltpu.VMEM((128, 16), BF),
            pltpu.VMEM((5, 125, 256), F32),
            pltpu.VMEM((5, 125, 256), F32),
            pltpu.SemaphoreType.DMA((9,)),
        ],
        compiler_params=pltpu.CompilerParams(vmem_limit_bytes=60 * 1024 * 1024),
        name="prolongation",
    )(resid, second, jnp.asarray(pro2))


def solution(mesh):
    whole = ("grp", "mem")
    return jax.shard_map(
        shards,
        mesh=mesh,
        in_specs=(
            P(None, None, whole), P(None, None, whole), P(None, None, whole), P(), P(),
            P(whole, None), P(whole, None), P(whole, None, None), P(whole, None, None), P(None, whole),
            P(None, None, whole), P(), P(), P(whole, None), P(None, whole),
        ),
        out_specs=(P(None, None, whole), P(None, None, whole)),
        check_vma=False,
    )
```

```python
import functools

import jax
import jax.numpy as jnp
import ml_dtypes
import numpy as np
from jax import lax
from jax.experimental import pallas as pl
from jax.experimental.pallas import tpu as pltpu
from jax.sharding import PartitionSpec as P

MESH = pl.DeviceIdType.MESH
HIGH = lax.Precision.HIGHEST
BF = jnp.bfloat16
F32 = jnp.float32


def tables():
    points = np.arange(125)
    coords = [points // 25, points // 5 % 5, points % 5]
    extract = np.zeros((6, 25, 125), np.float32)
    for face in range(6):
        along = face // 2
        others = [c for b, c in enumerate(coords) if b != along]
        index = others[0] * 5 + others[1]
        on_face = coords[along] == 4 * (face % 2)
        extract[face] = (index[None, :] == np.arange(25)[:, None]) & on_face[None, :]
    nodes = -1.0 + 0.5 * np.arange(5)
    basis = np.stack([(1.0 - nodes) / 2.0, (1.0 + nodes) / 2.0], axis=1)
    prolong = np.einsum("ia,jb,kc->ijkabc", basis, basis, basis).reshape(125, 8)
    ext = np.zeros((6, 128, 5, 128), np.float32)
    for v in range(5):
        ext[:, v * 25 : v * 25 + 25, v, :125] = extract
    ext = ext.reshape(768, 640)
    places = np.full((8, 640), -1, np.int32)
    for face in range(6):
        block = ext[face * 128 : face * 128 + 128]
        places[face] = np.where(block.any(axis=0), block.argmax(axis=0), -1)
    lift = np.ascontiguousarray(ext.T)
    rest = np.zeros((48, 5, 128), np.float32)
    for v in range(5):
        rest[v * 8 : v * 8 + 8, v, :125] = prolong.T
    rest = rest.reshape(48, 640)
    rest_lift = rest @ lift
    by_face = rest_lift.reshape(48, 6, 128).transpose(1, 0, 2).reshape(288, 128)
    by_face = np.concatenate([by_face, by_face], axis=1)
    pro2 = np.concatenate([rest[:8, :128].T, rest[:8, :128].T], axis=1)
    spread = np.zeros((8, 6, 5, 8), np.float32)
    for b in range(8):
        spread[b, :, :, b] = 1.0
    spread = spread.reshape(8, 240)
    gather_a = np.zeros((48, 48), np.float32)
    for v in range(5):
        for f in range(6):
            for a in range(8):
                gather_a[v * 8 + a, f * 8 + a] = 1.0
    same_f = np.zeros((6, 8, 6, 40), np.float32)
    for f in range(6):
        same_f[f, :, f, :] = 1.0
    same_f = same_f.reshape(48, 240)
    same_v = np.zeros((6, 8, 6, 5, 8), np.float32)
    for v in range(5):
        same_v[v, :, :, v, :] = 1.0
    same_v = same_v.reshape(48, 240)
    small = np.zeros((152, 240), np.float32)
    small[0:8] = spread
    small[8:56, :48] = gather_a
    small[56:104] = same_f
    small[104:152] = same_v
    cast = lambda a: np.asarray(a, ml_dtypes.bfloat16)
    return places, cast(lift), cast(rest), cast(rest_lift), cast(by_face), cast(pro2), small


def halves(x):
    hi = x.astype(BF)
    return hi, (x - hi.astype(F32)).astype(BF)


def stacked(x):
    hi = x.astype(BF).astype(F32)
    return jnp.concatenate([hi, x - hi], axis=0).astype(BF)


def dot(a, b):
    return jnp.dot(a, b, preferred_element_type=F32)


def exact(a, b):
    return jnp.dot(a, b, precision=HIGH, preferred_element_type=F32)


def hot(row, base, size):
    row = (row - base).astype(jnp.int16)
    places = lax.broadcasted_iota(jnp.int16, (size, row.shape[1]), 0)
    return jnp.where(places == row, jnp.ones((), BF), jnp.zeros((), BF))


def padded(x):
    return jnp.concatenate([x, jnp.zeros((3, x.shape[1]), F32)], axis=0)


def main_kernel(n_grp, *refs):
    sources, (resid_out, second_out), scratch = refs[:21], refs[21:23], refs[23:]
    (
        st, midx, gidx, mcount, gcount, places, cnbr, fsrc, rh, dg, q_fine, var_mix,
        rest, rest_lift, owner, cdiag, g_coarse, q_coarse, small, by_face, lift,
    ) = scratch[:21]
    (
        uh, ul, qs,
        ohs, ohm, tr, snd_g, snd_m, snd_n, rcv_g, rcv_m, rcv_n,
        ohr, ohrm, nlh, nll, resl, ohc, st_hot, blks, mine, resv, mine2, ext01, ext23, ext4, arr_g, arr_m,
        in_sem, st_sem, snd_sem, rcv_sem, out_sem,
    ) = scratch[21:]
    g = lax.axis_index("grp")
    m = lax.axis_index("mem")
    other = 1 - m
    has_prev, has_next = g > 0, g < n_grp - 1
    far = jnp.where(g == 0, 1, jnp.where((lax.rem(g, 4) == 3) & has_next, 1, 0))
    prev, nxt = jnp.maximum(g - 1, 0), jnp.minimum(g + 1, n_grp - 1)

    def side(t):
        return jnp.where(t == 0, prev, nxt), jnp.where(t == 0, has_prev, has_next)

    barrier = pltpu.get_barrier_semaphore()
    def greet(device):
        pl.semaphore_signal(barrier, inc=1, device_id=device, device_id_type=MESH)

    for t in (far, 1 - far):

        @pl.when(side(t)[1])
        def _(t=t):
            greet((side(t)[0], 0))
            greet((side(t)[0], 1))

    greet((g, other))

    loads = [None] + [pltpu.make_async_copy(sources[i], scratch[i], in_sem.at[i]) for i in range(1, 21)]
    fields = [pltpu.make_async_copy(sources[0].at[v], st.at[v], st_sem.at[v]) for v in range(5)]
    for c in loads[1:7] + fields + loads[7:8]:
        c.start()
    seen = set()

    def need(*which):
        for i in which:
            if i not in seen:
                seen.add(i)
                loads[i].wait()

    @pl.when(jnp.logical_not(has_prev))
    def _():
        rcv_g[0] = jnp.zeros((128, 256), F32)
        blks[0] = jnp.zeros((40, 256), F32)
        blks[1] = jnp.zeros((40, 256), F32)

    @pl.when(jnp.logical_not(has_next))
    def _():
        rcv_g[1] = jnp.zeros((128, 256), F32)
        blks[4] = jnp.zeros((40, 256), F32)
        blks[5] = jnp.zeros((40, 256), F32)

    need(1, 2, 3, 4, 5, 6)
    lane_g = lax.broadcasted_iota(jnp.int32, (1, 256), 1)
    lane_m = lax.broadcasted_iota(jnp.int32, (1, 128), 1)
    for t in range(2):
        row = jnp.where(lane_g < gcount[0:1, t : t + 1], gidx[0, t : t + 1, :], -1)
        ohs[t] = hot(row, 0, 1536)
    mrow = jnp.where(m == 0, midx[0, 1:2, :], midx[0, 0:1, :])
    mlim = jnp.where(m == 0, mcount[0:1, 1:2], mcount[0:1, 0:1])
    ohm[...] = hot(jnp.where(lane_m < mlim, mrow, -1), 0, 1536)
    nbr = cnbr[...]
    snd_n[0:6, :] = jnp.where(m == 0, nbr[:, 128:256], nbr[:, 0:128])
    snd_n[6:8, :] = jnp.zeros((2, 128), jnp.int32)

    for f in range(6):
        ext01[f * 64 : f * 64 + 64, :] = hot(places[f : f + 1, 0:256], 0, 64)
        ext23[f * 64 : f * 64 + 64, :] = hot(places[f : f + 1, 256:512], 48, 64)
        ext4[f * 32 : f * 32 + 32, :] = hot(places[f : f + 1, 512:640], 96, 32)

    for c in loads[8:]:
        c.start()
    for v in range(5):
        fields[v].wait()
        hi, lo = halves(padded(st[v]))
        uh[v * 128 : v * 128 + 128, :] = hi
        ul[v * 128 : v * 128 + 128, :] = lo
    for u, top in ((uh, 0), (ul, 128)):
        x, y, z = dot(ext01[...], u[0:256, :]), dot(ext23[...], u[256:512, :]), dot(ext4[...], u[512:640, :])
        for f in range(6):
            xf, yf, zf = x[f * 64 : f * 64 + 64], y[f * 64 : f * 64 + 64], z[f * 32 : f * 32 + 32]
            rows = [xf[:48], xf[48:] + yf[:16], yf[16:48], yf[48:] + zf[:16], zf[16:]]
            tr[top : top + 128, f * 256 : f * 256 + 256] = jnp.concatenate(rows, axis=0).astype(BF)

    def remote(src, dst, i, j, device):
        return pltpu.make_async_remote_copy(
            src_ref=src, dst_ref=dst, send_sem=snd_sem.at[i], recv_sem=rcv_sem.at[j],
            device_id=device, device_id_type=MESH,
        )

    c_nbr = remote(snd_n, rcv_n, 0, 0, (g, other))
    c_grp = []
    for t in (far, 1 - far):
        group, there = side(t)
        picked = dot(tr[...], ohs[t])
        snd_g[t] = picked[:128] + picked[128:]
        c = remote(snd_g.at[t], rcv_g.at[1 - t], 1 + t, 2 - t, (group, m))
        if t is far:
            pl.semaphore_wait(barrier, 1 + 2 * has_prev.astype(jnp.int32) + 2 * has_next.astype(jnp.int32))
        pl.when(there)(c.start)
        c_grp.append((there, c))
    picked = dot(tr[...], ohm[...])
    snd_m[...] = picked[:128] + picked[128:]
    c_mem = remote(snd_m, rcv_m, 3, 3, (g, other))
    c_mem.start()
    c_nbr.start()

    base_mem = 1536 + other * 128

    def local_faces(f, carry):
        row = fsrc[pl.ds(f, 1), :]
        acc = dot(tr[...], hot(row, 0, 1536))
        at = pl.multiple_of(f * 128, 128)
        nlh[pl.ds(at, 128), :] = acc[:128].astype(BF)
        nll[pl.ds(at, 128), :] = acc[128:].astype(BF)
        wide = pl.ds(pl.multiple_of(f * 256, 256), 256)
        ohr[0, wide, :] = hot(row, 1792, 256)
        ohr[1, wide, :] = hot(row, 2048, 256)
        ohrm[pl.ds(at, 128), :] = hot(row, base_mem, 128)
        return carry

    need(7)
    lax.fori_loop(0, 6, local_faces, 0)

    need(*range(8, 20))
    qs[...] = jnp.zeros((128, 128), F32)
    qs[0:125, 0:125] = q_fine[...]
    qh, ql = halves(qs[...])
    for v in range(5):
        total = dot(qh, uh[v * 128 : v * 128 + 128, :]) + dot(qh, ul[v * 128 : v * 128 + 128, :])
        total = (total + dot(ql, uh[v * 128 : v * 128 + 128, :]))[:125]
        total = total + dg[v] * st[v]
        for w in range(5):
            total = total + var_mix[v : v + 1, w : w + 1] * st[w]
        resl[v * 128 : v * 128 + 128, :] = padded(rh[v] - total)
    rl_h, rl_l = halves(resl[...])
    rest0 = dot(rest[...], rl_h) + dot(rest[...], rl_l)
    rest0 = rest0 + dot(rest_lift[...], nlh[...]) + dot(rest_lift[...], nll[...])
    rest0 = rest0[:40]

    own = owner[...].astype(F32)
    before = lax.broadcasted_iota(jnp.int32, (256, 256), 0) < lax.broadcasted_iota(jnp.int32, (256, 256), 1)
    ones_before = dot(jnp.broadcast_to(own, (16, 256)).astype(BF), jnp.where(before, 1.0, 0.0).astype(BF))[0:1]
    ones_before = ones_before.astype(jnp.int32)
    target = jnp.where(owner[...] == 1, 128 + ones_before, lane_g - ones_before)
    st_hot[...] = hot(target, 0, 256)

    gfa = g_coarse[...]
    gg = exact(gfa, small[0:8, :]) * small[56:104, :]
    gg = exact(small[8:56, 0:48], gg) * small[104:152, :]
    ggh, ggl = halves(gg)
    qrep = jnp.concatenate([q_coarse[...]] * 5, axis=0)
    qq = exact(qrep, small[0:8, 0:40]) * small[104:144, 0:40]

    c_nbr.wait_recv()
    own_nbr = jnp.where(m == 0, nbr[:, 0:128], nbr[:, 128:256])
    got_nbr = rcv_n[0:6, :]
    for o in range(2):
        lists = jnp.where(m == o, own_nbr, got_nbr)
        for f in range(6):
            for d in range(3):
                ohc[o, d, :, f * 128 : f * 128 + 128] = hot(lists[f : f + 1, :], d * 256, 256)

    def take(ref):
        hi, lo = halves(ref[...])
        return jnp.concatenate([hi, lo], axis=0)

    c_mem.wait_recv()
    arr_m[...] = take(rcv_m)

    def restricted(columns, places):
        z = dot(by_face[...], columns)
        part = dot(jnp.concatenate([stacked(z[f * 48 : f * 48 + 40]) for f in range(6)], axis=1), places)
        return part[:40] + part[40:]

    rest0 = rest0 + restricted(arr_m[...], ohrm[...])
    for t in (1 - far, far):
        group, there = side(t)
        pl.when(there)(remote(snd_g.at[t], rcv_g.at[t], 1 + t, 1 + t, (group, m)).wait_recv)
        arr_g[t] = take(rcv_g.at[t])
        rest0 = rest0 + restricted(arr_g[t], ohr[t])
    cd = cdiag[...]
    first = (0.8 * 0.064) * rest0 / cd
    packed = lax.dot_general(stacked(first), st_hot[...], (((1,), (1,)), ((), ())), preferred_element_type=F32)
    mine[...] = packed[:40] + packed[40:]
    c_two = []
    for t in (far, 1 - far):
        group, there = side(t)
        place = jnp.where(t == 0, 4 + m, m)
        for k in range(2):
            c = remote(mine, blks.at[place], 4 + 2 * t + k, 4 + place, (group, k))
            pl.when(there)(c.start)
            c_two.append((there, c))
    c_own = remote(mine, blks.at[2 + m], 8, 6 + m, (g, other))
    c_own.start()

    for f in range(6):
        wide = slice(f * 256, f * 256 + 256)
        acc = dot(arr_g[0], ohr[0, wide, :]) + dot(arr_g[1], ohr[1, wide, :])
        acc = acc + dot(arr_m[...], ohrm[f * 128 : f * 128 + 128, :])
        nlh[f * 128 : f * 128 + 128, :] += acc[:128].astype(BF)
        nll[f * 128 : f * 128 + 128, :] += acc[128:].astype(BF)
    need(20)
    for v in range(5):
        lf = lift[v * 128 : v * 128 + 128, :]
        full = resl[v * 128 : v * 128 + 128, :] + dot(lf, nlh[...]) + dot(lf, nll[...])
        resv[v] = full[:125]
    c_out = pltpu.make_async_copy(resv, resid_out, out_sem.at[0])
    c_out.start()
    inner = exact(qq, first)
    weight = 0.8 / cd
    base = 1.2 * first - weight * inner

    def arrived(place):
        remote(mine, blks.at[place], 8, 4 + place, (g, other)).wait_recv()

    def neighbours(d):
        a, b = stacked(blks[2 * d]), stacked(blks[2 * d + 1])
        return [
            dot(jnp.concatenate([a[:, o * 128 : o * 128 + 128], b[:, o * 128 : o * 128 + 128]], axis=1), ohc[o, d])
            for o in range(2)
        ]

    arrived(2 + other)
    blks[2 + m] = mine[...]
    nears = neighbours(1)
    for t in (1 - far, far):

        @pl.when(side(t)[1])
        def _(t=t):
            arrived(4 * t)
            arrived(4 * t + 1)

        nears = [x + y for x, y in zip(nears, neighbours(2 * t))]
    nhs, nls = [], []
    for o in range(2):
        near = nears[o]
        nhs.append(jnp.concatenate([near[:40, f * 128 : f * 128 + 128] for f in range(6)], axis=0))
        nls.append(jnp.concatenate([near[40:, f * 128 : f * 128 + 128] for f in range(6)], axis=0))
    nh = jnp.concatenate(nhs, axis=1).astype(BF)
    nl = jnp.concatenate(nls, axis=1).astype(BF)
    across = (dot(ggh, nh) + dot(ggh, nl) + dot(ggl, nh))[:40]
    back = dot(stacked(across), st_hot[...])
    mine2[...] = base + weight * (back[:40] + back[40:])
    c_second = pltpu.make_async_copy(mine2, second_out, out_sem.at[1])
    c_second.start()

    for c in (c_nbr, c_mem, c_own):
        c.wait_send()
    for there, c in c_grp + c_two:
        pl.when(there)(c.wait_send)
    c_out.wait()
    c_second.wait()


def last_kernel(resid, second_h, pro2_h, resid_out, corr_out, second, pro2, corr, held, sem):
    loads = [pltpu.make_async_copy(second_h, second, sem.at[0]), pltpu.make_async_copy(pro2_h, pro2, sem.at[1])]
    whole = pltpu.make_async_copy(resid, held, sem.at[2])
    for c in loads:
        c.start()
    whole.start()
    for c in loads:
        c.wait()
    copies = []
    for v in range(5):
        corr[v] = dot(pro2[...], stacked(second[v * 8 : v * 8 + 8, :]))[:125]
        c = pltpu.make_async_copy(corr.at[v], corr_out.at[v], sem.at[4 + v])
        c.start()
        copies.append(c)
    whole.wait()
    c = pltpu.make_async_copy(held, resid_out, sem.at[3])
    c.start()
    copies.append(c)
    for c in copies:
        c.wait()


def shards(
    state, rhs, fine_diag, q_fine, var_mix, mem_count, grp_count, send_mem_idx, send_grp_idx,
    face_src, coarse_diag, q_coarse, g_coarse, owner, coarse_nbr,
):
    places, lift, rest, rest_lift, by_face, pro2, small = tables()
    n_grp = lax.axis_size("grp")
    hbm = pl.BlockSpec(memory_space=pltpu.HBM)
    field = jax.ShapeDtypeStruct((5, 125, 256), F32)
    operands = (
        state, send_mem_idx, send_grp_idx, mem_count, grp_count, jnp.asarray(places), coarse_nbr, face_src, rhs, fine_diag,
        q_fine, var_mix, jnp.asarray(rest), jnp.asarray(rest_lift), owner.reshape(1, 256), coarse_diag.reshape(40, 256),
        g_coarse.reshape(48, 8), q_coarse, jnp.asarray(small), jnp.asarray(by_face), jnp.asarray(lift),
    )
    resid, second = pl.pallas_call(
        functools.partial(main_kernel, n_grp),
        out_shape=(field, jax.ShapeDtypeStruct((40, 256), F32)),
        in_specs=[hbm] * 21,
        out_specs=(hbm, hbm),
        scratch_shapes=[pltpu.VMEM(a.shape, a.dtype) for a in operands]
        + [
            pltpu.VMEM((640, 256), BF),
            pltpu.VMEM((640, 256), BF),
            pltpu.VMEM((128, 128), F32),
            pltpu.VMEM((2, 1536, 256), BF),
            pltpu.VMEM((1536, 128), BF),
            pltpu.VMEM((256, 1536), BF),
            pltpu.VMEM((2, 128, 256), F32),
            pltpu.VMEM((128, 128), F32),
            pltpu.VMEM((8, 128), jnp.int32),
            pltpu.VMEM((2, 128, 256), F32),
            pltpu.VMEM((128, 128), F32),
            pltpu.VMEM((8, 128), jnp.int32),
            pltpu.VMEM((2, 1536, 256), BF),
            pltpu.VMEM((768, 256), BF),
            pltpu.VMEM((768, 256), BF),
            pltpu.VMEM((768, 256), BF),
            pltpu.VMEM((640, 256), F32),
            pltpu.VMEM((2, 3, 256, 768), BF),
            pltpu.VMEM((256, 256), BF),
            pltpu.VMEM((6, 40, 256), F32),
            pltpu.VMEM((40, 256), F32),
            pltpu.VMEM((5, 125, 256), F32),
            pltpu.VMEM((40, 256), F32),
            pltpu.VMEM((384, 256), BF),
            pltpu.VMEM((384, 256), BF),
            pltpu.VMEM((192, 128), BF),
            pltpu.VMEM((2, 256, 256), BF),
            pltpu.VMEM((256, 128), BF),
            pltpu.SemaphoreType.DMA((21,)),
            pltpu.SemaphoreType.DMA((5,)),
            pltpu.SemaphoreType.DMA((9,)),
            pltpu.SemaphoreType.DMA((10,)),
            pltpu.SemaphoreType.DMA((2,)),
        ],
        compiler_params=pltpu.CompilerParams(
            collective_id=0, has_side_effects=True, vmem_limit_bytes=60 * 1024 * 1024
        ),
        name="residual_and_sweeps",
    )(*operands)
    return pl.pallas_call(
        last_kernel,
        out_shape=(field, field),
        in_specs=[hbm, hbm, hbm],
        out_specs=(hbm, hbm),
        scratch_shapes=[
            pltpu.VMEM((40, 256), F32),
            pltpu.VMEM((128, 16), BF),
            pltpu.VMEM((5, 125, 256), F32),
            pltpu.VMEM((5, 125, 256), F32),
            pltpu.SemaphoreType.DMA((9,)),
        ],
        compiler_params=pltpu.CompilerParams(vmem_limit_bytes=60 * 1024 * 1024),
        name="prolongation",
    )(resid, second, jnp.asarray(pro2))


def solution(mesh):
    whole = ("grp", "mem")
    return jax.shard_map(
        shards,
        mesh=mesh,
        in_specs=(
            P(None, None, whole), P(None, None, whole), P(None, None, whole), P(), P(),
            P(whole, None), P(whole, None), P(whole, None, None), P(whole, None, None), P(None, whole),
            P(None, None, whole), P(), P(), P(whole, None), P(None, whole),
        ),
        out_specs=(P(None, None, whole), P(None, None, whole)),
        check_vma=False,
    )
```
